32 devices in a mesh: grp: 2 (over x), wide: 16 (over z, y, core).
Axes of the slice: x: 2, y: 2, z: 4, core: 2. Of those that a mesh axis runs over, the one named last changes fastest.
Arguments:
- qkv: bfloat16 [4096, 3456], P(('grp', 'wide')), parts along dimension 0, may hold values from -51.854497 to 51.854497
- grid: int32 [4, 2], P('grp'), parts along dimension 0, may hold values from 2 to 512, as said below
- w_out: bfloat16 [1152, 1152], replicated, may hold values from -0.1875 to 0.1875
- ln_gain: float32 [4608], replicated, may hold values from 0.1 to 1.9
- ln_bias: float32 [4608], replicated, may hold values from -3 to 3
- w_merge: bfloat16 [4608, 2048], P('wide'), may hold values from -0.09375 to 0.09375
- w_router: bfloat16 [2048, 8], replicated, may hold values from -0.125 to 0.125
- expert_ids: int32 [1024, 6], P(('grp', 'wide')), parts along dimension 0, may hold values from 0 to 7, as said below
- slot_pos: int32 [1024, 6], P(('grp', 'wide')), parts along dimension 0, may hold values from 0 to 31, as said below
- w_gate: bfloat16 [16, 2048, 704], P('wide'), may hold values from -0.125 to 0.125
- w_up: bfloat16 [16, 2048, 704], P('wide'), may hold values from -0.125 to 0.125
- w_down: bfloat16 [16, 704, 2048], P('wide'), may hold values from -0.15625 to 0.15625
Outputs:
- moe_out: bfloat16 [1024, 2048], P(('grp', 'wide')), parts along dimension 0
The draws below stay inside these ranges and needn't reach their ends.
There are 2 independent parts, one for each index of `grp`. The reference program is written for one: setup_inputs(seed, part) draws one part's arguments, and reference() takes and returns one part's arrays. A program takes and returns all parts, laid end to end along the dimension named above; an argument that names none is the same for every part. Nothing has to cross between parts.
Inputs may be any that keep to these rules, and one draw needn't show every extreme that they name: `expert_ids`: each row names 6 different experts. Among the rows of one device no expert is named more than 32 times, and one expert is named exactly 32 times by the rows of every device. `slot_pos`: among the rows of one device, the pairs naming expert e take the slots 0, 1, ... up to the number of such pairs minus one, each once. `grid`: both numbers are even; one clip's product equals 1024, and every other clip's product lies between 512 and 768.
All inputs are finite; a program needn't handle non-finite values.
Results may differ from the reference program's by a relative error of at most 0.023.
Values may be sent and summed in bfloat16 or wider, within the bound.
No kernel may reach another device: no remote copies, remote signals or barrier semaphores. Data moves between devices by JAX's collectives and lax.ppermute only.
A program may use at most 128 MiB of HBM per device.

```python
import jax
import jax.numpy as jnp
from jax import lax

D_VIT = 1152
HEADS = 16
D_LLM = 2048
FFE = 1408
TOPK = 6
CLIPS = 2
MERGE_W = 4608
PATCHES = 2048
CLIP_LEN = 1024
MT_DEV = 32
EXPERTS = 8
CAP = 32
N_WIDE = 16


def draw_qkv(key, part):
    vit_width = D_VIT
    streams = jax.random.split(key, 2)
    paired = 1.4 * jax.random.truncated_normal(streams[0], -4.0, 4.0, (PATCHES, 2 * vit_width), jnp.float32)
    values = jax.random.truncated_normal(streams[1], -4.0, 4.0, (PATCHES, vit_width), jnp.float32)
    return jnp.concatenate([paired, values], axis=1).astype(jnp.bfloat16)


def draw_grid(key, part):
    streams = jax.random.split(jax.random.fold_in(key, 11), 3)
    quarter = CLIP_LEN // 4
    levels = quarter.bit_length() - 1
    lowest = levels // 3
    highest = levels - levels // 3
    exponent = jax.random.randint(streams[0], (CLIPS,), lowest, highest + 1)
    half_width = jnp.left_shift(jnp.ones((CLIPS,), jnp.int32), exponent)
    most_rows = quarter // half_width
    least_rows = (most_rows + 1) // 2
    upper_rows = 3 * most_rows // 4
    half_height = least_rows + jax.random.randint(streams[1], (CLIPS,), 0, 1 << 20) % (upper_rows - least_rows + 1)
    full_clip = jax.random.randint(streams[2], (), 0, CLIPS)
    is_full = jnp.arange(CLIPS, dtype=jnp.int32) == full_clip
    half_height = jnp.where(is_full, quarter, half_height)
    half_width = jnp.where(is_full, 1, half_width)
    return jnp.stack([2 * half_height, 2 * half_width], axis=1).astype(jnp.int32)


def routing(key):
    streams = jax.random.split(jax.random.fold_in(key, 29), 4)
    fair_load = MT_DEV * TOPK // EXPERTS
    extra_load = CAP - fair_load
    pair_count = EXPERTS // 2
    middle = (1 + jax.random.permutation(streams[0], EXPERTS - 2)).astype(jnp.int32)
    expert_order = jnp.concatenate([jnp.array([EXPERTS - 1], jnp.int32), middle[:1], jnp.array([0], jnp.int32), middle[1:]]).astype(jnp.int32)
    load_shift = jax.random.randint(streams[1], (N_WIDE, pair_count), 0, extra_load + 1)
    load_shift = load_shift.at[:, 0].set(extra_load)
    load_shift = load_shift.at[:, 1].set(extra_load)
    expert_loads = jnp.zeros((N_WIDE, EXPERTS), jnp.int32)
    expert_loads = expert_loads.at[:, expert_order[0::2]].set(fair_load + load_shift)
    expert_loads = expert_loads.at[:, expert_order[1::2]].set(fair_load - load_shift)
    load_ends = jnp.cumsum(expert_loads, axis=1)
    starts = load_ends - expert_loads
    flat_slots = jnp.arange(MT_DEV * TOPK, dtype=jnp.int32)
    owner_ids = jnp.sum((load_ends[:, None, :] <= flat_slots[None, :, None]).astype(jnp.int32), axis=2)
    place_ids = flat_slots[None, :] - jnp.take_along_axis(starts, owner_ids, axis=1)
    owner_ids = owner_ids.reshape(N_WIDE, TOPK, MT_DEV).transpose(0, 2, 1)
    place_ids = place_ids.reshape(N_WIDE, TOPK, MT_DEV).transpose(0, 2, 1)
    row_order = jax.vmap(lambda stream: jax.random.permutation(stream, MT_DEV))(jax.random.split(streams[2], N_WIDE)).astype(jnp.int32)
    owner_ids = jnp.take_along_axis(owner_ids, row_order[:, :, None], axis=1)
    place_ids = jnp.take_along_axis(place_ids, row_order[:, :, None], axis=1)
    column_score = jax.random.randint(streams[3], (N_WIDE, MT_DEV, TOPK), 0, 1 << 20) * TOPK + jnp.arange(TOPK, dtype=jnp.int32)
    column_order = jnp.argsort(column_score, axis=2).astype(jnp.int32)
    owner_ids = jnp.take_along_axis(owner_ids, column_order, axis=2)
    place_ids = jnp.take_along_axis(place_ids, column_order, axis=2)
    return (owner_ids.reshape(N_WIDE * MT_DEV, TOPK).astype(jnp.int32), place_ids.reshape(N_WIDE * MT_DEV, TOPK).astype(jnp.int32))


def draw_expert_ids(key, part):
    return routing(key)[0]


def draw_slot_pos(key, part):
    return routing(key)[1]


def shard_levels(stream_key, shape, pieces, least, largest):
    def one(dim, blocks):
        steps = jax.random.uniform(jax.random.fold_in(jax.random.fold_in(stream_key, 6), dim), (blocks,), jnp.float32, least / len(pieces), largest / len(pieces))
        return jnp.repeat(jnp.exp(steps), shape[dim] // blocks).reshape((-1,) + (1,) * (len(shape) - dim - 1))

    level = one(*pieces[0])
    for cut in pieces[1:]:
        level = level * one(*cut)
    return level


def gaussian(own_key, extent, width, bound, shards=(), kind=jnp.bfloat16):
    result = width * jax.random.normal(own_key, extent, jnp.float32)
    if shards:
        result = result * shard_levels(own_key, extent, shards, -0.22, 0.18)
    return jnp.clip(result, -bound, bound).astype(kind)


def setup_inputs(seed: int = 0, part: int = 0) -> dict:
    seeds = jax.random.split(jax.random.key(seed), 13)
    part_keys = jax.random.split(jax.random.fold_in(seeds[12], part), 13)
    qkv = draw_qkv(jax.random.fold_in(jax.random.fold_in(seeds[12], part), 71), part)
    grid = draw_grid(jax.random.fold_in(jax.random.fold_in(seeds[12], part), 71), part)
    w_out = gaussian(seeds[2], (D_VIT, D_VIT), D_VIT ** -0.5, 0.1875)
    ln_gain = jnp.clip(1.0 + 0.18 * jax.random.normal(seeds[3], (MERGE_W,), jnp.float32), 0.1, 1.9)
    ln_bias = gaussian(seeds[4], (MERGE_W,), 0.5, 3.0, (), jnp.float32)
    w_merge = gaussian(seeds[5], (MERGE_W, D_LLM), MERGE_W ** -0.5, 0.09375, ((0, 16),))
    w_router = gaussian(seeds[6], (D_LLM, EXPERTS), D_LLM ** -0.5, 0.125)
    expert_ids = draw_expert_ids(jax.random.fold_in(jax.random.fold_in(seeds[12], part), 71), part)
    slot_pos = draw_slot_pos(jax.random.fold_in(jax.random.fold_in(seeds[12], part), 71), part)
    w_gate = gaussian(seeds[9], (2 * EXPERTS, D_LLM, FFE // 2), D_LLM ** -0.5, 0.125, ((0, 16),))
    w_up = gaussian(seeds[10], (2 * EXPERTS, D_LLM, FFE // 2), D_LLM ** -0.5, 0.125, ((0, 16),))
    w_down = gaussian(seeds[11], (2 * EXPERTS, FFE // 2, D_LLM), FFE ** -0.5, 0.15625, ((0, 16),))
    return {"qkv": qkv, "grid": grid, "w_out": w_out, "ln_gain": ln_gain, "ln_bias": ln_bias, "w_merge": w_merge, "w_router": w_router, "expert_ids": expert_ids, "slot_pos": slot_pos, "w_gate": w_gate, "w_up": w_up, "w_down": w_down}


route_scale = 2.446
norm_eps = 1e-05

def attend(operands):
    query_rows, key_rows, value_rows, patch_count = operands
    head_dim = query_rows.shape[1]
    visible = jnp.arange(key_rows.shape[0], dtype=jnp.int32) < patch_count
    block_size = min(1024, query_rows.shape[0])

    def one_block(query_block):
        scores = jnp.dot(query_block, key_rows.T, preferred_element_type=jnp.float32) * head_dim ** (-0.5)
        scores = jnp.where(visible[None, :], scores, -jnp.inf)
        highest = lax.optimization_barrier(jnp.max(scores, axis=1, keepdims=True))
        weights = jnp.exp(scores - highest)
        running = lax.optimization_barrier(jnp.sum(weights, axis=1, keepdims=True))
        mixture = jnp.dot(weights.astype(jnp.bfloat16), value_rows, preferred_element_type=jnp.float32)
        return (mixture / running).astype(jnp.bfloat16)
    blocks = query_rows.reshape(-1, block_size, head_dim)
    return lax.map(one_block, blocks).reshape(query_rows.shape[0], head_dim)

def reference(qkv, grid, w_out, ln_gain, ln_bias, w_merge, w_router, expert_ids, slot_pos, w_gate, w_up, w_down):
    vit_width = w_out.shape[0]
    head_dim = vit_width // HEADS
    patch_total = qkv.shape[0]

    def heads_of(columns):
        return columns.reshape(CLIPS, CLIP_LEN, HEADS, head_dim).transpose(0, 2, 1, 3).reshape(CLIPS * HEADS, CLIP_LEN, head_dim)
    patch_counts = jnp.repeat((grid[:, 0] * grid[:, 1]).astype(jnp.int32), HEADS)
    attended = lax.map(attend, (heads_of(qkv[:, :vit_width]), heads_of(qkv[:, vit_width:2 * vit_width]), heads_of(qkv[:, 2 * vit_width:]), patch_counts))
    attention = attended.reshape(CLIPS, HEADS, CLIP_LEN, head_dim).transpose(0, 2, 1, 3).reshape(patch_total, vit_width)
    projected = jnp.dot(attention, w_out, preferred_element_type=jnp.float32).astype(jnp.bfloat16)
    merged = projected.reshape(patch_total // 4, 4 * vit_width).astype(jnp.float32)
    centre = lax.optimization_barrier(jnp.mean(merged, axis=1, keepdims=True))
    centered = merged - centre
    spread = lax.optimization_barrier(jnp.mean(centered * centered, axis=1, keepdims=True))
    normed = (centered * lax.rsqrt(spread + norm_eps) * ln_gain + ln_bias).astype(jnp.bfloat16)
    tokens = jnp.dot(normed, w_merge, preferred_element_type=jnp.float32).astype(jnp.bfloat16)
    logits = jnp.dot(tokens, w_router, preferred_element_type=jnp.float32)
    chosen = jnp.take_along_axis(logits, expert_ids, axis=1)
    gate_values = jax.nn.sigmoid(chosen)
    route_weight = route_scale * gate_values / lax.optimization_barrier(jnp.sum(gate_values, axis=1, keepdims=True))
    token_count = tokens.shape[0]
    llm_width = tokens.shape[1]
    row_ids = jnp.arange(token_count, dtype=jnp.int32)
    block_ids = jnp.broadcast_to((row_ids // MT_DEV)[:, None], expert_ids.shape)
    owners = jnp.broadcast_to(row_ids[:, None], expert_ids.shape)
    slot_table = jnp.full((EXPERTS, N_WIDE, CAP), token_count, jnp.int32).at[expert_ids, block_ids, slot_pos].set(owners)
    slot_weight = jnp.zeros((EXPERTS, N_WIDE, CAP), jnp.float32).at[expert_ids, block_ids, slot_pos].set(route_weight)
    padded = jnp.concatenate([tokens, jnp.zeros((1, llm_width), jnp.bfloat16)], axis=0)
    half_width = w_gate.shape[2]
    gate_all = w_gate.reshape(EXPERTS, 2, llm_width, half_width)
    up_all = w_up.reshape(EXPERTS, 2, llm_width, half_width)
    down_all = w_down.reshape(EXPERTS, 2, half_width, llm_width)

    def add_expert(running, operands):
        index_table, weight_table, gate_pair, up_pair, down_pair = operands
        flat_index = index_table.reshape(-1)
        inputs = padded[flat_index]
        combined = jnp.zeros((flat_index.shape[0], llm_width), jnp.float32)
        for half_index in range(2):
            gate_part = jnp.dot(inputs, gate_pair[half_index], preferred_element_type=jnp.float32)
            up_part = jnp.dot(inputs, up_pair[half_index], preferred_element_type=jnp.float32)
            hidden = (jax.nn.silu(gate_part) * up_part).astype(jnp.bfloat16)
            product = jnp.dot(hidden, down_pair[half_index], preferred_element_type=jnp.float32).astype(jnp.bfloat16)
            combined = combined + lax.optimization_barrier(product).astype(jnp.float32)
        joined = lax.optimization_barrier(combined.astype(jnp.bfloat16)).astype(jnp.float32)
        return (running.at[flat_index].add(weight_table.reshape(-1, 1) * joined), None)
    running = jnp.zeros((token_count + 1, llm_width), jnp.float32)
    running = lax.scan(add_expert, running, (slot_table, slot_weight, gate_all, up_all, down_all))[0]
    return running[:token_count].astype(jnp.bfloat16)
```

```python
import jax
import jax.numpy as jnp
from jax import lax
from jax.experimental import pallas as pl
from jax.experimental.pallas import tpu as pltpu
from jax.sharding import PartitionSpec as P

HEADS = 16
CLIPS = 2


route_scale = 2.446
norm_eps = 1e-05


def swapped(value, axis, stride):
    mask = 2**stride
    pairs = [(source, source ^ mask) for source in range(lax.axis_size(axis))]
    return lax.ppermute(value, axis, pairs)


def ordered_pair(own_part, partner, upper_bit):
    return jnp.where(
        upper_bit == 1,
        jnp.concatenate([partner, own_part], 0),
        jnp.concatenate([own_part, partner], 0),
    )


def general(
    qkv,
    grid,
    w_out,
    ln_gain,
    ln_bias,
    w_merge,
    w_router,
    expert_ids,
    slot_pos,
    w_gate,
    w_up,
    w_down,
):
    devices = lax.axis_size("wide")
    position_self = lax.axis_index("wide")
    vit_width = w_out.shape[0]
    head_dim = vit_width // HEADS
    groups = devices // HEADS
    local_rows = qkv.shape[0]
    sub_rows = local_rows // groups
    per_clip = devices // CLIPS
    query_send = (
        qkv[:, :vit_width]
        .reshape(groups, sub_rows, HEADS, head_dim)
        .transpose(2, 0, 1, 3)
        .reshape(devices, sub_rows, head_dim)
    )
    key_value = jnp.concatenate(
        [
            qkv[:, vit_width : 2 * vit_width].reshape(local_rows, HEADS, head_dim),
            qkv[:, 2 * vit_width :].reshape(local_rows, HEADS, head_dim),
        ],
        axis=2,
    )
    spread_send = jnp.broadcast_to(
        key_value.transpose(1, 0, 2)[:, None], (HEADS, groups, local_rows, 2 * head_dim)
    ).reshape(devices, local_rows, 2 * head_dim)
    queries, key_rows = (
        lax.all_to_all(query_send, "wide", split_axis=0, concat_axis=0, tiled=True),
        lax.all_to_all(spread_send, "wide", split_axis=0, concat_axis=0, tiled=True),
    )
    key_rows = key_rows[None]
    key_groups = key_rows.shape[0]
    key_count = key_rows.shape[2]
    key_place = (
        jnp.arange(per_clip, dtype=jnp.int32)[None, :, None] * local_rows
        + jnp.arange(key_groups, dtype=jnp.int32)[:, None, None] * local_rows
        + jnp.arange(key_count, dtype=jnp.int32)[None, None, :]
    ).reshape(-1)
    patch_counts = grid[:, 0] * grid[:, 1]
    clip_queries = queries.reshape(CLIPS, per_clip * sub_rows, head_dim)
    query_block_rows = min(512, per_clip * sub_rows)
    score_scale = head_dim ** (-0.5)

    def attend(clip_index):
        key_block = lax.dynamic_slice_in_dim(key_rows, clip_index * per_clip, per_clip, 1).reshape(
            -1, 2 * head_dim
        )
        visible = key_place < lax.dynamic_index_in_dim(patch_counts, clip_index, 0, keepdims=False)
        query_all = lax.dynamic_index_in_dim(clip_queries, clip_index, 0, keepdims=False)

        def one_block(query_block):
            scores = (
                lax.dot_general(
                    query_block,
                    key_block[:, :head_dim],
                    (((1,), (1,)), ((), ())),
                    preferred_element_type=jnp.float32,
                )
                * score_scale
            )
            scores = jnp.where(visible[None, :], scores, -jnp.inf)
            highest = jnp.max(scores, axis=1, keepdims=True)
            weights = jnp.exp(scores - highest)
            running = jnp.sum(weights, axis=1, keepdims=True)
            mixture = jnp.dot(
                weights.astype(jnp.bfloat16),
                key_block[:, head_dim:],
                preferred_element_type=jnp.float32,
            )
            return (mixture / running).astype(jnp.bfloat16)

        return lax.map(one_block, query_all.reshape(-1, query_block_rows, head_dim)).reshape(
            -1, head_dim
        )

    attended = lax.map(attend, jnp.arange(CLIPS, dtype=jnp.int32))
    returned = lax.all_to_all(
        attended.reshape(devices, sub_rows, head_dim),
        "wide",
        split_axis=0,
        concat_axis=0,
        tiled=True,
    )
    attention = (
        returned.reshape(HEADS, groups, sub_rows, head_dim)
        .transpose(1, 2, 0, 3)
        .reshape(local_rows, vit_width)
    )
    projected = jnp.dot(attention, w_out, preferred_element_type=jnp.float32).astype(jnp.bfloat16)
    merged = projected.reshape(local_rows // 4, 4 * vit_width).astype(jnp.float32)
    centre = jnp.mean(merged, axis=1, keepdims=True)
    centered = merged - centre
    spread = jnp.mean(centered * centered, axis=1, keepdims=True)
    normed = (centered * lax.rsqrt(spread + norm_eps) * ln_gain + ln_bias).astype(jnp.bfloat16)
    tok_groups = min(8, devices)
    feat_groups = devices // tok_groups
    merge_rows = w_merge
    for bit_index in range(tok_groups.bit_length() - 1):
        partner = swapped(merge_rows, "wide", bit_index)
        upper_bit = position_self // (1 << bit_index) % 2
        merge_rows = ordered_pair(merge_rows, partner, upper_bit)
    token_count = normed.shape[0]
    part_rows = token_count // tok_groups
    feat_width = normed.shape[1] // feat_groups
    out_width = w_merge.shape[1]
    merge_send = (
        normed.reshape(tok_groups, part_rows, feat_groups, feat_width)
        .transpose(2, 0, 1, 3)
        .reshape(devices, part_rows, feat_width)
    )
    flat_rows = lax.all_to_all(merge_send, "wide", split_axis=0, concat_axis=0, tiled=True).reshape(
        -1, feat_width
    )
    partial_value = jnp.dot(flat_rows, merge_rows, preferred_element_type=jnp.float32).reshape(
        devices, -1, out_width
    )
    summed = lax.all_to_all(partial_value, "wide", split_axis=0, concat_axis=0, tiled=True)
    tokens = (
        jnp.sum(summed.reshape(feat_groups, tok_groups, part_rows, out_width), axis=0)
        .reshape(token_count, out_width)
        .astype(jnp.bfloat16)
    )
    logits = jnp.dot(tokens, w_router, preferred_element_type=jnp.float32)
    experts = w_router.shape[1]
    top_count = expert_ids.shape[1]
    matches = expert_ids[:, :, None] == jnp.arange(experts, dtype=jnp.int32)[None, None, :]
    chosen = jnp.sum(jnp.where(matches, logits[:, None, :], 0.0), axis=2)
    gate_values = jax.nn.sigmoid(chosen)
    route_weight = route_scale * gate_values / jnp.sum(gate_values, axis=1, keepdims=True)
    capacity = min(token_count, 2 * token_count * top_count // experts)
    slot_count = experts * capacity
    target = expert_ids * capacity + slot_pos
    one_hot = jnp.any(
        target[None, :, :] == jnp.arange(slot_count, dtype=jnp.int32)[:, None, None], axis=2
    ).astype(jnp.bfloat16)
    buffer = jnp.dot(one_hot, tokens, preferred_element_type=jnp.float32).astype(jnp.bfloat16)
    gate_half = w_gate[0]
    up_half = w_up[0]
    down_half = w_down[0]
    half_cap = capacity // 2
    dispatch = buffer.reshape(devices, half_cap, out_width)
    portion = lax.all_to_all(dispatch, "wide", split_axis=0, concat_axis=0, tiled=True)
    item_count = portion.shape[1]
    partner_rows = swapped(portion, "wide", 0)
    both_rows = jnp.concatenate([portion, partner_rows], axis=1)
    flat_rows = both_rows.reshape(-1, out_width)
    gate_part = jnp.dot(flat_rows, gate_half, preferred_element_type=jnp.float32)
    up_part = jnp.dot(flat_rows, up_half, preferred_element_type=jnp.float32)
    hidden = (jax.nn.silu(gate_part) * up_part).astype(jnp.bfloat16)
    product = (
        jnp.dot(hidden, down_half, preferred_element_type=jnp.float32)
        .astype(jnp.bfloat16)
        .reshape(devices, 2 * item_count, out_width)
    )
    from_partner = swapped(product[:, item_count:], "wide", 0)
    joined = (
        product[:, :item_count].astype(jnp.float32) + from_partner.astype(jnp.float32)
    ).astype(jnp.bfloat16)
    answers = lax.all_to_all(joined, "wide", split_axis=0, concat_axis=0, tiled=True)
    slot_result = answers.reshape(slot_count, out_width)
    slot_result = lax.optimization_barrier(slot_result)
    picked = jnp.take(slot_result, target.reshape(-1), axis=0).reshape(
        token_count, top_count, out_width
    )
    return jnp.sum(picked.astype(jnp.float32) * route_weight[:, :, None], axis=1).astype(
        jnp.bfloat16
    )


BF = jnp.bfloat16
F32 = jnp.float32
VMEM = pl.BlockSpec(memory_space=pltpu.VMEM)
SMEM = pl.BlockSpec(memory_space=pltpu.SMEM)
HBM = pl.BlockSpec(memory_space=pl.ANY)
LANES = 128
MASKED = -1e30
LOG2E = 1.4426950408889634


def params(mib):
    return pltpu.CompilerParams(vmem_limit_bytes=mib * 2**20)


def pieces(value, count):
    out = []
    for _ in range(count):
        piece = value.astype(BF).astype(F32)
        out.append(piece)
        value = value - piece
    return out


def pack_kernel(qkv_ref, out_ref):
    rows, width = qkv_ref.shape
    tokens = rows // 4
    peers, parts, _ = out_ref.shape
    source = lax.broadcasted_iota(jnp.int32, (rows, rows), 0)
    place = lax.broadcasted_iota(jnp.int32, (rows, rows), 1)
    order = jnp.where(source == 4 * (place % tokens) + place // tokens, 1.0, 0.0).astype(BF)
    part = parts // 3
    third = width // 3
    for kind in range(3):
        turned = lax.dot_general(
            qkv_ref[:, kind * third : (kind + 1) * third],
            order,
            (((0,), (0,)), ((), ())),
            preferred_element_type=F32,
        ).astype(BF)
        for peer in range(peers):
            out_ref[peer, kind * part : (kind + 1) * part, :] = turned[peer * part : (peer + 1) * part]


def attend_kernel(x_ref, grid_ref, out_ref):
    peers, parts, lanes = x_ref.shape
    part = parts // 3
    dim = part // 2
    quarters = 4
    sides = peers // quarters
    tokens = lanes // 4
    clip = lax.axis_index("wide") // peers
    count = grid_ref[clip, 0] * grid_ref[clip, 1]
    factor = dim ** (-0.5) * LOG2E
    keys = jnp.concatenate([x_ref[s, part : 2 * part, :] for s in range(peers)], 1)
    lane = lax.broadcasted_iota(jnp.int32, (16, peers * lanes), 1)
    row = lax.broadcasted_iota(jnp.int32, (16, peers * lanes), 0)
    inner = lane % lanes
    place = lane // lanes * lanes + 4 * (inner % tokens) + inner // tokens
    hidden = jnp.where((row == 0) & (place >= count), MASKED, 0.0).astype(BF)
    keys = jnp.concatenate([keys, hidden], 0).T
    values = jnp.concatenate([x_ref[s, 2 * part :, :] for s in range(peers)], 1).astype(F32)
    values = [values[:dim].astype(BF), values[dim:].astype(BF)]
    ones = jnp.where(lax.broadcasted_iota(jnp.int32, (16, sides * lanes), 0) == 0, 1.0, 0.0).astype(BF)
    head_row = lax.broadcasted_iota(jnp.int32, (part, sides * lanes), 0) // dim
    group = lax.broadcasted_iota(jnp.int32, (dim, lanes), 1) // tokens
    for quarter in range(quarters):
        query = jnp.concatenate(
            [x_ref[quarter + quarters * s, :part, :] for s in range(sides)], 1
        ).astype(F32)
        mixed = []
        for head in range(2):
            own = jnp.concatenate([jnp.where(head_row == head, query, 0.0).astype(BF), ones], 0)
            scores = jnp.dot(keys, own, preferred_element_type=F32)
            highest = jnp.max(scores, axis=0, keepdims=True)
            weights = jnp.exp2(scores * factor - highest * factor)
            total = jnp.sum(weights, axis=0, keepdims=True)
            value = jnp.dot(values[head], weights.astype(BF), preferred_element_type=F32) / total
            mixed += [value[:, s * lanes : (s + 1) * lanes] for s in range(sides)]
        for position in range(4):
            block = mixed[position]
            for g in range(4):
                if g != position:
                    shift = (g - position) * tokens % lanes
                    block = jnp.where(group == g, pltpu.roll(mixed[g], shift, 1), block)
            out_ref[quarters * position + quarter] = block.astype(BF)


def merge_kernel(
    x_ref, w_out_ref, gain_ref, bias_ref, w0, w1, w2, w3, out_ref, att_ref, w_ref, sems
):
    me = lax.axis_index("wide")
    position, quarter = me // 4, me % 4
    blocks, dim, lanes = x_ref.shape
    pairs = blocks // 2
    depth = w0.shape[0]
    out_width = w0.shape[1]
    width = w_out_ref.shape[1]
    copies = []
    for k, source in enumerate((w0, w1, w2, w3)):
        low = (quarter % 2 + k % 2) % 2
        high = (quarter // 2 + k // 2) % 2
        spot = pl.multiple_of((2 * high + low) * depth, depth)
        copies.append(pltpu.make_async_copy(source, w_ref.at[pl.ds(spot, depth), :], sems.at[k]))
        copies[-1].start()
    left = lax.broadcasted_iota(jnp.int32, (dim, lanes), 1) < lanes // 2
    for pair in range(pairs):
        first, second = x_ref[pair].astype(F32), x_ref[pairs + pair].astype(F32)
        upper = jnp.where(left, first, pltpu.roll(second, lanes // 2, 1))
        lower = jnp.where(left, pltpu.roll(first, lanes // 2, 1), second)
        att_ref[2 * dim * pair : 2 * dim * (pair + 1), :] = jnp.concatenate([upper, lower], 0).astype(BF)
    mixed = lax.dot_general(
        att_ref[...], w_out_ref[...], (((0,), (0,)), ((), ())), preferred_element_type=F32
    )
    mixed = mixed.astype(BF).astype(F32)
    centre = jnp.sum(mixed, axis=1, keepdims=True) / width
    centered = mixed - centre
    square = jnp.sum(centered * centered, axis=1, keepdims=True)
    gain, bias = gain_ref[position], bias_ref[position]
    row = lax.broadcasted_iota(jnp.int32, (16, width), 0)
    extra = jnp.zeros((16, width), F32)
    for k, line in enumerate(pieces(gain, 2) + pieces(bias, 2)):
        extra = jnp.where(row == k, line, extra)
    left_side = jnp.concatenate([(centered * gain).astype(BF), extra.astype(BF)], 0)
    lane = lax.broadcasted_iota(jnp.int32, (lanes, LANES), 1)
    stats = jnp.zeros((lanes, LANES), F32)
    for k, column in enumerate(pieces(centre, 3) + pieces(square, 3)):
        stats = jnp.where(lane == k, column, stats)
    stats = stats.astype(BF)
    for copy in copies:
        copy.wait()
    planes, tokens, _ = out_ref.shape
    half = tokens // 2
    step = 2 * LANES
    shared = [None] * tokens
    for begin in range(0, out_width, step):
        part = jnp.dot(left_side, w_ref[:, begin : begin + step], preferred_element_type=F32)
        for plane in range(planes):
            out_ref[plane, :, begin : begin + step] = part[plane * tokens : (plane + 1) * tokens].astype(BF)
        scale = part[lanes : lanes + 1] + part[lanes + 1 : lanes + 2]
        shift = part[lanes + 2 : lanes + 3] + part[lanes + 3 : lanes + 4]
        for k in range(step // LANES):
            shared[begin // LANES + k] = scale[:, k * LANES : (k + 1) * LANES]
            shared[half + begin // LANES + k] = shift[:, k * LANES : (k + 1) * LANES]
    shared = jnp.concatenate(shared, 0).astype(BF)
    for plane in range(planes):
        out_ref[plane, :, out_width : out_width + LANES] = shared
        out_ref[plane, :, out_width + LANES :] = stats[plane * tokens : (plane + 1) * tokens]


def route_kernel(x_ref, router_ref, ids_ref, out_ref, *, merge_width, experts):
    planes, tokens, _ = x_ref.shape
    out_width = out_ref.shape[1] - LANES
    half = tokens // 2
    stats = [x_ref[p, :, out_width + LANES :].astype(F32) for p in range(planes)]
    shared = [x_ref[p, :, out_width : out_width + LANES].astype(F32) for p in range(planes)]
    centres = [s[:, 0:1] + s[:, 1:2] + s[:, 2:3] for s in stats]
    squares = [s[:, 3:4] + s[:, 4:5] + s[:, 5:6] for s in stats]
    mean = sum(centres) / planes
    offsets = [c - mean for c in centres]
    spread = sum(q + (merge_width // planes) * (o * o) for q, o in zip(squares, offsets)) / merge_width
    inverse = lax.rsqrt(spread + norm_eps)
    bias = sum(shared)
    for k in range(out_width // LANES):
        cut = slice(k * LANES, (k + 1) * LANES)
        total = sum(x_ref[p, :, cut].astype(F32) for p in range(planes))
        total += sum(offsets[p] * shared[p][k : k + 1] for p in range(planes))
        out_ref[:, cut] = (total * inverse + bias[half + k : half + k + 1]).astype(BF)
    logits = jnp.dot(out_ref[:, :out_width], router_ref[...], preferred_element_type=F32)
    lane = lax.broadcasted_iota(jnp.int32, (tokens, LANES), 1)
    expert = lane % experts
    chosen = lane < 0
    for k in range(ids_ref.shape[1]):
        chosen = chosen | (ids_ref[:, k : k + 1] == expert)
    gates = jnp.where(chosen & (lane < 2 * experts), 1.0 / (1.0 + jnp.exp(-logits)), 0.0)
    total = jnp.sum(jnp.where(lane < experts, gates, 0.0), axis=1, keepdims=True)
    weight = route_scale * gates / total
    high, low = pieces(weight, 2)
    out_ref[:, out_width:] = jnp.where(lane < experts, high, low).astype(BF)


def expert_kernel(x_ref, gate_ref, up_ref, down_ref, out_ref, *, experts):
    blocks, tokens, width = out_ref.shape
    expert = lax.axis_index("wide") // 2
    rows = x_ref.shape[0]
    inputs = x_ref[:, :width]
    lane = lax.broadcasted_iota(jnp.int32, (rows, LANES), 1)
    weight = jnp.where(
        (lane == expert) | (lane == expert + experts), x_ref[:, width:].astype(F32), 0.0
    )
    weight = jnp.sum(weight, axis=1, keepdims=True)
    gate = jnp.dot(inputs, gate_ref[0], preferred_element_type=F32)
    up = jnp.dot(inputs, up_ref[0], preferred_element_type=F32)
    hidden = (gate / (1.0 + jnp.exp(-gate)) * up).astype(BF)
    step = 4 * LANES
    for begin in range(0, width, step):
        product = jnp.dot(hidden, down_ref[0, :, begin : begin + step], preferred_element_type=F32)
        product = (product * weight).astype(BF)
        for block in range(blocks):
            out_ref[block, :, begin : begin + step] = product[block * tokens : (block + 1) * tokens]


def crossed(value, mask):
    pairs = [(source, source ^ mask) for source in range(lax.axis_size("wide"))]
    return lax.ppermute(value, "wide", pairs)


def local(
    qkv, grid, w_out, ln_gain, ln_bias, w_merge, w_router, expert_ids, slot_pos, w_gate, w_up, w_down
):
    devices = lax.axis_size("wide")
    rows = qkv.shape[0]
    vit_width = w_out.shape[0]
    experts = w_router.shape[1]
    out_width = w_merge.shape[1]
    tokens = rows // 4
    peers = devices // CLIPS
    suits = (
        devices == HEADS
        and peers == 8
        and rows == LANES
        and devices == 2 * experts
        and 2 * out_width == tokens * LANES
        and 4 * w_merge.shape[0] == vit_width
    )
    if not suits:
        return general(
            qkv, grid, w_out, ln_gain, ln_bias, w_merge, w_router, expert_ids, slot_pos, w_gate, w_up, w_down
        )
    part = vit_width // peers
    dim = vit_width // HEADS
    packed = pl.pallas_call(
        pack_kernel,
        out_shape=jax.ShapeDtypeStruct((peers, 3 * part, rows), BF),
        in_specs=[VMEM],
        out_specs=VMEM,
        compiler_params=params(32),
    )(qkv)
    clips = [[c * peers + i for i in range(peers)] for c in range(CLIPS)]
    gathered = lax.all_to_all(
        packed, "wide", split_axis=0, concat_axis=0, tiled=True, axis_index_groups=clips
    )
    gathered, held = lax.optimization_barrier((gathered, w_merge))
    held_y = crossed(held, 2)
    held_c = crossed(held, 1)
    held_yc = crossed(held_y, 1)
    attended = pl.pallas_call(
        attend_kernel,
        out_shape=jax.ShapeDtypeStruct((devices, dim, rows), BF),
        in_specs=[VMEM, SMEM],
        out_specs=VMEM,
        compiler_params=params(48),
    )(gathered, grid)
    returned = lax.all_to_all(attended, "wide", split_axis=0, concat_axis=0, tiled=True)
    planes = devices // 4
    message = out_width + 2 * LANES
    partial = pl.pallas_call(
        merge_kernel,
        out_shape=jax.ShapeDtypeStruct((planes, tokens, message), BF),
        in_specs=[VMEM, VMEM, VMEM, VMEM, HBM, HBM, HBM, HBM],
        out_specs=VMEM,
        scratch_shapes=[
            pltpu.VMEM((vit_width, rows), BF),
            pltpu.VMEM((vit_width, out_width), BF),
            pltpu.SemaphoreType.DMA((4,)),
        ],
        compiler_params=params(48),
    )(
        returned,
        w_out,
        ln_gain.reshape(4, 1, vit_width),
        ln_bias.reshape(4, 1, vit_width),
        held,
        held_c,
        held_y,
        held_yc,
    )
    columns = [[q + 4 * i for i in range(planes)] for q in range(4)]
    summed = lax.all_to_all(
        partial, "wide", split_axis=0, concat_axis=0, tiled=True, axis_index_groups=columns
    )
    router = jnp.concatenate(
        [w_router, w_router, jnp.zeros((out_width, LANES - 2 * experts), BF)], 1
    )
    routed = pl.pallas_call(
        lambda *refs: route_kernel(*refs, merge_width=4 * vit_width, experts=experts),
        out_shape=jax.ShapeDtypeStruct((tokens, out_width + LANES), BF),
        in_specs=[VMEM, VMEM, VMEM],
        out_specs=VMEM,
        compiler_params=params(32),
    )(summed, router, expert_ids)
    along = (4, 8, 12)
    near = [routed] + [crossed(routed, mask) for mask in along]
    far = [crossed(block, 2) for block in near]
    own_plane = jnp.concatenate(near + far, 0)
    other_plane = crossed(own_plane, 1)

    def experts_of(block):
        return pl.pallas_call(
            lambda *refs: expert_kernel(*refs, experts=experts),
            out_shape=jax.ShapeDtypeStruct((devices // 2, tokens, out_width), BF),
            in_specs=[VMEM, VMEM, VMEM, VMEM],
            out_specs=VMEM,
            compiler_params=params(48),
        )(block, w_gate, w_up, w_down)

    own_out = experts_of(own_plane)
    other_out = experts_of(other_plane)
    total = (own_out.astype(F32) + crossed(other_out, 1).astype(F32)).astype(BF)
    total = total.reshape(2, planes, tokens, out_width)
    cut = out_width // 2
    first, second = total[..., :cut], total[..., cut:]
    first_y = crossed(first[1], 2)
    second_z = [crossed(second[:, i], mask) for i, mask in enumerate(along, 1)]
    first = (first[0].astype(F32) + first_y.astype(F32)).astype(BF)
    second = second[:, 0].astype(F32) + sum(block.astype(F32) for block in second_z)
    second_y = crossed(second[1].astype(BF), 2)
    first_z = [crossed(first[i], mask) for i, mask in enumerate(along, 1)]
    first = first[0].astype(F32) + sum(block.astype(F32) for block in first_z)
    second = second[0] + second_y.astype(F32)
    return jnp.concatenate([first, second], 1).astype(BF)


def solution(mesh):
    placed = (
        P(("grp", "wide"), None),
        P("grp", None),
        P(),
        P(),
        P(),
        P("wide", None),
        P(),
        P(("grp", "wide"), None),
        P(("grp", "wide"), None),
        P("wide", None, None),
        P("wide", None, None),
        P("wide", None, None),
    )
    return jax.shard_map(
        local, mesh=mesh, in_specs=placed, out_specs=P(("grp", "wide"), None), check_vma=False
    )
```

```python
import jax
import jax.numpy as jnp
from jax import lax
from jax.experimental import pallas as pl
from jax.experimental.pallas import tpu as pltpu
from jax.sharding import PartitionSpec as P

HEADS = 16
CLIPS = 2


route_scale = 2.446
norm_eps = 1e-05


def swapped(value, axis, stride):
    mask = 2**stride
    pairs = [(source, source ^ mask) for source in range(lax.axis_size(axis))]
    return lax.ppermute(value, axis, pairs)


def ordered_pair(own_part, partner, upper_bit):
    return jnp.where(
        upper_bit == 1,
        jnp.concatenate([partner, own_part], 0),
        jnp.concatenate([own_part, partner], 0),
    )


def general(
    qkv,
    grid,
    w_out,
    ln_gain,
    ln_bias,
    w_merge,
    w_router,
    expert_ids,
    slot_pos,
    w_gate,
    w_up,
    w_down,
):
    devices = lax.axis_size("wide")
    position_self = lax.axis_index("wide")
    vit_width = w_out.shape[0]
    head_dim = vit_width // HEADS
    groups = devices // HEADS
    local_rows = qkv.shape[0]
    sub_rows = local_rows // groups
    per_clip = devices // CLIPS
    query_send = (
        qkv[:, :vit_width]
        .reshape(groups, sub_rows, HEADS, head_dim)
        .transpose(2, 0, 1, 3)
        .reshape(devices, sub_rows, head_dim)
    )
    key_value = jnp.concatenate(
        [
            qkv[:, vit_width : 2 * vit_width].reshape(local_rows, HEADS, head_dim),
            qkv[:, 2 * vit_width :].reshape(local_rows, HEADS, head_dim),
        ],
        axis=2,
    )
    spread_send = jnp.broadcast_to(
        key_value.transpose(1, 0, 2)[:, None], (HEADS, groups, local_rows, 2 * head_dim)
    ).reshape(devices, local_rows, 2 * head_dim)
    queries, key_rows = (
        lax.all_to_all(query_send, "wide", split_axis=0, concat_axis=0, tiled=True),
        lax.all_to_all(spread_send, "wide", split_axis=0, concat_axis=0, tiled=True),
    )
    key_rows = key_rows[None]
    key_groups = key_rows.shape[0]
    key_count = key_rows.shape[2]
    key_place = (
        jnp.arange(per_clip, dtype=jnp.int32)[None, :, None] * local_rows
        + jnp.arange(key_groups, dtype=jnp.int32)[:, None, None] * local_rows
        + jnp.arange(key_count, dtype=jnp.int32)[None, None, :]
    ).reshape(-1)
    patch_counts = grid[:, 0] * grid[:, 1]
    clip_queries = queries.reshape(CLIPS, per_clip * sub_rows, head_dim)
    query_block_rows = min(512, per_clip * sub_rows)
    score_scale = head_dim ** (-0.5)

    def attend(clip_index):
        key_block = lax.dynamic_slice_in_dim(key_rows, clip_index * per_clip, per_clip, 1).reshape(
            -1, 2 * head_dim
        )
        visible = key_place < lax.dynamic_index_in_dim(patch_counts, clip_index, 0, keepdims=False)
        query_all = lax.dynamic_index_in_dim(clip_queries, clip_index, 0, keepdims=False)

        def one_block(query_block):
            scores = (
                lax.dot_general(
                    query_block,
                    key_block[:, :head_dim],
                    (((1,), (1,)), ((), ())),
                    preferred_element_type=jnp.float32,
                )
                * score_scale
            )
            scores = jnp.where(visible[None, :], scores, -jnp.inf)
            highest = jnp.max(scores, axis=1, keepdims=True)
            weights = jnp.exp(scores - highest)
            running = jnp.sum(weights, axis=1, keepdims=True)
            mixture = jnp.dot(
                weights.astype(jnp.bfloat16),
                key_block[:, head_dim:],
                preferred_element_type=jnp.float32,
            )
            return (mixture / running).astype(jnp.bfloat16)

        return lax.map(one_block, query_all.reshape(-1, query_block_rows, head_dim)).reshape(
            -1, head_dim
        )

    attended = lax.map(attend, jnp.arange(CLIPS, dtype=jnp.int32))
    returned = lax.all_to_all(
        attended.reshape(devices, sub_rows, head_dim),
        "wide",
        split_axis=0,
        concat_axis=0,
        tiled=True,
    )
    attention = (
        returned.reshape(HEADS, groups, sub_rows, head_dim)
        .transpose(1, 2, 0, 3)
        .reshape(local_rows, vit_width)
    )
    projected = jnp.dot(attention, w_out, preferred_element_type=jnp.float32).astype(jnp.bfloat16)
    merged = projected.reshape(local_rows // 4, 4 * vit_width).astype(jnp.float32)
    centre = jnp.mean(merged, axis=1, keepdims=True)
    centered = merged - centre
    spread = jnp.mean(centered * centered, axis=1, keepdims=True)
    normed = (centered * lax.rsqrt(spread + norm_eps) * ln_gain + ln_bias).astype(jnp.bfloat16)
    tok_groups = min(8, devices)
    feat_groups = devices // tok_groups
    merge_rows = w_merge
    for bit_index in range(tok_groups.bit_length() - 1):
        partner = swapped(merge_rows, "wide", bit_index)
        upper_bit = position_self // (1 << bit_index) % 2
        merge_rows = ordered_pair(merge_rows, partner, upper_bit)
    token_count = normed.shape[0]
    part_rows = token_count // tok_groups
    feat_width = normed.shape[1] // feat_groups
    out_width = w_merge.shape[1]
    merge_send = (
        normed.reshape(tok_groups, part_rows, feat_groups, feat_width)
        .transpose(2, 0, 1, 3)
        .reshape(devices, part_rows, feat_width)
    )
    flat_rows = lax.all_to_all(merge_send, "wide", split_axis=0, concat_axis=0, tiled=True).reshape(
        -1, feat_width
    )
    partial_value = jnp.dot(flat_rows, merge_rows, preferred_element_type=jnp.float32).reshape(
        devices, -1, out_width
    )
    summed = lax.all_to_all(partial_value, "wide", split_axis=0, concat_axis=0, tiled=True)
    tokens = (
        jnp.sum(summed.reshape(feat_groups, tok_groups, part_rows, out_width), axis=0)
        .reshape(token_count, out_width)
        .astype(jnp.bfloat16)
    )
    logits = jnp.dot(tokens, w_router, preferred_element_type=jnp.float32)
    experts = w_router.shape[1]
    top_count = expert_ids.shape[1]
    matches = expert_ids[:, :, None] == jnp.arange(experts, dtype=jnp.int32)[None, None, :]
    chosen = jnp.sum(jnp.where(matches, logits[:, None, :], 0.0), axis=2)
    gate_values = jax.nn.sigmoid(chosen)
    route_weight = route_scale * gate_values / jnp.sum(gate_values, axis=1, keepdims=True)
    capacity = min(token_count, 2 * token_count * top_count // experts)
    slot_count = experts * capacity
    target = expert_ids * capacity + slot_pos
    one_hot = jnp.any(
        target[None, :, :] == jnp.arange(slot_count, dtype=jnp.int32)[:, None, None], axis=2
    ).astype(jnp.bfloat16)
    buffer = jnp.dot(one_hot, tokens, preferred_element_type=jnp.float32).astype(jnp.bfloat16)
    gate_half = w_gate[0]
    up_half = w_up[0]
    down_half = w_down[0]
    half_cap = capacity // 2
    dispatch = buffer.reshape(devices, half_cap, out_width)
    portion = lax.all_to_all(dispatch, "wide", split_axis=0, concat_axis=0, tiled=True)
    item_count = portion.shape[1]
    partner_rows = swapped(portion, "wide", 0)
    both_rows = jnp.concatenate([portion, partner_rows], axis=1)
    flat_rows = both_rows.reshape(-1, out_width)
    gate_part = jnp.dot(flat_rows, gate_half, preferred_element_type=jnp.float32)
    up_part = jnp.dot(flat_rows, up_half, preferred_element_type=jnp.float32)
    hidden = (jax.nn.silu(gate_part) * up_part).astype(jnp.bfloat16)
    product = (
        jnp.dot(hidden, down_half, preferred_element_type=jnp.float32)
        .astype(jnp.bfloat16)
        .reshape(devices, 2 * item_count, out_width)
    )
    from_partner = swapped(product[:, item_count:], "wide", 0)
    joined = (
        product[:, :item_count].astype(jnp.float32) + from_partner.astype(jnp.float32)
    ).astype(jnp.bfloat16)
    answers = lax.all_to_all(joined, "wide", split_axis=0, concat_axis=0, tiled=True)
    slot_result = answers.reshape(slot_count, out_width)
    slot_result = lax.optimization_barrier(slot_result)
    picked = jnp.take(slot_result, target.reshape(-1), axis=0).reshape(
        token_count, top_count, out_width
    )
    return jnp.sum(picked.astype(jnp.float32) * route_weight[:, :, None], axis=1).astype(
        jnp.bfloat16
    )


BF = jnp.bfloat16
F32 = jnp.float32
VMEM = pl.BlockSpec(memory_space=pltpu.VMEM)
SMEM = pl.BlockSpec(memory_space=pltpu.SMEM)
HBM = pl.BlockSpec(memory_space=pl.ANY)
LANES = 128
MASKED = -1e30
LOG2E = 1.4426950408889634


def params(mib):
    return pltpu.CompilerParams(vmem_limit_bytes=mib * 2**20)


def cost(flops, size, exps=0):
    return pl.CostEstimate(flops=flops, bytes_accessed=size, transcendentals=exps)


def flipped(number, bits):
    low = (number % 2 + bits % 2) % 2
    return 2 * ((number // 2 + bits // 2) % 2) + low


def pieces(value, count):
    out = []
    for _ in range(count):
        piece = value.astype(BF).astype(F32)
        out.append(piece)
        value = value - piece
    return out


def pack_kernel(qkv_ref, out_ref):
    rows, width = qkv_ref.shape
    tokens = rows // 4
    peers, parts, _ = out_ref.shape
    source = lax.broadcasted_iota(jnp.int32, (rows, rows), 0)
    place = lax.broadcasted_iota(jnp.int32, (rows, rows), 1)
    order = jnp.where(source == 4 * (place % tokens) + place // tokens, 1.0, 0.0).astype(BF)
    part = parts // 3
    third = width // 3
    for kind in range(3):
        turned = lax.dot_general(
            qkv_ref[:, kind * third : (kind + 1) * third],
            order,
            (((0,), (0,)), ((), ())),
            preferred_element_type=F32,
        ).astype(BF)
        for peer in range(peers):
            out_ref[peer, kind * part : (kind + 1) * part, :] = turned[peer * part : (peer + 1) * part]


def attend_kernel(x_ref, grid_ref, out_ref):
    peers, parts, lanes = x_ref.shape
    part = parts // 3
    dim = part // 2
    quarters = 4
    sides = peers // quarters
    tokens = lanes // 4
    clip = lax.axis_index("wide") // peers
    count = grid_ref[clip, 0] * grid_ref[clip, 1]
    factor = dim ** (-0.5) * LOG2E
    keys = jnp.concatenate([x_ref[s, part : 2 * part, :] for s in range(peers)], 1)
    lane = lax.broadcasted_iota(jnp.int32, (16, peers * lanes), 1)
    row = lax.broadcasted_iota(jnp.int32, (16, peers * lanes), 0)
    inner = lane % lanes
    place = lane // lanes * lanes + 4 * (inner % tokens) + inner // tokens
    hidden = jnp.where((row == 0) & (place >= count), MASKED, 0.0).astype(BF)
    keys = jnp.concatenate([keys, hidden], 0).T
    values = jnp.concatenate([x_ref[s, 2 * part :, :] for s in range(peers)], 1).astype(F32)
    values = [values[:dim].astype(BF), values[dim:].astype(BF)]
    ones = jnp.where(lax.broadcasted_iota(jnp.int32, (16, sides * lanes), 0) == 0, 1.0, 0.0).astype(BF)
    head_row = lax.broadcasted_iota(jnp.int32, (part, sides * lanes), 0) // dim
    group = lax.broadcasted_iota(jnp.int32, (dim, lanes), 1) // tokens
    for quarter in range(quarters):
        query = jnp.concatenate(
            [x_ref[quarter + quarters * s, :part, :] for s in range(sides)], 1
        ).astype(F32)
        mixed = []
        for head in range(2):
            own = jnp.concatenate([jnp.where(head_row == head, query, 0.0).astype(BF), ones], 0)
            scores = jnp.dot(keys, own, preferred_element_type=F32)
            highest = jnp.max(scores, axis=0, keepdims=True)
            weights = jnp.exp2(scores * factor - highest * factor)
            total = jnp.sum(weights, axis=0, keepdims=True)
            value = jnp.dot(values[head], weights.astype(BF), preferred_element_type=F32) / total
            mixed += [value[:, s * lanes : (s + 1) * lanes] for s in range(sides)]
        for position in range(4):
            block = mixed[position]
            for g in range(4):
                if g != position:
                    shift = (g - position) * tokens % lanes
                    block = jnp.where(group == g, pltpu.roll(mixed[g], shift, 1), block)
            out_ref[quarters * position + quarter] = block.astype(BF)


def merge_kernel(
    x_ref, w_out_ref, gain_ref, bias_ref, w0, w1, w2, w3, out_ref, att_ref, w_ref, sems
):
    me = lax.axis_index("wide")
    position, quarter = me // 4, me % 4
    blocks, dim, lanes = x_ref.shape
    pairs = blocks // 2
    depth = w0.shape[0]
    out_width = w0.shape[1]
    width = w_out_ref.shape[1]
    copies = []
    for k, source in enumerate((w0, w1, w2, w3)):
        spot = pl.multiple_of(flipped(quarter, k) * depth, depth)
        copies.append(pltpu.make_async_copy(source, w_ref.at[pl.ds(spot, depth), :], sems.at[k]))
        copies[-1].start()
    left = lax.broadcasted_iota(jnp.int32, (dim, lanes), 1) < lanes // 2
    for pair in range(pairs):
        first, second = x_ref[pair].astype(F32), x_ref[pairs + pair].astype(F32)
        upper = jnp.where(left, first, pltpu.roll(second, lanes // 2, 1))
        lower = jnp.where(left, pltpu.roll(first, lanes // 2, 1), second)
        att_ref[2 * dim * pair : 2 * dim * (pair + 1), :] = jnp.concatenate([upper, lower], 0).astype(BF)
    mixed = lax.dot_general(
        att_ref[...], w_out_ref[...], (((0,), (0,)), ((), ())), preferred_element_type=F32
    )
    mixed = mixed.astype(BF).astype(F32)
    centre = jnp.sum(mixed, axis=1, keepdims=True) / width
    centered = mixed - centre
    square = jnp.sum(centered * centered, axis=1, keepdims=True)
    here = pl.ds(pl.multiple_of(position * width, LANES), width)
    gain, bias = gain_ref[:, here], bias_ref[:, here]
    row = lax.broadcasted_iota(jnp.int32, (16, width), 0)
    extra = jnp.zeros((16, width), F32)
    for k, line in enumerate(pieces(gain, 2) + pieces(bias, 2)):
        extra = jnp.where(row == k, line, extra)
    left_side = jnp.concatenate([(centered * gain).astype(BF), extra.astype(BF)], 0)
    lane = lax.broadcasted_iota(jnp.int32, (lanes, LANES), 1)
    stats = jnp.zeros((lanes, LANES), F32)
    for k, column in enumerate(pieces(centre, 3) + pieces(square, 3)):
        stats = jnp.where(lane == k, column, stats)
    stats = stats.astype(BF)
    for copy in copies:
        copy.wait()
    planes, tokens, _ = out_ref.shape
    half = tokens // 2
    step = 2 * LANES
    shared = [None] * tokens
    for begin in range(0, out_width, step):
        part = jnp.dot(left_side, w_ref[:, begin : begin + step], preferred_element_type=F32)
        for plane in range(planes):
            out_ref[flipped(position, plane), :, begin : begin + step] = part[plane * tokens : (plane + 1) * tokens].astype(BF)
        scale = part[lanes : lanes + 1] + part[lanes + 1 : lanes + 2]
        shift = part[lanes + 2 : lanes + 3] + part[lanes + 3 : lanes + 4]
        for k in range(step // LANES):
            shared[begin // LANES + k] = scale[:, k * LANES : (k + 1) * LANES]
            shared[half + begin // LANES + k] = shift[:, k * LANES : (k + 1) * LANES]
    shared = jnp.concatenate(shared, 0).astype(BF)
    for plane in range(planes):
        out_ref[flipped(position, plane), :, out_width : out_width + LANES] = shared
        out_ref[flipped(position, plane), :, out_width + LANES :] = stats[plane * tokens : (plane + 1) * tokens]


def route_kernel(x0, x1, x2, x3, router_ref, ids_ref, out_ref, *, merge_width, experts):
    blocks = (x0, x1, x2, x3)
    planes, tokens = len(blocks), x0.shape[0]
    out_width = out_ref.shape[1] - LANES
    half = tokens // 2
    stats = [blocks[p][:, out_width + LANES :].astype(F32) for p in range(planes)]
    shared = [blocks[p][:, out_width : out_width + LANES].astype(F32) for p in range(planes)]
    centres = [s[:, 0:1] + s[:, 1:2] + s[:, 2:3] for s in stats]
    squares = [s[:, 3:4] + s[:, 4:5] + s[:, 5:6] for s in stats]
    mean = sum(centres) / planes
    offsets = [c - mean for c in centres]
    spread = sum(q + (merge_width // planes) * (o * o) for q, o in zip(squares, offsets)) / merge_width
    inverse = lax.rsqrt(spread + norm_eps)
    bias = sum(shared)
    for k in range(out_width // LANES):
        cut = slice(k * LANES, (k + 1) * LANES)
        total = sum(blocks[p][:, cut].astype(F32) for p in range(planes))
        total += sum(offsets[p] * shared[p][k : k + 1] for p in range(planes))
        out_ref[:, cut] = (total * inverse + bias[half + k : half + k + 1]).astype(BF)
    logits = jnp.dot(out_ref[:, :out_width], router_ref[...], preferred_element_type=F32)
    lane = lax.broadcasted_iota(jnp.int32, (tokens, LANES), 1)
    expert = lane % experts
    chosen = lane < 0
    for k in range(ids_ref.shape[1]):
        chosen = chosen | (ids_ref[:, k : k + 1] == expert)
    gates = jnp.where(chosen & (lane < 2 * experts), 1.0 / (1.0 + jnp.exp(-logits)), 0.0)
    total = jnp.sum(jnp.where(lane < experts, gates, 0.0), axis=1, keepdims=True)
    weight = route_scale * gates / total
    high, low = pieces(weight, 2)
    out_ref[:, out_width:] = jnp.where(lane < experts, high, low).astype(BF)


def expert_kernel(*refs, experts):
    *blocks, gate_ref, up_ref, down_ref, own_ref, other_ref, x_ref = refs
    tokens, width = own_ref.shape[1:]
    half = len(blocks) // 2
    expert = lax.axis_index("wide") // 2
    lane = lax.broadcasted_iota(jnp.int32, (tokens, LANES), 1)
    weights = []
    for k, block in enumerate(blocks):
        x_ref[k * tokens : (k + 1) * tokens, :] = block[:, :width]
        picked = (lane == expert) | (lane == expert + experts)
        picked = jnp.where(picked, block[:, width:].astype(F32), 0.0)
        weights.append(jnp.sum(picked, axis=1, keepdims=True))
    inputs = x_ref[...]
    turned = (((1,), (1,)), ((), ()))
    gate = lax.dot_general(inputs, gate_ref[0], turned, preferred_element_type=F32)
    up = lax.dot_general(inputs, up_ref[0], turned, preferred_element_type=F32)
    hidden = (gate / (1.0 + jnp.exp(-gate)) * up).astype(BF)
    step = 4 * LANES
    for begin in range(0, width, step):
        product = jnp.dot(hidden, down_ref[0, :, begin : begin + step], preferred_element_type=F32)
        for k in range(len(blocks)):
            value = (product[k * tokens : (k + 1) * tokens] * weights[k]).astype(BF)
            out_ref = own_ref if k < half else other_ref
            out_ref[k % half, :, begin : begin + step] = value


def crossed(value, mask):
    pairs = [(source, source ^ mask) for source in range(lax.axis_size("wide"))]
    return lax.ppermute(value, "wide", pairs)


def local(
    qkv, grid, w_out, ln_gain, ln_bias, w_merge, w_router, expert_ids, slot_pos, w_gate, w_up, w_down
):
    devices = lax.axis_size("wide")
    rows = qkv.shape[0]
    vit_width = w_out.shape[0]
    experts = w_router.shape[1]
    out_width = w_merge.shape[1]
    tokens = rows // 4
    peers = devices // CLIPS
    suits = (
        devices == HEADS
        and peers == 8
        and rows == LANES
        and devices == 2 * experts
        and 2 * out_width == tokens * LANES
        and 4 * w_merge.shape[0] == vit_width
    )
    if not suits:
        return general(
            qkv, grid, w_out, ln_gain, ln_bias, w_merge, w_router, expert_ids, slot_pos, w_gate, w_up, w_down
        )
    part = vit_width // peers
    dim = vit_width // HEADS
    packed = pl.pallas_call(
        pack_kernel,
        out_shape=jax.ShapeDtypeStruct((peers, 3 * part, rows), BF),
        in_specs=[VMEM],
        out_specs=VMEM,
        compiler_params=params(32),
    )(qkv)
    clips = [[c * peers + i for i in range(peers)] for c in range(CLIPS)]
    gathered = lax.all_to_all(
        packed, "wide", split_axis=0, concat_axis=0, tiled=True, axis_index_groups=clips
    )
    gathered, held = lax.optimization_barrier((gathered, w_merge))
    held_y = crossed(held, 2)
    attended = pl.pallas_call(
        attend_kernel,
        out_shape=jax.ShapeDtypeStruct((devices, dim, rows), BF),
        in_specs=[VMEM, SMEM],
        out_specs=VMEM,
        compiler_params=params(48),
        cost_estimate=cost(2**32, 2**22, 2**21),
    )(gathered, grid)
    attended, held_y, held = lax.optimization_barrier((attended, held_y, held))
    held_c = crossed(held, 1)
    held_yc = crossed(held_y, 1)
    returned = lax.all_to_all(attended, "wide", split_axis=0, concat_axis=0, tiled=True)
    planes = devices // 4
    message = out_width + 2 * LANES
    partial = pl.pallas_call(
        merge_kernel,
        out_shape=jax.ShapeDtypeStruct((planes, tokens, message), BF),
        in_specs=[VMEM, VMEM, VMEM, VMEM, HBM, HBM, HBM, HBM],
        out_specs=VMEM,
        scratch_shapes=[
            pltpu.VMEM((vit_width, rows), BF),
            pltpu.VMEM((vit_width, out_width), BF),
            pltpu.SemaphoreType.DMA((4,)),
        ],
        compiler_params=params(48),
    )(
        returned,
        w_out,
        ln_gain.reshape(1, 4 * vit_width),
        ln_bias.reshape(1, 4 * vit_width),
        held,
        held_c,
        held_y,
        held_yc,
    )
    along = (4, 8, 12)
    arrived = [partial[0]] + [crossed(partial[k], mask) for k, mask in enumerate(along, 1)]
    router = jnp.concatenate(
        [w_router, w_router, jnp.zeros((out_width, LANES - 2 * experts), BF)], 1
    )
    routed = pl.pallas_call(
        lambda *refs: route_kernel(*refs, merge_width=4 * vit_width, experts=experts),
        out_shape=jax.ShapeDtypeStruct((tokens, out_width + LANES), BF),
        in_specs=[VMEM] * 6,
        out_specs=VMEM,
        compiler_params=params(32),
    )(*arrived, router, expert_ids)
    near = [routed] + [crossed(routed, mask) for mask in along]
    far = [crossed(block, 2) for block in near]
    gate_turned, up_turned = jnp.swapaxes(w_gate, 1, 2), jnp.swapaxes(w_up, 1, 2)

    def experts_of(blocks):
        own, other = pl.pallas_call(
            lambda *refs: expert_kernel(*refs, experts=experts),
            out_shape=[jax.ShapeDtypeStruct((planes, tokens, out_width), BF)] * 2,
            in_specs=[VMEM] * (2 * planes + 3),
            out_specs=[VMEM, VMEM],
            scratch_shapes=[pltpu.VMEM((2 * planes * tokens, out_width), BF)],
            compiler_params=params(48),
            cost_estimate=cost(2**32, 2**24),
        )(*blocks, *[crossed(block, 1) for block in blocks], gate_turned, up_turned, w_down)
        total = (own.astype(F32) + crossed(other, 1).astype(F32)).astype(BF)
        others = [crossed(total[k], mask) for k, mask in enumerate(along, 1)]
        return total[0].astype(F32) + sum(block.astype(F32) for block in others)

    near_sum = experts_of(near)
    far_sum = experts_of(far)
    return (near_sum + crossed(far_sum.astype(BF), 2).astype(F32)).astype(BF)


def solution(mesh):
    placed = (
        P(("grp", "wide"), None),
        P("grp", None),
        P(),
        P(),
        P(),
        P("wide", None),
        P(),
        P(("grp", "wide"), None),
        P(("grp", "wide"), None),
        P("wide", None, None),
        P("wide", None, None),
        P("wide", None, None),
    )
    return jax.shard_map(
        local, mesh=mesh, in_specs=placed, out_specs=P(("grp", "wide"), None), check_vma=False
    )
```

```python
import jax
import jax.numpy as jnp
from jax import lax
from jax.experimental import pallas as pl
from jax.experimental.pallas import tpu as pltpu
from jax.sharding import PartitionSpec as P

HEADS = 16
CLIPS = 2


route_scale = 2.446
norm_eps = 1e-05


def swapped(value, axis, stride):
    mask = 2**stride
    pairs = [(source, source ^ mask) for source in range(lax.axis_size(axis))]
    return lax.ppermute(value, axis, pairs)


def ordered_pair(own_part, partner, upper_bit):
    return jnp.where(
        upper_bit == 1,
        jnp.concatenate([partner, own_part], 0),
        jnp.concatenate([own_part, partner], 0),
    )


def general(
    qkv,
    grid,
    w_out,
    ln_gain,
    ln_bias,
    w_merge,
    w_router,
    expert_ids,
    slot_pos,
    w_gate,
    w_up,
    w_down,
):
    devices = lax.axis_size("wide")
    position_self = lax.axis_index("wide")
    vit_width = w_out.shape[0]
    head_dim = vit_width // HEADS
    groups = devices // HEADS
    local_rows = qkv.shape[0]
    sub_rows = local_rows // groups
    per_clip = devices // CLIPS
    query_send = (
        qkv[:, :vit_width]
        .reshape(groups, sub_rows, HEADS, head_dim)
        .transpose(2, 0, 1, 3)
        .reshape(devices, sub_rows, head_dim)
    )
    key_value = jnp.concatenate(
        [
            qkv[:, vit_width : 2 * vit_width].reshape(local_rows, HEADS, head_dim),
            qkv[:, 2 * vit_width :].reshape(local_rows, HEADS, head_dim),
        ],
        axis=2,
    )
    spread_send = jnp.broadcast_to(
        key_value.transpose(1, 0, 2)[:, None], (HEADS, groups, local_rows, 2 * head_dim)
    ).reshape(devices, local_rows, 2 * head_dim)
    queries, key_rows = (
        lax.all_to_all(query_send, "wide", split_axis=0, concat_axis=0, tiled=True),
        lax.all_to_all(spread_send, "wide", split_axis=0, concat_axis=0, tiled=True),
    )
    key_rows = key_rows[None]
    key_groups = key_rows.shape[0]
    key_count = key_rows.shape[2]
    key_place = (
        jnp.arange(per_clip, dtype=jnp.int32)[None, :, None] * local_rows
        + jnp.arange(key_groups, dtype=jnp.int32)[:, None, None] * local_rows
        + jnp.arange(key_count, dtype=jnp.int32)[None, None, :]
    ).reshape(-1)
    patch_counts = grid[:, 0] * grid[:, 1]
    clip_queries = queries.reshape(CLIPS, per_clip * sub_rows, head_dim)
    query_block_rows = min(512, per_clip * sub_rows)
    score_scale = head_dim ** (-0.5)

    def attend(clip_index):
        key_block = lax.dynamic_slice_in_dim(key_rows, clip_index * per_clip, per_clip, 1).reshape(
            -1, 2 * head_dim
        )
        visible = key_place < lax.dynamic_index_in_dim(patch_counts, clip_index, 0, keepdims=False)
        query_all = lax.dynamic_index_in_dim(clip_queries, clip_index, 0, keepdims=False)

        def one_block(query_block):
            scores = (
                lax.dot_general(
                    query_block,
                    key_block[:, :head_dim],
                    (((1,), (1,)), ((), ())),
                    preferred_element_type=jnp.float32,
                )
                * score_scale
            )
            scores = jnp.where(visible[None, :], scores, -jnp.inf)
            highest = jnp.max(scores, axis=1, keepdims=True)
            weights = jnp.exp(scores - highest)
            running = jnp.sum(weights, axis=1, keepdims=True)
            mixture = jnp.dot(
                weights.astype(jnp.bfloat16),
                key_block[:, head_dim:],
                preferred_element_type=jnp.float32,
            )
            return (mixture / running).astype(jnp.bfloat16)

        return lax.map(one_block, query_all.reshape(-1, query_block_rows, head_dim)).reshape(
            -1, head_dim
        )

    attended = lax.map(attend, jnp.arange(CLIPS, dtype=jnp.int32))
    returned = lax.all_to_all(
        attended.reshape(devices, sub_rows, head_dim),
        "wide",
        split_axis=0,
        concat_axis=0,
        tiled=True,
    )
    attention = (
        returned.reshape(HEADS, groups, sub_rows, head_dim)
        .transpose(1, 2, 0, 3)
        .reshape(local_rows, vit_width)
    )
    projected = jnp.dot(attention, w_out, preferred_element_type=jnp.float32).astype(jnp.bfloat16)
    merged = projected.reshape(local_rows // 4, 4 * vit_width).astype(jnp.float32)
    centre = jnp.mean(merged, axis=1, keepdims=True)
    centered = merged - centre
    spread = jnp.mean(centered * centered, axis=1, keepdims=True)
    normed = (centered * lax.rsqrt(spread + norm_eps) * ln_gain + ln_bias).astype(jnp.bfloat16)
    tok_groups = min(8, devices)
    feat_groups = devices // tok_groups
    merge_rows = w_merge
    for bit_index in range(tok_groups.bit_length() - 1):
        partner = swapped(merge_rows, "wide", bit_index)
        upper_bit = position_self // (1 << bit_index) % 2
        merge_rows = ordered_pair(merge_rows, partner, upper_bit)
    token_count = normed.shape[0]
    part_rows = token_count // tok_groups
    feat_width = normed.shape[1] // feat_groups
    out_width = w_merge.shape[1]
    merge_send = (
        normed.reshape(tok_groups, part_rows, feat_groups, feat_width)
        .transpose(2, 0, 1, 3)
        .reshape(devices, part_rows, feat_width)
    )
    flat_rows = lax.all_to_all(merge_send, "wide", split_axis=0, concat_axis=0, tiled=True).reshape(
        -1, feat_width
    )
    partial_value = jnp.dot(flat_rows, merge_rows, preferred_element_type=jnp.float32).reshape(
        devices, -1, out_width
    )
    summed = lax.all_to_all(partial_value, "wide", split_axis=0, concat_axis=0, tiled=True)
    tokens = (
        jnp.sum(summed.reshape(feat_groups, tok_groups, part_rows, out_width), axis=0)
        .reshape(token_count, out_width)
        .astype(jnp.bfloat16)
    )
    logits = jnp.dot(tokens, w_router, preferred_element_type=jnp.float32)
    experts = w_router.shape[1]
    top_count = expert_ids.shape[1]
    matches = expert_ids[:, :, None] == jnp.arange(experts, dtype=jnp.int32)[None, None, :]
    chosen = jnp.sum(jnp.where(matches, logits[:, None, :], 0.0), axis=2)
    gate_values = jax.nn.sigmoid(chosen)
    route_weight = route_scale * gate_values / jnp.sum(gate_values, axis=1, keepdims=True)
    capacity = min(token_count, 2 * token_count * top_count // experts)
    slot_count = experts * capacity
    target = expert_ids * capacity + slot_pos
    one_hot = jnp.any(
        target[None, :, :] == jnp.arange(slot_count, dtype=jnp.int32)[:, None, None], axis=2
    ).astype(jnp.bfloat16)
    buffer = jnp.dot(one_hot, tokens, preferred_element_type=jnp.float32).astype(jnp.bfloat16)
    gate_half = w_gate[0]
    up_half = w_up[0]
    down_half = w_down[0]
    half_cap = capacity // 2
    dispatch = buffer.reshape(devices, half_cap, out_width)
    portion = lax.all_to_all(dispatch, "wide", split_axis=0, concat_axis=0, tiled=True)
    item_count = portion.shape[1]
    partner_rows = swapped(portion, "wide", 0)
    both_rows = jnp.concatenate([portion, partner_rows], axis=1)
    flat_rows = both_rows.reshape(-1, out_width)
    gate_part = jnp.dot(flat_rows, gate_half, preferred_element_type=jnp.float32)
    up_part = jnp.dot(flat_rows, up_half, preferred_element_type=jnp.float32)
    hidden = (jax.nn.silu(gate_part) * up_part).astype(jnp.bfloat16)
    product = (
        jnp.dot(hidden, down_half, preferred_element_type=jnp.float32)
        .astype(jnp.bfloat16)
        .reshape(devices, 2 * item_count, out_width)
    )
    from_partner = swapped(product[:, item_count:], "wide", 0)
    joined = (
        product[:, :item_count].astype(jnp.float32) + from_partner.astype(jnp.float32)
    ).astype(jnp.bfloat16)
    answers = lax.all_to_all(joined, "wide", split_axis=0, concat_axis=0, tiled=True)
    slot_result = answers.reshape(slot_count, out_width)
    slot_result = lax.optimization_barrier(slot_result)
    picked = jnp.take(slot_result, target.reshape(-1), axis=0).reshape(
        token_count, top_count, out_width
    )
    return jnp.sum(picked.astype(jnp.float32) * route_weight[:, :, None], axis=1).astype(
        jnp.bfloat16
    )


BF = jnp.bfloat16
F32 = jnp.float32
VMEM = pl.BlockSpec(memory_space=pltpu.VMEM)
SMEM = pl.BlockSpec(memory_space=pltpu.SMEM)
HBM = pl.BlockSpec(memory_space=pl.ANY)
LANES = 128
MASKED = -1e30
LOG2E = 1.4426950408889634


def params(mib):
    return pltpu.CompilerParams(vmem_limit_bytes=mib * 2**20)


def cost(flops, size, exps=0):
    return pl.CostEstimate(flops=flops, bytes_accessed=size, transcendentals=exps)


def flipped(number, bits):
    low = (number % 2 + bits % 2) % 2
    return 2 * ((number // 2 + bits // 2) % 2) + low


def pieces(value, count):
    out = []
    for _ in range(count):
        piece = value.astype(BF).astype(F32)
        out.append(piece)
        value = value - piece
    return out


def pack_kernel(qkv_ref, out_ref):
    rows, width = qkv_ref.shape
    tokens = rows // 4
    peers, parts, _ = out_ref.shape
    source = lax.broadcasted_iota(jnp.int32, (rows, rows), 0)
    place = lax.broadcasted_iota(jnp.int32, (rows, rows), 1)
    order = jnp.where(source == 4 * (place % tokens) + place // tokens, 1.0, 0.0).astype(BF)
    part = parts // 3
    third = width // 3
    for kind in range(3):
        turned = lax.dot_general(
            qkv_ref[:, kind * third : (kind + 1) * third],
            order,
            (((0,), (0,)), ((), ())),
            preferred_element_type=F32,
        ).astype(BF)
        for peer in range(peers):
            out_ref[peer, kind * part : (kind + 1) * part, :] = turned[peer * part : (peer + 1) * part]


def attend_kernel(x_ref, grid_ref, out_ref):
    peers, parts, lanes = x_ref.shape
    part = parts // 3
    dim = part // 2
    quarters = 4
    sides = peers // quarters
    tokens = lanes // 4
    clip = lax.axis_index("wide") // peers
    count = grid_ref[clip, 0] * grid_ref[clip, 1]
    factor = dim ** (-0.5) * LOG2E
    keys = jnp.concatenate([x_ref[s, part : 2 * part, :] for s in range(peers)], 1)
    lane = lax.broadcasted_iota(jnp.int32, (16, peers * lanes), 1)
    row = lax.broadcasted_iota(jnp.int32, (16, peers * lanes), 0)
    inner = lane % lanes
    place = lane // lanes * lanes + 4 * (inner % tokens) + inner // tokens
    hidden = jnp.where((row == 0) & (place >= count), MASKED, 0.0).astype(BF)
    keys = jnp.concatenate([keys, hidden], 0).T
    values = jnp.concatenate([x_ref[s, 2 * part :, :] for s in range(peers)], 1).astype(F32)
    values = [values[:dim].astype(BF), values[dim:].astype(BF)]
    ones = jnp.where(lax.broadcasted_iota(jnp.int32, (16, sides * lanes), 0) == 0, 1.0, 0.0).astype(BF)
    head_row = lax.broadcasted_iota(jnp.int32, (part, sides * lanes), 0) // dim
    group = lax.broadcasted_iota(jnp.int32, (dim, lanes), 1) // tokens
    for quarter in range(quarters):
        query = jnp.concatenate(
            [x_ref[quarter + quarters * s, :part, :] for s in range(sides)], 1
        ).astype(F32)
        mixed = []
        for head in range(2):
            own = jnp.concatenate([jnp.where(head_row == head, query, 0.0).astype(BF), ones], 0)
            scores = jnp.dot(keys, own, preferred_element_type=F32)
            highest = jnp.max(scores, axis=0, keepdims=True)
            weights = jnp.exp2(scores * factor - highest * factor)
            total = jnp.sum(weights, axis=0, keepdims=True)
            value = jnp.dot(values[head], weights.astype(BF), preferred_element_type=F32) / total
            mixed += [value[:, s * lanes : (s + 1) * lanes] for s in range(sides)]
        for position in range(4):
            block = mixed[position]
            for g in range(4):
                if g != position:
                    shift = (g - position) * tokens % lanes
                    block = jnp.where(group == g, pltpu.roll(mixed[g], shift, 1), block)
            out_ref[quarters * position + quarter] = block.astype(BF)


def merge_kernel(
    x_ref, w_out_ref, gain_ref, bias_ref, *refs
):
    *sources, out_ref, att_ref, w_ref, sems = refs
    me = lax.axis_index("wide")
    position, quarter = me // 4, me % 4
    blocks, dim, lanes = x_ref.shape
    pairs = blocks // 2
    early, out_width = sources[0].shape
    depth = early + sources[4].shape[0]
    width = w_out_ref.shape[1]
    copies = []
    for k, source in enumerate(sources):
        rows = source.shape[0]
        spot = pl.multiple_of(flipped(quarter, k % 4) * depth + k // 4 * early, 16)
        copies.append(pltpu.make_async_copy(source, w_ref.at[pl.ds(spot, rows), :], sems.at[k]))
        copies[-1].start()
    left = lax.broadcasted_iota(jnp.int32, (dim, lanes), 1) < lanes // 2
    for pair in range(pairs):
        first, second = x_ref[pair].astype(F32), x_ref[pairs + pair].astype(F32)
        upper = jnp.where(left, first, pltpu.roll(second, lanes // 2, 1))
        lower = jnp.where(left, pltpu.roll(first, lanes // 2, 1), second)
        att_ref[2 * dim * pair : 2 * dim * (pair + 1), :] = jnp.concatenate([upper, lower], 0).astype(BF)
    mixed = lax.dot_general(
        att_ref[...], w_out_ref[...], (((0,), (0,)), ((), ())), preferred_element_type=F32
    )
    mixed = mixed.astype(BF).astype(F32)
    centre = jnp.sum(mixed, axis=1, keepdims=True) / width
    centered = mixed - centre
    square = jnp.sum(centered * centered, axis=1, keepdims=True)
    here = pl.ds(pl.multiple_of(position * width, LANES), width)
    gain, bias = gain_ref[:, here], bias_ref[:, here]
    row = lax.broadcasted_iota(jnp.int32, (16, width), 0)
    extra = jnp.zeros((16, width), F32)
    for k, line in enumerate(pieces(gain, 2) + pieces(bias, 2)):
        extra = jnp.where(row == k, line, extra)
    left_side = jnp.concatenate([(centered * gain).astype(BF), extra.astype(BF)], 0)
    lane = lax.broadcasted_iota(jnp.int32, (lanes, LANES), 1)
    stats = jnp.zeros((lanes, LANES), F32)
    for k, column in enumerate(pieces(centre, 3) + pieces(square, 3)):
        stats = jnp.where(lane == k, column, stats)
    stats = stats.astype(BF)
    for copy in copies:
        copy.wait()
    planes, tokens, _ = out_ref.shape
    half = tokens // 2
    step = 2 * LANES
    shared = [None] * tokens
    for begin in range(0, out_width, step):
        part = jnp.dot(left_side, w_ref[:, begin : begin + step], preferred_element_type=F32)
        for plane in range(planes):
            out_ref[flipped(position, plane), :, begin : begin + step] = part[plane * tokens : (plane + 1) * tokens].astype(BF)
        scale = part[lanes : lanes + 1] + part[lanes + 1 : lanes + 2]
        shift = part[lanes + 2 : lanes + 3] + part[lanes + 3 : lanes + 4]
        for k in range(step // LANES):
            shared[begin // LANES + k] = scale[:, k * LANES : (k + 1) * LANES]
            shared[half + begin // LANES + k] = shift[:, k * LANES : (k + 1) * LANES]
    shared = jnp.concatenate(shared, 0).astype(BF)
    for plane in range(planes):
        out_ref[flipped(position, plane), :, out_width : out_width + LANES] = shared
        out_ref[flipped(position, plane), :, out_width + LANES :] = stats[plane * tokens : (plane + 1) * tokens]


def route_kernel(x0, x1, x2, x3, router_ref, ids_ref, out_ref, *, merge_width, experts):
    blocks = (x0, x1, x2, x3)
    planes, tokens = len(blocks), x0.shape[0]
    out_width = out_ref.shape[1] - LANES
    half = tokens // 2
    stats = [blocks[p][:, out_width + LANES :].astype(F32) for p in range(planes)]
    shared = [blocks[p][:, out_width : out_width + LANES].astype(F32) for p in range(planes)]
    centres = [s[:, 0:1] + s[:, 1:2] + s[:, 2:3] for s in stats]
    squares = [s[:, 3:4] + s[:, 4:5] + s[:, 5:6] for s in stats]
    mean = sum(centres) / planes
    offsets = [c - mean for c in centres]
    spread = sum(q + (merge_width // planes) * (o * o) for q, o in zip(squares, offsets)) / merge_width
    inverse = lax.rsqrt(spread + norm_eps)
    bias = sum(shared)
    for k in range(out_width // LANES):
        cut = slice(k * LANES, (k + 1) * LANES)
        total = sum(blocks[p][:, cut].astype(F32) for p in range(planes))
        total += sum(offsets[p] * shared[p][k : k + 1] for p in range(planes))
        out_ref[:, cut] = (total * inverse + bias[half + k : half + k + 1]).astype(BF)
    logits = jnp.dot(out_ref[:, :out_width], router_ref[...], preferred_element_type=F32)
    lane = lax.broadcasted_iota(jnp.int32, (tokens, LANES), 1)
    expert = lane % experts
    chosen = lane < 0
    for k in range(ids_ref.shape[1]):
        chosen = chosen | (ids_ref[:, k : k + 1] == expert)
    gates = jnp.where(chosen & (lane < 2 * experts), 1.0 / (1.0 + jnp.exp(-logits)), 0.0)
    total = jnp.sum(jnp.where(lane < experts, gates, 0.0), axis=1, keepdims=True)
    weight = route_scale * gates / total
    high, low = pieces(weight, 2)
    out_ref[:, out_width:] = jnp.where(lane < experts, high, low).astype(BF)


def expert_kernel(*refs, experts):
    *blocks, g0, g1, u0, u1, d0, d1, out_ref, x_ref = refs
    tokens, width = out_ref.shape[1:]
    expert = lax.axis_index("wide") // 2
    lane = lax.broadcasted_iota(jnp.int32, (tokens, LANES), 1)
    weights = []
    for k, block in enumerate(blocks):
        x_ref[k * tokens : (k + 1) * tokens, :] = block[:, :width]
        picked = (lane == expert) | (lane == expert + experts)
        picked = jnp.where(picked, block[:, width:].astype(F32), 0.0)
        weights.append(jnp.sum(picked, axis=1, keepdims=True))
    inputs = x_ref[...]
    turned = (((1,), (1,)), ((), ()))
    hidden = []
    for gate_ref, up_ref in ((g0, u0), (g1, u1)):
        gate = lax.dot_general(inputs, gate_ref[0], turned, preferred_element_type=F32)
        up = lax.dot_general(inputs, up_ref[0], turned, preferred_element_type=F32)
        hidden.append((gate / (1.0 + jnp.exp(-gate)) * up).astype(BF))
    step = 4 * LANES
    for begin in range(0, width, step):
        cut = slice(begin, begin + step)
        product = jnp.dot(hidden[0], d0[0, :, cut], preferred_element_type=F32)
        product += jnp.dot(hidden[1], d1[0, :, cut], preferred_element_type=F32)
        for k in range(len(blocks)):
            out_ref[k, :, cut] = (product[k * tokens : (k + 1) * tokens] * weights[k]).astype(BF)


def crossed(value, mask):
    pairs = [(source, source ^ mask) for source in range(lax.axis_size("wide"))]
    return lax.ppermute(value, "wide", pairs)


def local(
    qkv, grid, w_out, ln_gain, ln_bias, w_merge, w_router, expert_ids, slot_pos, w_gate, w_up, w_down
):
    devices = lax.axis_size("wide")
    rows = qkv.shape[0]
    vit_width = w_out.shape[0]
    experts = w_router.shape[1]
    out_width = w_merge.shape[1]
    tokens = rows // 4
    peers = devices // CLIPS
    suits = (
        devices == HEADS
        and peers == 8
        and rows == LANES
        and devices == 2 * experts
        and 2 * out_width == tokens * LANES
        and 4 * w_merge.shape[0] == vit_width
    )
    if not suits:
        return general(
            qkv, grid, w_out, ln_gain, ln_bias, w_merge, w_router, expert_ids, slot_pos, w_gate, w_up, w_down
        )
    part = vit_width // peers
    dim = vit_width // HEADS
    early = w_merge.shape[0] // 3
    early_y = crossed(w_merge[:early], 2)
    packed = pl.pallas_call(
        pack_kernel,
        out_shape=jax.ShapeDtypeStruct((peers, 3 * part, rows), BF),
        in_specs=[VMEM],
        out_specs=VMEM,
        compiler_params=params(32),
    )(qkv)
    clips = [[c * peers + i for i in range(peers)] for c in range(CLIPS)]
    gathered = lax.all_to_all(
        packed, "wide", split_axis=0, concat_axis=0, tiled=True, axis_index_groups=clips
    )
    halves = (jnp.swapaxes(w_gate, 1, 2), jnp.swapaxes(w_up, 1, 2), w_down)
    gathered, early_y, held, *sent = lax.optimization_barrier((gathered, early_y, w_merge, *halves))
    late = held[early:]
    late_y = crossed(late, 2)
    early_c, late_c, early_yc = crossed(held[:early], 1), crossed(late, 1), crossed(early_y, 1)
    weights = [w for half in zip(halves, [crossed(half, 1) for half in sent]) for w in half]
    attended = pl.pallas_call(
        attend_kernel,
        out_shape=jax.ShapeDtypeStruct((devices, dim, rows), BF),
        in_specs=[VMEM, SMEM],
        out_specs=VMEM,
        compiler_params=params(48),
        cost_estimate=cost(2**32, 2**22, 2**21),
    )(gathered, grid)
    returned = lax.all_to_all(attended, "wide", split_axis=0, concat_axis=0, tiled=True)
    returned, late_y = lax.optimization_barrier((returned, late_y))
    late_yc = crossed(late_y, 1)
    planes = devices // 4
    message = out_width + 2 * LANES
    partial = pl.pallas_call(
        merge_kernel,
        out_shape=jax.ShapeDtypeStruct((planes, tokens, message), BF),
        in_specs=[VMEM] * 4 + [HBM] * 8,
        out_specs=VMEM,
        scratch_shapes=[
            pltpu.VMEM((vit_width, rows), BF),
            pltpu.VMEM((vit_width, out_width), BF),
            pltpu.SemaphoreType.DMA((8,)),
        ],
        compiler_params=params(48),
    )(
        returned,
        w_out,
        ln_gain.reshape(1, 4 * vit_width),
        ln_bias.reshape(1, 4 * vit_width),
        w_merge[:early],
        early_c,
        early_y,
        early_yc,
        w_merge[early:],
        late_c,
        late_y,
        late_yc,
    )
    along = (4, 8, 12)
    arrived = [partial[0]] + [crossed(partial[k], mask) for k, mask in enumerate(along, 1)]
    router = jnp.concatenate(
        [w_router, w_router, jnp.zeros((out_width, LANES - 2 * experts), BF)], 1
    )
    routed = pl.pallas_call(
        lambda *refs: route_kernel(*refs, merge_width=4 * vit_width, experts=experts),
        out_shape=jax.ShapeDtypeStruct((tokens, out_width + LANES), BF),
        in_specs=[VMEM] * 6,
        out_specs=VMEM,
        compiler_params=params(32),
    )(*arrived, router, expert_ids)
    near = [routed] + [crossed(routed, mask) for mask in along]
    far = [crossed(block, 2) for block in near]

    def experts_of(blocks):
        return pl.pallas_call(
            lambda *refs: expert_kernel(*refs, experts=experts),
            out_shape=jax.ShapeDtypeStruct((planes, tokens, out_width), BF),
            in_specs=[VMEM] * (planes + 6),
            out_specs=VMEM,
            scratch_shapes=[pltpu.VMEM((planes * tokens, out_width), BF)],
            compiler_params=params(40),
            cost_estimate=cost(2**31, 2**24),
        )(*blocks, *weights)

    def scattered(blocks):
        others = [crossed(blocks[k], mask) for k, mask in enumerate(along, 1)]
        return blocks[0].astype(F32) + sum(block.astype(F32) for block in others)

    near_sum = scattered(experts_of(near))
    far_out, near_sum = lax.optimization_barrier((experts_of(far), near_sum))
    far_sum = scattered(far_out)
    return (near_sum + crossed(far_sum.astype(BF), 2).astype(F32)).astype(BF)


def solution(mesh):
    placed = (
        P(("grp", "wide"), None),
        P("grp", None),
        P(),
        P(),
        P(),
        P("wide", None),
        P(),
        P(("grp", "wide"), None),
        P(("grp", "wide"), None),
        P("wide", None, None),
        P("wide", None, None),
        P("wide", None, None),
    )
    return jax.shard_map(
        local, mesh=mesh, in_specs=placed, out_specs=P(("grp", "wide"), None), check_vma=False
    )
```

```python
import jax
import jax.numpy as jnp
from jax import lax
from jax.experimental import pallas as pl
from jax.experimental.pallas import tpu as pltpu
from jax.sharding import PartitionSpec as P

HEADS = 16
CLIPS = 2


route_scale = 2.446
norm_eps = 1e-05


def swapped(value, axis, stride):
    mask = 2**stride
    pairs = [(source, source ^ mask) for source in range(lax.axis_size(axis))]
    return lax.ppermute(value, axis, pairs)


def ordered_pair(own_part, partner, upper_bit):
    return jnp.where(
        upper_bit == 1,
        jnp.concatenate([partner, own_part], 0),
        jnp.concatenate([own_part, partner], 0),
    )


def general(
    qkv,
    grid,
    w_out,
    ln_gain,
    ln_bias,
    w_merge,
    w_router,
    expert_ids,
    slot_pos,
    w_gate,
    w_up,
    w_down,
):
    devices = lax.axis_size("wide")
    position_self = lax.axis_index("wide")
    vit_width = w_out.shape[0]
    head_dim = vit_width // HEADS
    groups = devices // HEADS
    local_rows = qkv.shape[0]
    sub_rows = local_rows // groups
    per_clip = devices // CLIPS
    query_send = (
        qkv[:, :vit_width]
        .reshape(groups, sub_rows, HEADS, head_dim)
        .transpose(2, 0, 1, 3)
        .reshape(devices, sub_rows, head_dim)
    )
    key_value = jnp.concatenate(
        [
            qkv[:, vit_width : 2 * vit_width].reshape(local_rows, HEADS, head_dim),
            qkv[:, 2 * vit_width :].reshape(local_rows, HEADS, head_dim),
        ],
        axis=2,
    )
    spread_send = jnp.broadcast_to(
        key_value.transpose(1, 0, 2)[:, None], (HEADS, groups, local_rows, 2 * head_dim)
    ).reshape(devices, local_rows, 2 * head_dim)
    queries, key_rows = (
        lax.all_to_all(query_send, "wide", split_axis=0, concat_axis=0, tiled=True),
        lax.all_to_all(spread_send, "wide", split_axis=0, concat_axis=0, tiled=True),
    )
    key_rows = key_rows[None]
    key_groups = key_rows.shape[0]
    key_count = key_rows.shape[2]
    key_place = (
        jnp.arange(per_clip, dtype=jnp.int32)[None, :, None] * local_rows
        + jnp.arange(key_groups, dtype=jnp.int32)[:, None, None] * local_rows
        + jnp.arange(key_count, dtype=jnp.int32)[None, None, :]
    ).reshape(-1)
    patch_counts = grid[:, 0] * grid[:, 1]
    clip_queries = queries.reshape(CLIPS, per_clip * sub_rows, head_dim)
    query_block_rows = min(512, per_clip * sub_rows)
    score_scale = head_dim ** (-0.5)

    def attend(clip_index):
        key_block = lax.dynamic_slice_in_dim(key_rows, clip_index * per_clip, per_clip, 1).reshape(
            -1, 2 * head_dim
        )
        visible = key_place < lax.dynamic_index_in_dim(patch_counts, clip_index, 0, keepdims=False)
        query_all = lax.dynamic_index_in_dim(clip_queries, clip_index, 0, keepdims=False)

        def one_block(query_block):
            scores = (
                lax.dot_general(
                    query_block,
                    key_block[:, :head_dim],
                    (((1,), (1,)), ((), ())),
                    preferred_element_type=jnp.float32,
                )
                * score_scale
            )
            scores = jnp.where(visible[None, :], scores, -jnp.inf)
            highest = jnp.max(scores, axis=1, keepdims=True)
            weights = jnp.exp(scores - highest)
            running = jnp.sum(weights, axis=1, keepdims=True)
            mixture = jnp.dot(
                weights.astype(jnp.bfloat16),
                key_block[:, head_dim:],
                preferred_element_type=jnp.float32,
            )
            return (mixture / running).astype(jnp.bfloat16)

        return lax.map(one_block, query_all.reshape(-1, query_block_rows, head_dim)).reshape(
            -1, head_dim
        )

    attended = lax.map(attend, jnp.arange(CLIPS, dtype=jnp.int32))
    returned = lax.all_to_all(
        attended.reshape(devices, sub_rows, head_dim),
        "wide",
        split_axis=0,
        concat_axis=0,
        tiled=True,
    )
    attention = (
        returned.reshape(HEADS, groups, sub_rows, head_dim)
        .transpose(1, 2, 0, 3)
        .reshape(local_rows, vit_width)
    )
    projected = jnp.dot(attention, w_out, preferred_element_type=jnp.float32).astype(jnp.bfloat16)
    merged = projected.reshape(local_rows // 4, 4 * vit_width).astype(jnp.float32)
    centre = jnp.mean(merged, axis=1, keepdims=True)
    centered = merged - centre
    spread = jnp.mean(centered * centered, axis=1, keepdims=True)
    normed = (centered * lax.rsqrt(spread + norm_eps) * ln_gain + ln_bias).astype(jnp.bfloat16)
    tok_groups = min(8, devices)
    feat_groups = devices // tok_groups
    merge_rows = w_merge
    for bit_index in range(tok_groups.bit_length() - 1):
        partner = swapped(merge_rows, "wide", bit_index)
        upper_bit = position_self // (1 << bit_index) % 2
        merge_rows = ordered_pair(merge_rows, partner, upper_bit)
    token_count = normed.shape[0]
    part_rows = token_count // tok_groups
    feat_width = normed.shape[1] // feat_groups
    out_width = w_merge.shape[1]
    merge_send = (
        normed.reshape(tok_groups, part_rows, feat_groups, feat_width)
        .transpose(2, 0, 1, 3)
        .reshape(devices, part_rows, feat_width)
    )
    flat_rows = lax.all_to_all(merge_send, "wide", split_axis=0, concat_axis=0, tiled=True).reshape(
        -1, feat_width
    )
    partial_value = jnp.dot(flat_rows, merge_rows, preferred_element_type=jnp.float32).reshape(
        devices, -1, out_width
    )
    summed = lax.all_to_all(partial_value, "wide", split_axis=0, concat_axis=0, tiled=True)
    tokens = (
        jnp.sum(summed.reshape(feat_groups, tok_groups, part_rows, out_width), axis=0)
        .reshape(token_count, out_width)
        .astype(jnp.bfloat16)
    )
    logits = jnp.dot(tokens, w_router, preferred_element_type=jnp.float32)
    experts = w_router.shape[1]
    top_count = expert_ids.shape[1]
    matches = expert_ids[:, :, None] == jnp.arange(experts, dtype=jnp.int32)[None, None, :]
    chosen = jnp.sum(jnp.where(matches, logits[:, None, :], 0.0), axis=2)
    gate_values = jax.nn.sigmoid(chosen)
    route_weight = route_scale * gate_values / jnp.sum(gate_values, axis=1, keepdims=True)
    capacity = min(token_count, 2 * token_count * top_count // experts)
    slot_count = experts * capacity
    target = expert_ids * capacity + slot_pos
    one_hot = jnp.any(
        target[None, :, :] == jnp.arange(slot_count, dtype=jnp.int32)[:, None, None], axis=2
    ).astype(jnp.bfloat16)
    buffer = jnp.dot(one_hot, tokens, preferred_element_type=jnp.float32).astype(jnp.bfloat16)
    gate_half = w_gate[0]
    up_half = w_up[0]
    down_half = w_down[0]
    half_cap = capacity // 2
    dispatch = buffer.reshape(devices, half_cap, out_width)
    portion = lax.all_to_all(dispatch, "wide", split_axis=0, concat_axis=0, tiled=True)
    item_count = portion.shape[1]
    partner_rows = swapped(portion, "wide", 0)
    both_rows = jnp.concatenate([portion, partner_rows], axis=1)
    flat_rows = both_rows.reshape(-1, out_width)
    gate_part = jnp.dot(flat_rows, gate_half, preferred_element_type=jnp.float32)
    up_part = jnp.dot(flat_rows, up_half, preferred_element_type=jnp.float32)
    hidden = (jax.nn.silu(gate_part) * up_part).astype(jnp.bfloat16)
    product = (
        jnp.dot(hidden, down_half, preferred_element_type=jnp.float32)
        .astype(jnp.bfloat16)
        .reshape(devices, 2 * item_count, out_width)
    )
    from_partner = swapped(product[:, item_count:], "wide", 0)
    joined = (
        product[:, :item_count].astype(jnp.float32) + from_partner.astype(jnp.float32)
    ).astype(jnp.bfloat16)
    answers = lax.all_to_all(joined, "wide", split_axis=0, concat_axis=0, tiled=True)
    slot_result = answers.reshape(slot_count, out_width)
    slot_result = lax.optimization_barrier(slot_result)
    picked = jnp.take(slot_result, target.reshape(-1), axis=0).reshape(
        token_count, top_count, out_width
    )
    return jnp.sum(picked.astype(jnp.float32) * route_weight[:, :, None], axis=1).astype(
        jnp.bfloat16
    )


BF = jnp.bfloat16
F32 = jnp.float32
VMEM = pl.BlockSpec(memory_space=pltpu.VMEM)
SMEM = pl.BlockSpec(memory_space=pltpu.SMEM)
HBM = pl.BlockSpec(memory_space=pltpu.HBM)
LANES = 128
MASKED = -1e30
LOG2E = 1.4426950408889634


def params(mib):
    return pltpu.CompilerParams(vmem_limit_bytes=mib * 2**20)


def cost(flops, size, exps=0):
    return pl.CostEstimate(flops=flops, bytes_accessed=size, transcendentals=exps)


def flipped(number, bits):
    low = (number % 2 + bits % 2) % 2
    return 2 * ((number // 2 + bits // 2) % 2) + low


def pieces(value, count):
    out = []
    for _ in range(count):
        piece = value.astype(BF).astype(F32)
        out.append(piece)
        value = value - piece
    return out


def pack_kernel(qkv_ref, out_ref):
    rows, width = qkv_ref.shape
    tokens = rows // 4
    peers, parts, _ = out_ref.shape
    source = lax.broadcasted_iota(jnp.int32, (rows, rows), 0)
    place = lax.broadcasted_iota(jnp.int32, (rows, rows), 1)
    order = jnp.where(source == 4 * (place % tokens) + place // tokens, 1.0, 0.0).astype(BF)
    part = parts // 3
    third = width // 3
    for kind in range(3):
        turned = lax.dot_general(
            qkv_ref[:, kind * third : (kind + 1) * third],
            order,
            (((0,), (0,)), ((), ())),
            preferred_element_type=F32,
        ).astype(BF)
        for peer in range(peers):
            out_ref[peer, kind * part : (kind + 1) * part, :] = turned[peer * part : (peer + 1) * part]


def attend_kernel(x_ref, grid_ref, out_ref):
    peers, parts, lanes = x_ref.shape
    part = parts // 3
    dim = part // 2
    quarters = 4
    sides = peers // quarters
    tokens = lanes // 4
    clip = lax.axis_index("wide") // peers
    count = grid_ref[clip, 0] * grid_ref[clip, 1]
    factor = dim ** (-0.5) * LOG2E
    keys = jnp.concatenate([x_ref[s, part : 2 * part, :] for s in range(peers)], 1)
    lane = lax.broadcasted_iota(jnp.int32, (16, peers * lanes), 1)
    row = lax.broadcasted_iota(jnp.int32, (16, peers * lanes), 0)
    inner = lane % lanes
    place = lane // lanes * lanes + 4 * (inner % tokens) + inner // tokens
    hidden = jnp.where((row == 0) & (place >= count), MASKED, 0.0).astype(BF)
    keys = jnp.concatenate([keys, hidden], 0).T
    values = jnp.concatenate([x_ref[s, 2 * part :, :] for s in range(peers)], 1).astype(F32)
    values = [values[:dim].astype(BF), values[dim:].astype(BF)]
    ones = jnp.where(lax.broadcasted_iota(jnp.int32, (16, sides * lanes), 0) == 0, 1.0, 0.0).astype(BF)
    head_row = lax.broadcasted_iota(jnp.int32, (part, sides * lanes), 0) // dim
    group = lax.broadcasted_iota(jnp.int32, (dim, lanes), 1) // tokens
    for quarter in range(quarters):
        query = jnp.concatenate(
            [x_ref[quarter + quarters * s, :part, :] for s in range(sides)], 1
        ).astype(F32)
        mixed = []
        for head in range(2):
            own = jnp.concatenate([jnp.where(head_row == head, query, 0.0).astype(BF), ones], 0)
            scores = jnp.dot(keys, own, preferred_element_type=F32)
            highest = jnp.max(scores, axis=0, keepdims=True)
            weights = jnp.exp2(scores * factor - highest * factor)
            total = jnp.sum(weights, axis=0, keepdims=True)
            value = jnp.dot(values[head], weights.astype(BF), preferred_element_type=F32) / total
            mixed += [value[:, s * lanes : (s + 1) * lanes] for s in range(sides)]
        for position in range(4):
            block = mixed[position]
            for g in range(4):
                if g != position:
                    shift = (g - position) * tokens % lanes
                    block = jnp.where(group == g, pltpu.roll(mixed[g], shift, 1), block)
            out_ref[quarters * position + quarter] = block.astype(BF)


def merge_kernel(
    x_ref, w_out_ref, gain_ref, bias_ref, w0, w1, w2, w3, out_ref, att_ref, w_ref, sems
):
    me = lax.axis_index("wide")
    position, quarter = me // 4, me % 4
    blocks, dim, lanes = x_ref.shape
    pairs = blocks // 2
    depth = w0.shape[0]
    out_width = w0.shape[1]
    width = w_out_ref.shape[1]
    copies = []
    for k, source in enumerate((w0, w1, w2, w3)):
        spot = pl.multiple_of(flipped(quarter, k) * depth, depth)
        copies.append(pltpu.make_async_copy(source, w_ref.at[pl.ds(spot, depth), :], sems.at[k]))
        copies[-1].start()
    left = lax.broadcasted_iota(jnp.int32, (dim, lanes), 1) < lanes // 2
    for pair in range(pairs):
        first, second = x_ref[pair].astype(F32), x_ref[pairs + pair].astype(F32)
        upper = jnp.where(left, first, pltpu.roll(second, lanes // 2, 1))
        lower = jnp.where(left, pltpu.roll(first, lanes // 2, 1), second)
        att_ref[2 * dim * pair : 2 * dim * (pair + 1), :] = jnp.concatenate([upper, lower], 0).astype(BF)
    mixed = lax.dot_general(
        att_ref[...], w_out_ref[...], (((0,), (0,)), ((), ())), preferred_element_type=F32
    )
    mixed = mixed.astype(BF).astype(F32)
    centre = jnp.sum(mixed, axis=1, keepdims=True) / width
    centered = mixed - centre
    square = jnp.sum(centered * centered, axis=1, keepdims=True)
    here = pl.ds(pl.multiple_of(position * width, LANES), width)
    gain, bias = gain_ref[:, here], bias_ref[:, here]
    row = lax.broadcasted_iota(jnp.int32, (16, width), 0)
    extra = jnp.zeros((16, width), F32)
    for k, line in enumerate(pieces(gain, 2) + pieces(bias, 2)):
        extra = jnp.where(row == k, line, extra)
    left_side = jnp.concatenate([(centered * gain).astype(BF), extra.astype(BF)], 0)
    lane = lax.broadcasted_iota(jnp.int32, (lanes, LANES), 1)
    stats = jnp.zeros((lanes, LANES), F32)
    for k, column in enumerate(pieces(centre, 3) + pieces(square, 3)):
        stats = jnp.where(lane == k, column, stats)
    stats = stats.astype(BF)
    for copy in copies:
        copy.wait()
    planes, tokens, _ = out_ref.shape
    half = tokens // 2
    step = 2 * LANES
    shared = [None] * tokens
    for begin in range(0, out_width, step):
        part = jnp.dot(left_side, w_ref[:, begin : begin + step], preferred_element_type=F32)
        for plane in range(planes):
            out_ref[flipped(position, plane), :, begin : begin + step] = part[plane * tokens : (plane + 1) * tokens].astype(BF)
        scale = part[lanes : lanes + 1] + part[lanes + 1 : lanes + 2]
        shift = part[lanes + 2 : lanes + 3] + part[lanes + 3 : lanes + 4]
        for k in range(step // LANES):
            shared[begin // LANES + k] = scale[:, k * LANES : (k + 1) * LANES]
            shared[half + begin // LANES + k] = shift[:, k * LANES : (k + 1) * LANES]
    shared = jnp.concatenate(shared, 0).astype(BF)
    for plane in range(planes):
        out_ref[flipped(position, plane), :, out_width : out_width + LANES] = shared
        out_ref[flipped(position, plane), :, out_width + LANES :] = stats[plane * tokens : (plane + 1) * tokens]


def route_kernel(x0, x1, x2, x3, router_ref, ids_ref, out_ref, *, merge_width, experts):
    blocks = (x0, x1, x2, x3)
    planes, tokens = len(blocks), x0.shape[0]
    out_width = out_ref.shape[1] - LANES
    half = tokens // 2
    stats = [blocks[p][:, out_width + LANES :].astype(F32) for p in range(planes)]
    shared = [blocks[p][:, out_width : out_width + LANES].astype(F32) for p in range(planes)]
    centres = [s[:, 0:1] + s[:, 1:2] + s[:, 2:3] for s in stats]
    squares = [s[:, 3:4] + s[:, 4:5] + s[:, 5:6] for s in stats]
    mean = sum(centres) / planes
    offsets = [c - mean for c in centres]
    spread = sum(q + (merge_width // planes) * (o * o) for q, o in zip(squares, offsets)) / merge_width
    inverse = lax.rsqrt(spread + norm_eps)
    bias = sum(shared)
    for k in range(out_width // LANES):
        cut = slice(k * LANES, (k + 1) * LANES)
        total = sum(blocks[p][:, cut].astype(F32) for p in range(planes))
        total += sum(offsets[p] * shared[p][k : k + 1] for p in range(planes))
        out_ref[:, cut] = (total * inverse + bias[half + k : half + k + 1]).astype(BF)
    logits = jnp.dot(out_ref[:, :out_width], router_ref[...], preferred_element_type=F32)
    lane = lax.broadcasted_iota(jnp.int32, (tokens, LANES), 1)
    expert = lane % experts
    chosen = lane < 0
    for k in range(ids_ref.shape[1]):
        chosen = chosen | (ids_ref[:, k : k + 1] == expert)
    gates = jnp.where(chosen & (lane < 2 * experts), 1.0 / (1.0 + jnp.exp(-logits)), 0.0)
    total = jnp.sum(jnp.where(lane < experts, gates, 0.0), axis=1, keepdims=True)
    weight = route_scale * gates / total
    high, low = pieces(weight, 2)
    out_ref[:, out_width:] = jnp.where(lane < experts, high, low).astype(BF)


def expert_kernel(*refs, experts, cuts):
    *blocks, gate_hbm, up_hbm, down_hbm, own_ref, other_ref, x_ref, gate_ref, up_ref, down_ref, sems = refs
    tokens, width = own_ref.shape[1:]
    half = len(blocks) // 2
    copies = []
    for k, cut in enumerate(cuts):
        for kind, source, target in ((0, gate_hbm, gate_ref), (1, up_hbm, up_ref)):
            copies.append(pltpu.make_async_copy(source.at[0, cut, :], target.at[cut, :], sems.at[2 * k + kind]))
            copies[-1].start()
    last = pltpu.make_async_copy(down_hbm.at[0], down_ref, sems.at[2 * len(cuts)])
    last.start()
    expert = lax.axis_index("wide") // 2
    lane = lax.broadcasted_iota(jnp.int32, (tokens, LANES), 1)
    weights = []
    for k, block in enumerate(blocks):
        x_ref[k * tokens : (k + 1) * tokens, :] = block[:, :width]
        picked = (lane == expert) | (lane == expert + experts)
        picked = jnp.where(picked, block[:, width:].astype(F32), 0.0)
        weights.append(jnp.sum(picked, axis=1, keepdims=True))
    inputs = x_ref[...]
    turned = (((1,), (1,)), ((), ()))
    hidden = []
    for k, cut in enumerate(cuts):
        copies[2 * k].wait()
        gate = lax.dot_general(inputs, gate_ref[cut, :], turned, preferred_element_type=F32)
        copies[2 * k + 1].wait()
        up = lax.dot_general(inputs, up_ref[cut, :], turned, preferred_element_type=F32)
        hidden.append((gate / (1.0 + jnp.exp(-gate)) * up).astype(BF))
    hidden = jnp.concatenate(hidden, 1)
    last.wait()
    step = 4 * LANES
    for begin in range(0, width, step):
        product = jnp.dot(hidden, down_ref[:, begin : begin + step], preferred_element_type=F32)
        for k in range(len(blocks)):
            value = (product[k * tokens : (k + 1) * tokens] * weights[k]).astype(BF)
            out_ref = own_ref if k < half else other_ref
            out_ref[k % half, :, begin : begin + step] = value


def crossed(value, mask):
    pairs = [(source, source ^ mask) for source in range(lax.axis_size("wide"))]
    return lax.ppermute(value, "wide", pairs)


def local(
    qkv, grid, w_out, ln_gain, ln_bias, w_merge, w_router, expert_ids, slot_pos, w_gate, w_up, w_down
):
    devices = lax.axis_size("wide")
    rows = qkv.shape[0]
    vit_width = w_out.shape[0]
    experts = w_router.shape[1]
    out_width = w_merge.shape[1]
    tokens = rows // 4
    peers = devices // CLIPS
    suits = (
        devices == HEADS
        and peers == 8
        and rows == LANES
        and devices == 2 * experts
        and 2 * out_width == tokens * LANES
        and 4 * w_merge.shape[0] == vit_width
    )
    if not suits:
        return general(
            qkv, grid, w_out, ln_gain, ln_bias, w_merge, w_router, expert_ids, slot_pos, w_gate, w_up, w_down
        )
    part = vit_width // peers
    dim = vit_width // HEADS
    packed = pl.pallas_call(
        pack_kernel,
        out_shape=jax.ShapeDtypeStruct((peers, 3 * part, rows), BF),
        in_specs=[VMEM],
        out_specs=VMEM,
        compiler_params=params(8),
    )(qkv)
    clips = [[c * peers + i for i in range(peers)] for c in range(CLIPS)]
    gathered = lax.all_to_all(
        packed, "wide", split_axis=0, concat_axis=0, tiled=True, axis_index_groups=clips
    )
    gathered, held = lax.optimization_barrier((gathered, w_merge))
    held_y = crossed(held, 2)
    attended = pl.pallas_call(
        attend_kernel,
        out_shape=jax.ShapeDtypeStruct((devices, dim, rows), BF),
        in_specs=[VMEM, SMEM],
        out_specs=VMEM,
        compiler_params=params(20),
        cost_estimate=cost(2**32, 2**22, 2**21),
    )(gathered, grid)
    held_c = crossed(held, 1)
    returned = lax.all_to_all(attended, "wide", split_axis=0, concat_axis=0, tiled=True)
    returned, held_y = lax.optimization_barrier((returned, held_y))
    held_yc = crossed(held_y, 1)
    planes = devices // 4
    message = out_width + 2 * LANES
    partial = pl.pallas_call(
        merge_kernel,
        out_shape=jax.ShapeDtypeStruct((planes, tokens, message), BF),
        in_specs=[VMEM, VMEM, VMEM, VMEM, HBM, HBM, HBM, HBM],
        out_specs=VMEM,
        scratch_shapes=[
            pltpu.VMEM((vit_width, rows), BF),
            pltpu.VMEM((vit_width, out_width), BF),
            pltpu.SemaphoreType.DMA((4,)),
        ],
        compiler_params=params(20),
    )(
        returned,
        w_out,
        ln_gain.reshape(1, 4 * vit_width),
        ln_bias.reshape(1, 4 * vit_width),
        held,
        held_c,
        held_y,
        held_yc,
    )
    along = (4, 8, 12)
    arrived = [partial[0]] + [crossed(partial[k], mask) for k, mask in enumerate(along, 1)]
    router = jnp.concatenate(
        [w_router, w_router, jnp.zeros((out_width, LANES - 2 * experts), BF)], 1
    )
    routed = pl.pallas_call(
        lambda *refs: route_kernel(*refs, merge_width=4 * vit_width, experts=experts),
        out_shape=jax.ShapeDtypeStruct((tokens, out_width + LANES), BF),
        in_specs=[VMEM] * 6,
        out_specs=VMEM,
        compiler_params=params(6),
    )(*arrived, router, expert_ids)
    near = [routed] + [crossed(routed, mask) for mask in along]
    far = [crossed(block, 2) for block in near]
    gate_turned, up_turned = jnp.swapaxes(w_gate, 1, 2), jnp.swapaxes(w_up, 1, 2)

    inner = w_down.shape[1]
    cuts = [slice(k, min(k + 2 * LANES, inner)) for k in range(0, inner, 2 * LANES)]

    def experts_of(blocks):
        return pl.pallas_call(
            lambda *refs: expert_kernel(*refs, experts=experts, cuts=cuts),
            out_shape=[jax.ShapeDtypeStruct((planes, tokens, out_width), BF)] * 2,
            in_specs=[VMEM] * (2 * planes) + [HBM] * 3,
            out_specs=[VMEM, VMEM],
            scratch_shapes=[
                pltpu.VMEM((2 * planes * tokens, out_width), BF),
                pltpu.VMEM((inner, out_width), BF),
                pltpu.VMEM((inner, out_width), BF),
                pltpu.VMEM((inner, out_width), BF),
                pltpu.SemaphoreType.DMA((2 * len(cuts) + 1,)),
            ],
            compiler_params=params(32),
            cost_estimate=cost(2**32, 2**24),
        )(*blocks, *[crossed(block, 1) for block in blocks], gate_turned, up_turned, w_down)

    def scattered(blocks):
        others = [crossed(blocks[k], mask) for k, mask in enumerate(along, 1)]
        return blocks[0].astype(F32) + sum(block.astype(F32) for block in others)

    def paired(own, other):
        return (own.astype(F32) + crossed(other, 1).astype(F32)).astype(BF)

    near_own, near_other = experts_of(near)
    *far, near_own, near_other = lax.optimization_barrier((*far, near_own, near_other))
    far_own, far_other = experts_of(far)
    near_sum = scattered(paired(near_own, near_other))
    far_out, near_sum = lax.optimization_barrier((paired(far_own, far_other), near_sum))
    far_sum = scattered(far_out)
    return (near_sum + crossed(far_sum.astype(BF), 2).astype(F32)).astype(BF)


def solution(mesh):
    placed = (
        P(("grp", "wide"), None),
        P("grp", None),
        P(),
        P(),
        P(),
        P("wide", None),
        P(),
        P(("grp", "wide"), None),
        P(("grp", "wide"), None),
        P("wide", None, None),
        P("wide", None, None),
        P("wide", None, None),
    )
    return jax.shard_map(
        local, mesh=mesh, in_specs=placed, out_specs=P(("grp", "wide"), None), check_vma=False
    )
```

```python
import jax
import jax.numpy as jnp
from jax import lax
from jax.experimental import pallas as pl
from jax.experimental.pallas import tpu as pltpu
from jax.sharding import PartitionSpec as P

HEADS = 16
CLIPS = 2


route_scale = 2.446
norm_eps = 1e-05


def swapped(value, axis, stride):
    mask = 2**stride
    pairs = [(source, source ^ mask) for source in range(lax.axis_size(axis))]
    return lax.ppermute(value, axis, pairs)


def ordered_pair(own_part, partner, upper_bit):
    return jnp.where(
        upper_bit == 1,
        jnp.concatenate([partner, own_part], 0),
        jnp.concatenate([own_part, partner], 0),
    )


def general(
    qkv,
    grid,
    w_out,
    ln_gain,
    ln_bias,
    w_merge,
    w_router,
    expert_ids,
    slot_pos,
    w_gate,
    w_up,
    w_down,
):
    devices = lax.axis_size("wide")
    position_self = lax.axis_index("wide")
    vit_width = w_out.shape[0]
    head_dim = vit_width // HEADS
    groups = devices // HEADS
    local_rows = qkv.shape[0]
    sub_rows = local_rows // groups
    per_clip = devices // CLIPS
    query_send = (
        qkv[:, :vit_width]
        .reshape(groups, sub_rows, HEADS, head_dim)
        .transpose(2, 0, 1, 3)
        .reshape(devices, sub_rows, head_dim)
    )
    key_value = jnp.concatenate(
        [
            qkv[:, vit_width : 2 * vit_width].reshape(local_rows, HEADS, head_dim),
            qkv[:, 2 * vit_width :].reshape(local_rows, HEADS, head_dim),
        ],
        axis=2,
    )
    spread_send = jnp.broadcast_to(
        key_value.transpose(1, 0, 2)[:, None], (HEADS, groups, local_rows, 2 * head_dim)
    ).reshape(devices, local_rows, 2 * head_dim)
    queries, key_rows = (
        lax.all_to_all(query_send, "wide", split_axis=0, concat_axis=0, tiled=True),
        lax.all_to_all(spread_send, "wide", split_axis=0, concat_axis=0, tiled=True),
    )
    key_rows = key_rows[None]
    key_groups = key_rows.shape[0]
    key_count = key_rows.shape[2]
    key_place = (
        jnp.arange(per_clip, dtype=jnp.int32)[None, :, None] * local_rows
        + jnp.arange(key_groups, dtype=jnp.int32)[:, None, None] * local_rows
        + jnp.arange(key_count, dtype=jnp.int32)[None, None, :]
    ).reshape(-1)
    patch_counts = grid[:, 0] * grid[:, 1]
    clip_queries = queries.reshape(CLIPS, per_clip * sub_rows, head_dim)
    query_block_rows = min(512, per_clip * sub_rows)
    score_scale = head_dim ** (-0.5)

    def attend(clip_index):
        key_block = lax.dynamic_slice_in_dim(key_rows, clip_index * per_clip, per_clip, 1).reshape(
            -1, 2 * head_dim
        )
        visible = key_place < lax.dynamic_index_in_dim(patch_counts, clip_index, 0, keepdims=False)
        query_all = lax.dynamic_index_in_dim(clip_queries, clip_index, 0, keepdims=False)

        def one_block(query_block):
            scores = (
                lax.dot_general(
                    query_block,
                    key_block[:, :head_dim],
                    (((1,), (1,)), ((), ())),
                    preferred_element_type=jnp.float32,
                )
                * score_scale
            )
            scores = jnp.where(visible[None, :], scores, -jnp.inf)
            highest = jnp.max(scores, axis=1, keepdims=True)
            weights = jnp.exp(scores - highest)
            running = jnp.sum(weights, axis=1, keepdims=True)
            mixture = jnp.dot(
                weights.astype(jnp.bfloat16),
                key_block[:, head_dim:],
                preferred_element_type=jnp.float32,
            )
            return (mixture / running).astype(jnp.bfloat16)

        return lax.map(one_block, query_all.reshape(-1, query_block_rows, head_dim)).reshape(
            -1, head_dim
        )

    attended = lax.map(attend, jnp.arange(CLIPS, dtype=jnp.int32))
    returned = lax.all_to_all(
        attended.reshape(devices, sub_rows, head_dim),
        "wide",
        split_axis=0,
        concat_axis=0,
        tiled=True,
    )
    attention = (
        returned.reshape(HEADS, groups, sub_rows, head_dim)
        .transpose(1, 2, 0, 3)
        .reshape(local_rows, vit_width)
    )
    projected = jnp.dot(attention, w_out, preferred_element_type=jnp.float32).astype(jnp.bfloat16)
    merged = projected.reshape(local_rows // 4, 4 * vit_width).astype(jnp.float32)
    centre = jnp.mean(merged, axis=1, keepdims=True)
    centered = merged - centre
    spread = jnp.mean(centered * centered, axis=1, keepdims=True)
    normed = (centered * lax.rsqrt(spread + norm_eps) * ln_gain + ln_bias).astype(jnp.bfloat16)
    tok_groups = min(8, devices)
    feat_groups = devices // tok_groups
    merge_rows = w_merge
    for bit_index in range(tok_groups.bit_length() - 1):
        partner = swapped(merge_rows, "wide", bit_index)
        upper_bit = position_self // (1 << bit_index) % 2
        merge_rows = ordered_pair(merge_rows, partner, upper_bit)
    token_count = normed.shape[0]
    part_rows = token_count // tok_groups
    feat_width = normed.shape[1] // feat_groups
    out_width = w_merge.shape[1]
    merge_send = (
        normed.reshape(tok_groups, part_rows, feat_groups, feat_width)
        .transpose(2, 0, 1, 3)
        .reshape(devices, part_rows, feat_width)
    )
    flat_rows = lax.all_to_all(merge_send, "wide", split_axis=0, concat_axis=0, tiled=True).reshape(
        -1, feat_width
    )
    partial_value = jnp.dot(flat_rows, merge_rows, preferred_element_type=jnp.float32).reshape(
        devices, -1, out_width
    )
    summed = lax.all_to_all(partial_value, "wide", split_axis=0, concat_axis=0, tiled=True)
    tokens = (
        jnp.sum(summed.reshape(feat_groups, tok_groups, part_rows, out_width), axis=0)
        .reshape(token_count, out_width)
        .astype(jnp.bfloat16)
    )
    logits = jnp.dot(tokens, w_router, preferred_element_type=jnp.float32)
    experts = w_router.shape[1]
    top_count = expert_ids.shape[1]
    matches = expert_ids[:, :, None] == jnp.arange(experts, dtype=jnp.int32)[None, None, :]
    chosen = jnp.sum(jnp.where(matches, logits[:, None, :], 0.0), axis=2)
    gate_values = jax.nn.sigmoid(chosen)
    route_weight = route_scale * gate_values / jnp.sum(gate_values, axis=1, keepdims=True)
    capacity = min(token_count, 2 * token_count * top_count // experts)
    slot_count = experts * capacity
    target = expert_ids * capacity + slot_pos
    one_hot = jnp.any(
        target[None, :, :] == jnp.arange(slot_count, dtype=jnp.int32)[:, None, None], axis=2
    ).astype(jnp.bfloat16)
    buffer = jnp.dot(one_hot, tokens, preferred_element_type=jnp.float32).astype(jnp.bfloat16)
    gate_half = w_gate[0]
    up_half = w_up[0]
    down_half = w_down[0]
    half_cap = capacity // 2
    dispatch = buffer.reshape(devices, half_cap, out_width)
    portion = lax.all_to_all(dispatch, "wide", split_axis=0, concat_axis=0, tiled=True)
    item_count = portion.shape[1]
    partner_rows = swapped(portion, "wide", 0)
    both_rows = jnp.concatenate([portion, partner_rows], axis=1)
    flat_rows = both_rows.reshape(-1, out_width)
    gate_part = jnp.dot(flat_rows, gate_half, preferred_element_type=jnp.float32)
    up_part = jnp.dot(flat_rows, up_half, preferred_element_type=jnp.float32)
    hidden = (jax.nn.silu(gate_part) * up_part).astype(jnp.bfloat16)
    product = (
        jnp.dot(hidden, down_half, preferred_element_type=jnp.float32)
        .astype(jnp.bfloat16)
        .reshape(devices, 2 * item_count, out_width)
    )
    from_partner = swapped(product[:, item_count:], "wide", 0)
    joined = (
        product[:, :item_count].astype(jnp.float32) + from_partner.astype(jnp.float32)
    ).astype(jnp.bfloat16)
    answers = lax.all_to_all(joined, "wide", split_axis=0, concat_axis=0, tiled=True)
    slot_result = answers.reshape(slot_count, out_width)
    slot_result = lax.optimization_barrier(slot_result)
    picked = jnp.take(slot_result, target.reshape(-1), axis=0).reshape(
        token_count, top_count, out_width
    )
    return jnp.sum(picked.astype(jnp.float32) * route_weight[:, :, None], axis=1).astype(
        jnp.bfloat16
    )


BF = jnp.bfloat16
F32 = jnp.float32
VMEM = pl.BlockSpec(memory_space=pltpu.VMEM)
SMEM = pl.BlockSpec(memory_space=pltpu.SMEM)
HBM = pl.BlockSpec(memory_space=pltpu.HBM)
LANES = 128
MASKED = -1e30
LOG2E = 1.4426950408889634


def params(mib):
    return pltpu.CompilerParams(vmem_limit_bytes=mib * 2**20)


def cost(flops, size, exps=0):
    return pl.CostEstimate(flops=flops, bytes_accessed=size, transcendentals=exps)


def flipped(number, bits):
    low = (number % 2 + bits % 2) % 2
    return 2 * ((number // 2 + bits // 2) % 2) + low


def pieces(value, count):
    out = []
    for _ in range(count):
        piece = value.astype(BF).astype(F32)
        out.append(piece)
        value = value - piece
    return out


def pack_kernel(qkv_ref, out_ref):
    rows, width = qkv_ref.shape
    tokens = rows // 4
    peers, parts, _ = out_ref.shape
    source = lax.broadcasted_iota(jnp.int32, (rows, rows), 0)
    place = lax.broadcasted_iota(jnp.int32, (rows, rows), 1)
    order = jnp.where(source == 4 * (place % tokens) + place // tokens, 1.0, 0.0).astype(BF)
    part = parts // 3
    third = width // 3
    for kind in range(3):
        turned = lax.dot_general(
            qkv_ref[:, kind * third : (kind + 1) * third],
            order,
            (((0,), (0,)), ((), ())),
            preferred_element_type=F32,
        ).astype(BF)
        for peer in range(peers):
            out_ref[peer, kind * part : (kind + 1) * part, :] = turned[peer * part : (peer + 1) * part]


def attend_kernel(x_ref, grid_ref, out_ref):
    peers, parts, lanes = x_ref.shape
    part = parts // 3
    dim = part // 2
    quarters = 4
    sides = peers // quarters
    tokens = lanes // 4
    clip = lax.axis_index("wide") // peers
    count = grid_ref[clip, 0] * grid_ref[clip, 1]
    factor = dim ** (-0.5) * LOG2E
    keys = jnp.concatenate([x_ref[s, part : 2 * part, :] for s in range(peers)], 1)
    lane = lax.broadcasted_iota(jnp.int32, (16, peers * lanes), 1)
    row = lax.broadcasted_iota(jnp.int32, (16, peers * lanes), 0)
    inner = lane % lanes
    place = lane // lanes * lanes + 4 * (inner % tokens) + inner // tokens
    hidden = jnp.where((row == 0) & (place >= count), MASKED, 0.0).astype(BF)
    keys = jnp.concatenate([keys, hidden], 0).T
    values = jnp.concatenate([x_ref[s, 2 * part :, :] for s in range(peers)], 1).astype(F32)
    values = [values[:dim].astype(BF), values[dim:].astype(BF)]
    ones = jnp.where(lax.broadcasted_iota(jnp.int32, (16, sides * lanes), 0) == 0, 1.0, 0.0).astype(BF)
    head_row = lax.broadcasted_iota(jnp.int32, (part, sides * lanes), 0) // dim
    group = lax.broadcasted_iota(jnp.int32, (dim, lanes), 1) // tokens
    for quarter in range(quarters):
        query = jnp.concatenate(
            [x_ref[quarter + quarters * s, :part, :] for s in range(sides)], 1
        ).astype(F32)
        mixed = []
        for head in range(2):
            own = jnp.concatenate([jnp.where(head_row == head, query, 0.0).astype(BF), ones], 0)
            scores = jnp.dot(keys, own, preferred_element_type=F32)
            highest = jnp.max(scores, axis=0, keepdims=True)
            weights = jnp.exp2(scores * factor - highest * factor)
            total = jnp.sum(weights, axis=0, keepdims=True)
            value = jnp.dot(values[head], weights.astype(BF), preferred_element_type=F32) / total
            mixed += [value[:, s * lanes : (s + 1) * lanes] for s in range(sides)]
        for position in range(4):
            block = mixed[position]
            for g in range(4):
                if g != position:
                    shift = (g - position) * tokens % lanes
                    block = jnp.where(group == g, pltpu.roll(mixed[g], shift, 1), block)
            out_ref[quarters * position + quarter] = block.astype(BF)


def merge_kernel(
    x_ref, w_out_ref, gain_ref, bias_ref, w0, w1, w2, w3, out_ref, att_ref, w_ref, sems
):
    me = lax.axis_index("wide")
    position, quarter = me // 4, me % 4
    blocks, dim, lanes = x_ref.shape
    pairs = blocks // 2
    depth = w0.shape[0]
    out_width = w0.shape[1]
    width = w_out_ref.shape[1]
    copies = []
    for k, source in enumerate((w0, w1, w2, w3)):
        spot = pl.multiple_of(flipped(quarter, k) * depth, depth)
        copies.append(pltpu.make_async_copy(source, w_ref.at[pl.ds(spot, depth), :], sems.at[k]))
        copies[-1].start()
    left = lax.broadcasted_iota(jnp.int32, (dim, lanes), 1) < lanes // 2
    for pair in range(pairs):
        first, second = x_ref[pair].astype(F32), x_ref[pairs + pair].astype(F32)
        upper = jnp.where(left, first, pltpu.roll(second, lanes // 2, 1))
        lower = jnp.where(left, pltpu.roll(first, lanes // 2, 1), second)
        att_ref[2 * dim * pair : 2 * dim * (pair + 1), :] = jnp.concatenate([upper, lower], 0).astype(BF)
    mixed = lax.dot_general(
        att_ref[...], w_out_ref[...], (((0,), (0,)), ((), ())), preferred_element_type=F32
    )
    mixed = mixed.astype(BF).astype(F32)
    centre = jnp.sum(mixed, axis=1, keepdims=True) / width
    centered = mixed - centre
    square = jnp.sum(centered * centered, axis=1, keepdims=True)
    here = pl.ds(pl.multiple_of(position * width, LANES), width)
    gain, bias = gain_ref[:, here], bias_ref[:, here]
    row = lax.broadcasted_iota(jnp.int32, (16, width), 0)
    extra = jnp.zeros((16, width), F32)
    for k, line in enumerate(pieces(gain, 2) + pieces(bias, 2)):
        extra = jnp.where(row == k, line, extra)
    left_side = jnp.concatenate([(centered * gain).astype(BF), extra.astype(BF)], 0)
    lane = lax.broadcasted_iota(jnp.int32, (lanes, LANES), 1)
    stats = jnp.zeros((lanes, LANES), F32)
    for k, column in enumerate(pieces(centre, 3) + pieces(square, 3)):
        stats = jnp.where(lane == k, column, stats)
    stats = stats.astype(BF)
    for copy in copies:
        copy.wait()
    planes, tokens, _ = out_ref.shape
    half = tokens // 2
    step = 2 * LANES
    shared = [None] * tokens
    for begin in range(0, out_width, step):
        part = jnp.dot(left_side, w_ref[:, begin : begin + step], preferred_element_type=F32)
        for plane in range(planes):
            out_ref[flipped(position, plane), :, begin : begin + step] = part[plane * tokens : (plane + 1) * tokens].astype(BF)
        scale = part[lanes : lanes + 1] + part[lanes + 1 : lanes + 2]
        shift = part[lanes + 2 : lanes + 3] + part[lanes + 3 : lanes + 4]
        for k in range(step // LANES):
            shared[begin // LANES + k] = scale[:, k * LANES : (k + 1) * LANES]
            shared[half + begin // LANES + k] = shift[:, k * LANES : (k + 1) * LANES]
    shared = jnp.concatenate(shared, 0).astype(BF)
    for plane in range(planes):
        out_ref[flipped(position, plane), :, out_width : out_width + LANES] = shared
        out_ref[flipped(position, plane), :, out_width + LANES :] = stats[plane * tokens : (plane + 1) * tokens]


def route_kernel(x0, x1, x2, x3, router_ref, ids_ref, out_ref, *, merge_width, experts):
    blocks = (x0, x1, x2, x3)
    planes, tokens = len(blocks), x0.shape[0]
    out_width = out_ref.shape[1] - LANES
    half = tokens // 2
    stats = [blocks[p][:, out_width + LANES :].astype(F32) for p in range(planes)]
    shared = [blocks[p][:, out_width : out_width + LANES].astype(F32) for p in range(planes)]
    centres = [s[:, 0:1] + s[:, 1:2] + s[:, 2:3] for s in stats]
    squares = [s[:, 3:4] + s[:, 4:5] + s[:, 5:6] for s in stats]
    mean = sum(centres) / planes
    offsets = [c - mean for c in centres]
    spread = sum(q + (merge_width // planes) * (o * o) for q, o in zip(squares, offsets)) / merge_width
    inverse = lax.rsqrt(spread + norm_eps)
    bias = sum(shared)
    for k in range(out_width // LANES):
        cut = slice(k * LANES, (k + 1) * LANES)
        total = sum(blocks[p][:, cut].astype(F32) for p in range(planes))
        total += sum(offsets[p] * shared[p][k : k + 1] for p in range(planes))
        out_ref[:, cut] = (total * inverse + bias[half + k : half + k + 1]).astype(BF)
    logits = jnp.dot(out_ref[:, :out_width], router_ref[...], preferred_element_type=F32)
    lane = lax.broadcasted_iota(jnp.int32, (tokens, LANES), 1)
    expert = lane % experts
    chosen = lane < 0
    for k in range(ids_ref.shape[1]):
        chosen = chosen | (ids_ref[:, k : k + 1] == expert)
    gates = jnp.where(chosen & (lane < 2 * experts), 1.0 / (1.0 + jnp.exp(-logits)), 0.0)
    total = jnp.sum(jnp.where(lane < experts, gates, 0.0), axis=1, keepdims=True)
    weight = route_scale * gates / total
    high, low = pieces(weight, 2)
    out_ref[:, out_width:] = jnp.where(lane < experts, high, low).astype(BF)


def expert_kernel(*refs, experts, cuts):
    *blocks, gate_hbm, up_hbm, down_hbm, own_ref, other_ref, x_ref, gate_ref, up_ref, down_ref, sems = refs
    tokens, width = own_ref.shape[1:]
    half = len(blocks) // 2
    copies = []
    for k, cut in enumerate(cuts):
        for kind, source, target in ((0, gate_hbm, gate_ref), (1, up_hbm, up_ref)):
            copies.append(pltpu.make_async_copy(source.at[0, cut, :], target.at[cut, :], sems.at[2 * k + kind]))
            copies[-1].start()
    last = pltpu.make_async_copy(down_hbm.at[0], down_ref, sems.at[2 * len(cuts)])
    last.start()
    expert = lax.axis_index("wide") // 2
    lane = lax.broadcasted_iota(jnp.int32, (tokens, LANES), 1)
    weights = []
    for k, block in enumerate(blocks):
        x_ref[k * tokens : (k + 1) * tokens, :] = block[:, :width]
        picked = (lane == expert) | (lane == expert + experts)
        picked = jnp.where(picked, block[:, width:].astype(F32), 0.0)
        weights.append(jnp.sum(picked, axis=1, keepdims=True))
    inputs = x_ref[...]
    turned = (((1,), (1,)), ((), ()))
    hidden = []
    for k, cut in enumerate(cuts):
        copies[2 * k].wait()
        gate = lax.dot_general(inputs, gate_ref[cut, :], turned, preferred_element_type=F32)
        copies[2 * k + 1].wait()
        up = lax.dot_general(inputs, up_ref[cut, :], turned, preferred_element_type=F32)
        hidden.append((gate / (1.0 + jnp.exp(-gate)) * up).astype(BF))
    hidden = jnp.concatenate(hidden, 1)
    last.wait()
    step = 4 * LANES
    for begin in range(0, width, step):
        product = jnp.dot(hidden, down_ref[:, begin : begin + step], preferred_element_type=F32)
        for k in range(len(blocks)):
            value = (product[k * tokens : (k + 1) * tokens] * weights[k]).astype(BF)
            out_ref = own_ref if k < half else other_ref
            out_ref[k % half, :, begin : begin + step] = value


def crossed(value, mask):
    pairs = [(source, source ^ mask) for source in range(lax.axis_size("wide"))]
    return lax.ppermute(value, "wide", pairs)


def local(
    qkv, grid, w_out, ln_gain, ln_bias, w_merge, w_router, expert_ids, slot_pos, w_gate, w_up, w_down
):
    devices = lax.axis_size("wide")
    rows = qkv.shape[0]
    vit_width = w_out.shape[0]
    experts = w_router.shape[1]
    out_width = w_merge.shape[1]
    tokens = rows // 4
    peers = devices // CLIPS
    suits = (
        devices == HEADS
        and peers == 8
        and rows == LANES
        and devices == 2 * experts
        and 2 * out_width == tokens * LANES
        and 4 * w_merge.shape[0] == vit_width
    )
    if not suits:
        return general(
            qkv, grid, w_out, ln_gain, ln_bias, w_merge, w_router, expert_ids, slot_pos, w_gate, w_up, w_down
        )
    part = vit_width // peers
    dim = vit_width // HEADS
    packed = pl.pallas_call(
        pack_kernel,
        out_shape=jax.ShapeDtypeStruct((peers, 3 * part, rows), BF),
        in_specs=[VMEM],
        out_specs=VMEM,
        compiler_params=params(8),
    )(qkv)
    clips = [[c * peers + i for i in range(peers)] for c in range(CLIPS)]
    gathered = lax.all_to_all(
        packed, "wide", split_axis=0, concat_axis=0, tiled=True, axis_index_groups=clips
    )
    gathered, held = lax.optimization_barrier((gathered, w_merge))
    held_y = crossed(held, 2)
    attended = pl.pallas_call(
        attend_kernel,
        out_shape=jax.ShapeDtypeStruct((devices, dim, rows), BF),
        in_specs=[VMEM, SMEM],
        out_specs=VMEM,
        compiler_params=params(20),
        cost_estimate=cost(2**32, 2**22, 2**21),
    )(gathered, grid)
    held_c = crossed(held, 1)
    returned = lax.all_to_all(attended, "wide", split_axis=0, concat_axis=0, tiled=True)
    returned, held_y = lax.optimization_barrier((returned, held_y))
    held_yc = crossed(held_y, 1)
    planes = devices // 4
    message = out_width + 2 * LANES
    partial = pl.pallas_call(
        merge_kernel,
        out_shape=jax.ShapeDtypeStruct((planes, tokens, message), BF),
        in_specs=[VMEM, VMEM, VMEM, VMEM, HBM, HBM, HBM, HBM],
        out_specs=VMEM,
        scratch_shapes=[
            pltpu.VMEM((vit_width, rows), BF),
            pltpu.VMEM((vit_width, out_width), BF),
            pltpu.SemaphoreType.DMA((4,)),
        ],
        compiler_params=params(20),
    )(
        returned,
        w_out,
        ln_gain.reshape(1, 4 * vit_width),
        ln_bias.reshape(1, 4 * vit_width),
        held,
        held_c,
        held_y,
        held_yc,
    )
    along = (8, 12, 4)
    arrived = [partial[0]] + [crossed(partial[mask // 4], mask) for mask in along]
    router = jnp.concatenate(
        [w_router, w_router, jnp.zeros((out_width, LANES - 2 * experts), BF)], 1
    )
    routed = pl.pallas_call(
        lambda *refs: route_kernel(*refs, merge_width=4 * vit_width, experts=experts),
        out_shape=jax.ShapeDtypeStruct((tokens, out_width + LANES), BF),
        in_specs=[VMEM] * 6,
        out_specs=VMEM,
        compiler_params=params(6),
    )(*arrived, router, expert_ids)
    near = [routed] + [crossed(routed, mask) for mask in along]
    far = [crossed(block, 2) for block in near]
    *near, far[0] = lax.optimization_barrier((*near, far[0]))
    gate_turned, up_turned = jnp.swapaxes(w_gate, 1, 2), jnp.swapaxes(w_up, 1, 2)

    inner = w_down.shape[1]
    cuts = [slice(k, min(k + 2 * LANES, inner)) for k in range(0, inner, 2 * LANES)]

    def experts_of(blocks):
        return pl.pallas_call(
            lambda *refs: expert_kernel(*refs, experts=experts, cuts=cuts),
            out_shape=[jax.ShapeDtypeStruct((planes, tokens, out_width), BF)] * 2,
            in_specs=[VMEM] * (2 * planes) + [HBM] * 3,
            out_specs=[VMEM, VMEM],
            scratch_shapes=[
                pltpu.VMEM((2 * planes * tokens, out_width), BF),
                pltpu.VMEM((inner, out_width), BF),
                pltpu.VMEM((inner, out_width), BF),
                pltpu.VMEM((inner, out_width), BF),
                pltpu.SemaphoreType.DMA((2 * len(cuts) + 1,)),
            ],
            compiler_params=params(50),
            cost_estimate=cost(2**32, 2**24),
        )(*blocks, *[crossed(block, 1) for block in blocks], gate_turned, up_turned, w_down)

    def scattered(blocks):
        others = [crossed(blocks[1 + along.index(mask)], mask) for mask in along]
        return blocks[0].astype(F32) + sum(block.astype(F32) for block in others)

    def paired(own, other):
        return (own.astype(F32) + crossed(other, 1).astype(F32)).astype(BF)

    near_own, near_other = experts_of(near)
    *far, near_own, near_other = lax.optimization_barrier((*far, near_own, near_other))
    far_own, far_other = experts_of(far)
    near_sum = scattered(paired(near_own, near_other))
    far_out, near_sum = lax.optimization_barrier((paired(far_own, far_other), near_sum))
    far_sum = scattered(far_out)
    return (near_sum + crossed(far_sum.astype(BF), 2).astype(F32)).astype(BF)


def solution(mesh):
    placed = (
        P(("grp", "wide"), None),
        P("grp", None),
        P(),
        P(),
        P(),
        P("wide", None),
        P(),
        P(("grp", "wide"), None),
        P(("grp", "wide"), None),
        P("wide", None, None),
        P("wide", None, None),
        P("wide", None, None),
    )
    return jax.shard_map(
        local, mesh=mesh, in_specs=placed, out_specs=P(("grp", "wide"), None), check_vma=False
    )
```

```python
import jax
import jax.numpy as jnp
from jax import lax
from jax.experimental import pallas as pl
from jax.experimental.pallas import tpu as pltpu
from jax.sharding import PartitionSpec as P

HEADS = 16
CLIPS = 2


route_scale = 2.446
norm_eps = 1e-05


def swapped(value, axis, stride):
    mask = 2**stride
    pairs = [(source, source ^ mask) for source in range(lax.axis_size(axis))]
    return lax.ppermute(value, axis, pairs)


def ordered_pair(own_part, partner, upper_bit):
    return jnp.where(
        upper_bit == 1,
        jnp.concatenate([partner, own_part], 0),
        jnp.concatenate([own_part, partner], 0),
    )


def general(
    qkv,
    grid,
    w_out,
    ln_gain,
    ln_bias,
    w_merge,
    w_router,
    expert_ids,
    slot_pos,
    w_gate,
    w_up,
    w_down,
):
    devices = lax.axis_size("wide")
    position_self = lax.axis_index("wide")
    vit_width = w_out.shape[0]
    head_dim = vit_width // HEADS
    groups = devices // HEADS
    local_rows = qkv.shape[0]
    sub_rows = local_rows // groups
    per_clip = devices // CLIPS
    query_send = (
        qkv[:, :vit_width]
        .reshape(groups, sub_rows, HEADS, head_dim)
        .transpose(2, 0, 1, 3)
        .reshape(devices, sub_rows, head_dim)
    )
    key_value = jnp.concatenate(
        [
            qkv[:, vit_width : 2 * vit_width].reshape(local_rows, HEADS, head_dim),
            qkv[:, 2 * vit_width :].reshape(local_rows, HEADS, head_dim),
        ],
        axis=2,
    )
    spread_send = jnp.broadcast_to(
        key_value.transpose(1, 0, 2)[:, None], (HEADS, groups, local_rows, 2 * head_dim)
    ).reshape(devices, local_rows, 2 * head_dim)
    queries, key_rows = (
        lax.all_to_all(query_send, "wide", split_axis=0, concat_axis=0, tiled=True),
        lax.all_to_all(spread_send, "wide", split_axis=0, concat_axis=0, tiled=True),
    )
    key_rows = key_rows[None]
    key_groups = key_rows.shape[0]
    key_count = key_rows.shape[2]
    key_place = (
        jnp.arange(per_clip, dtype=jnp.int32)[None, :, None] * local_rows
        + jnp.arange(key_groups, dtype=jnp.int32)[:, None, None] * local_rows
        + jnp.arange(key_count, dtype=jnp.int32)[None, None, :]
    ).reshape(-1)
    patch_counts = grid[:, 0] * grid[:, 1]
    clip_queries = queries.reshape(CLIPS, per_clip * sub_rows, head_dim)
    query_block_rows = min(512, per_clip * sub_rows)
    score_scale = head_dim ** (-0.5)

    def attend(clip_index):
        key_block = lax.dynamic_slice_in_dim(key_rows, clip_index * per_clip, per_clip, 1).reshape(
            -1, 2 * head_dim
        )
        visible = key_place < lax.dynamic_index_in_dim(patch_counts, clip_index, 0, keepdims=False)
        query_all = lax.dynamic_index_in_dim(clip_queries, clip_index, 0, keepdims=False)

        def one_block(query_block):
            scores = (
                lax.dot_general(
                    query_block,
                    key_block[:, :head_dim],
                    (((1,), (1,)), ((), ())),
                    preferred_element_type=jnp.float32,
                )
                * score_scale
            )
            scores = jnp.where(visible[None, :], scores, -jnp.inf)
            highest = jnp.max(scores, axis=1, keepdims=True)
            weights = jnp.exp(scores - highest)
            running = jnp.sum(weights, axis=1, keepdims=True)
            mixture = jnp.dot(
                weights.astype(jnp.bfloat16),
                key_block[:, head_dim:],
                preferred_element_type=jnp.float32,
            )
            return (mixture / running).astype(jnp.bfloat16)

        return lax.map(one_block, query_all.reshape(-1, query_block_rows, head_dim)).reshape(
            -1, head_dim
        )

    attended = lax.map(attend, jnp.arange(CLIPS, dtype=jnp.int32))
    returned = lax.all_to_all(
        attended.reshape(devices, sub_rows, head_dim),
        "wide",
        split_axis=0,
        concat_axis=0,
        tiled=True,
    )
    attention = (
        returned.reshape(HEADS, groups, sub_rows, head_dim)
        .transpose(1, 2, 0, 3)
        .reshape(local_rows, vit_width)
    )
    projected = jnp.dot(attention, w_out, preferred_element_type=jnp.float32).astype(jnp.bfloat16)
    merged = projected.reshape(local_rows // 4, 4 * vit_width).astype(jnp.float32)
    centre = jnp.mean(merged, axis=1, keepdims=True)
    centered = merged - centre
    spread = jnp.mean(centered * centered, axis=1, keepdims=True)
    normed = (centered * lax.rsqrt(spread + norm_eps) * ln_gain + ln_bias).astype(jnp.bfloat16)
    tok_groups = min(8, devices)
    feat_groups = devices // tok_groups
    merge_rows = w_merge
    for bit_index in range(tok_groups.bit_length() - 1):
        partner = swapped(merge_rows, "wide", bit_index)
        upper_bit = position_self // (1 << bit_index) % 2
        merge_rows = ordered_pair(merge_rows, partner, upper_bit)
    token_count = normed.shape[0]
    part_rows = token_count // tok_groups
    feat_width = normed.shape[1] // feat_groups
    out_width = w_merge.shape[1]
    merge_send = (
        normed.reshape(tok_groups, part_rows, feat_groups, feat_width)
        .transpose(2, 0, 1, 3)
        .reshape(devices, part_rows, feat_width)
    )
    flat_rows = lax.all_to_all(merge_send, "wide", split_axis=0, concat_axis=0, tiled=True).reshape(
        -1, feat_width
    )
    partial_value = jnp.dot(flat_rows, merge_rows, preferred_element_type=jnp.float32).reshape(
        devices, -1, out_width
    )
    summed = lax.all_to_all(partial_value, "wide", split_axis=0, concat_axis=0, tiled=True)
    tokens = (
        jnp.sum(summed.reshape(feat_groups, tok_groups, part_rows, out_width), axis=0)
        .reshape(token_count, out_width)
        .astype(jnp.bfloat16)
    )
    logits = jnp.dot(tokens, w_router, preferred_element_type=jnp.float32)
    experts = w_router.shape[1]
    top_count = expert_ids.shape[1]
    matches = expert_ids[:, :, None] == jnp.arange(experts, dtype=jnp.int32)[None, None, :]
    chosen = jnp.sum(jnp.where(matches, logits[:, None, :], 0.0), axis=2)
    gate_values = jax.nn.sigmoid(chosen)
    route_weight = route_scale * gate_values / jnp.sum(gate_values, axis=1, keepdims=True)
    capacity = min(token_count, 2 * token_count * top_count // experts)
    slot_count = experts * capacity
    target = expert_ids * capacity + slot_pos
    one_hot = jnp.any(
        target[None, :, :] == jnp.arange(slot_count, dtype=jnp.int32)[:, None, None], axis=2
    ).astype(jnp.bfloat16)
    buffer = jnp.dot(one_hot, tokens, preferred_element_type=jnp.float32).astype(jnp.bfloat16)
    gate_half = w_gate[0]
    up_half = w_up[0]
    down_half = w_down[0]
    half_cap = capacity // 2
    dispatch = buffer.reshape(devices, half_cap, out_width)
    portion = lax.all_to_all(dispatch, "wide", split_axis=0, concat_axis=0, tiled=True)
    item_count = portion.shape[1]
    partner_rows = swapped(portion, "wide", 0)
    both_rows = jnp.concatenate([portion, partner_rows], axis=1)
    flat_rows = both_rows.reshape(-1, out_width)
    gate_part = jnp.dot(flat_rows, gate_half, preferred_element_type=jnp.float32)
    up_part = jnp.dot(flat_rows, up_half, preferred_element_type=jnp.float32)
    hidden = (jax.nn.silu(gate_part) * up_part).astype(jnp.bfloat16)
    product = (
        jnp.dot(hidden, down_half, preferred_element_type=jnp.float32)
        .astype(jnp.bfloat16)
        .reshape(devices, 2 * item_count, out_width)
    )
    from_partner = swapped(product[:, item_count:], "wide", 0)
    joined = (
        product[:, :item_count].astype(jnp.float32) + from_partner.astype(jnp.float32)
    ).astype(jnp.bfloat16)
    answers = lax.all_to_all(joined, "wide", split_axis=0, concat_axis=0, tiled=True)
    slot_result = answers.reshape(slot_count, out_width)
    slot_result = lax.optimization_barrier(slot_result)
    picked = jnp.take(slot_result, target.reshape(-1), axis=0).reshape(
        token_count, top_count, out_width
    )
    return jnp.sum(picked.astype(jnp.float32) * route_weight[:, :, None], axis=1).astype(
        jnp.bfloat16
    )


BF = jnp.bfloat16
F32 = jnp.float32
VMEM = pl.BlockSpec(memory_space=pltpu.VMEM)
SMEM = pl.BlockSpec(memory_space=pltpu.SMEM)
HBM = pl.BlockSpec(memory_space=pltpu.HBM)
LANES = 128
MASKED = -1e30
LOG2E = 1.4426950408889634


def params(mib):
    return pltpu.CompilerParams(vmem_limit_bytes=mib * 2**20)


def cost(flops, size, exps=0):
    return pl.CostEstimate(flops=flops, bytes_accessed=size, transcendentals=exps)


def flipped(number, bits):
    low = (number % 2 + bits % 2) % 2
    return 2 * ((number // 2 + bits // 2) % 2) + low


def pieces(value, count):
    out = []
    for _ in range(count):
        piece = value.astype(BF).astype(F32)
        out.append(piece)
        value = value - piece
    return out


def pack_kernel(qkv_ref, out_ref):
    rows, width = qkv_ref.shape
    tokens = rows // 4
    peers, parts, _ = out_ref.shape
    source = lax.broadcasted_iota(jnp.int32, (rows, rows), 0)
    place = lax.broadcasted_iota(jnp.int32, (rows, rows), 1)
    order = jnp.where(source == 4 * (place % tokens) + place // tokens, 1.0, 0.0).astype(BF)
    part = parts // 3
    third = width // 3
    for kind in range(3):
        turned = lax.dot_general(
            qkv_ref[:, kind * third : (kind + 1) * third],
            order,
            (((0,), (0,)), ((), ())),
            preferred_element_type=F32,
        ).astype(BF)
        for peer in range(peers):
            out_ref[peer, kind * part : (kind + 1) * part, :] = turned[peer * part : (peer + 1) * part]


def attend_kernel(x_ref, grid_ref, out_ref):
    peers, parts, lanes = x_ref.shape
    part = parts // 3
    dim = part // 2
    quarters = 4
    sides = peers // quarters
    tokens = lanes // 4
    clip = lax.axis_index("wide") // peers
    count = grid_ref[clip, 0] * grid_ref[clip, 1]
    factor = dim ** (-0.5) * LOG2E
    keys = jnp.concatenate([x_ref[s, part : 2 * part, :] for s in range(peers)], 1)
    lane = lax.broadcasted_iota(jnp.int32, (16, peers * lanes), 1)
    row = lax.broadcasted_iota(jnp.int32, (16, peers * lanes), 0)
    inner = lane % lanes
    place = lane // lanes * lanes + 4 * (inner % tokens) + inner // tokens
    hidden = jnp.where((row == 0) & (place >= count), MASKED, 0.0).astype(BF)
    keys = jnp.concatenate([keys, hidden], 0).T
    values = jnp.concatenate([x_ref[s, 2 * part :, :] for s in range(peers)], 1).astype(F32)
    values = [values[:dim].astype(BF), values[dim:].astype(BF)]
    ones = jnp.where(lax.broadcasted_iota(jnp.int32, (16, sides * lanes), 0) == 0, 1.0, 0.0).astype(BF)
    head_row = lax.broadcasted_iota(jnp.int32, (part, sides * lanes), 0) // dim
    group = lax.broadcasted_iota(jnp.int32, (dim, lanes), 1) // tokens
    for quarter in range(quarters):
        query = jnp.concatenate(
            [x_ref[quarter + quarters * s, :part, :] for s in range(sides)], 1
        ).astype(F32)
        mixed = []
        for head in range(2):
            own = jnp.concatenate([jnp.where(head_row == head, query, 0.0).astype(BF), ones], 0)
            scores = jnp.dot(keys, own, preferred_element_type=F32)
            highest = jnp.max(scores, axis=0, keepdims=True)
            weights = jnp.exp2(scores * factor - highest * factor)
            total = jnp.sum(weights, axis=0, keepdims=True)
            value = jnp.dot(values[head], weights.astype(BF), preferred_element_type=F32) / total
            mixed += [value[:, s * lanes : (s + 1) * lanes] for s in range(sides)]
        for position in range(4):
            block = mixed[position]
            for g in range(4):
                if g != position:
                    shift = (g - position) * tokens % lanes
                    block = jnp.where(group == g, pltpu.roll(mixed[g], shift, 1), block)
            out_ref[quarters * position + quarter] = block.astype(BF)


def merge_kernel(
    x_ref, w_out_ref, gain_ref, bias_ref, w0, w1, w2, w3, out_ref, att_ref, w_ref, sems
):
    me = lax.axis_index("wide")
    position, quarter = me // 4, me % 4
    blocks, dim, lanes = x_ref.shape
    pairs = blocks // 2
    depth = w0.shape[0]
    out_width = w0.shape[1]
    width = w_out_ref.shape[1]
    copies = []
    for k, source in enumerate((w0, w1, w2, w3)):
        spot = pl.multiple_of(flipped(quarter, k) * depth, depth)
        copies.append(pltpu.make_async_copy(source, w_ref.at[pl.ds(spot, depth), :], sems.at[k]))
        copies[-1].start()
    left = lax.broadcasted_iota(jnp.int32, (dim, lanes), 1) < lanes // 2
    for pair in range(pairs):
        first, second = x_ref[pair].astype(F32), x_ref[pairs + pair].astype(F32)
        upper = jnp.where(left, first, pltpu.roll(second, lanes // 2, 1))
        lower = jnp.where(left, pltpu.roll(first, lanes // 2, 1), second)
        att_ref[2 * dim * pair : 2 * dim * (pair + 1), :] = jnp.concatenate([upper, lower], 0).astype(BF)
    mixed = lax.dot_general(
        att_ref[...], w_out_ref[...], (((0,), (0,)), ((), ())), preferred_element_type=F32
    )
    mixed = mixed.astype(BF).astype(F32)
    centre = jnp.sum(mixed, axis=1, keepdims=True) / width
    centered = mixed - centre
    square = jnp.sum(centered * centered, axis=1, keepdims=True)
    here = pl.ds(pl.multiple_of(position * width, LANES), width)
    gain, bias = gain_ref[:, here], bias_ref[:, here]
    row = lax.broadcasted_iota(jnp.int32, (16, width), 0)
    extra = jnp.zeros((16, width), F32)
    for k, line in enumerate(pieces(gain, 2) + pieces(bias, 2)):
        extra = jnp.where(row == k, line, extra)
    left_side = jnp.concatenate([(centered * gain).astype(BF), extra.astype(BF)], 0)
    lane = lax.broadcasted_iota(jnp.int32, (lanes, LANES), 1)
    stats = jnp.zeros((lanes, LANES), F32)
    for k, column in enumerate(pieces(centre, 3) + pieces(square, 3)):
        stats = jnp.where(lane == k, column, stats)
    stats = stats.astype(BF)
    for copy in copies:
        copy.wait()
    planes, tokens, _ = out_ref.shape
    half = tokens // 2
    step = 2 * LANES
    shared = [None] * tokens
    for begin in range(0, out_width, step):
        part = jnp.dot(left_side, w_ref[:, begin : begin + step], preferred_element_type=F32)
        for plane in range(planes):
            out_ref[flipped(position, plane), :, begin : begin + step] = part[plane * tokens : (plane + 1) * tokens].astype(BF)
        scale = part[lanes : lanes + 1] + part[lanes + 1 : lanes + 2]
        shift = part[lanes + 2 : lanes + 3] + part[lanes + 3 : lanes + 4]
        for k in range(step // LANES):
            shared[begin // LANES + k] = scale[:, k * LANES : (k + 1) * LANES]
            shared[half + begin // LANES + k] = shift[:, k * LANES : (k + 1) * LANES]
    shared = jnp.concatenate(shared, 0).astype(BF)
    for plane in range(planes):
        out_ref[flipped(position, plane), :, out_width : out_width + LANES] = shared
        out_ref[flipped(position, plane), :, out_width + LANES :] = stats[plane * tokens : (plane + 1) * tokens]


def route_kernel(x0, x1, x2, x3, router_ref, ids_ref, out_ref, *, merge_width, experts):
    blocks = (x0, x1, x2, x3)
    planes, tokens = len(blocks), x0.shape[0]
    out_width = out_ref.shape[1] - LANES
    half = tokens // 2
    stats = [blocks[p][:, out_width + LANES :].astype(F32) for p in range(planes)]
    shared = [blocks[p][:, out_width : out_width + LANES].astype(F32) for p in range(planes)]
    centres = [s[:, 0:1] + s[:, 1:2] + s[:, 2:3] for s in stats]
    squares = [s[:, 3:4] + s[:, 4:5] + s[:, 5:6] for s in stats]
    mean = sum(centres) / planes
    offsets = [c - mean for c in centres]
    spread = sum(q + (merge_width // planes) * (o * o) for q, o in zip(squares, offsets)) / merge_width
    inverse = lax.rsqrt(spread + norm_eps)
    bias = sum(shared)
    for k in range(out_width // LANES):
        cut = slice(k * LANES, (k + 1) * LANES)
        total = sum(blocks[p][:, cut].astype(F32) for p in range(planes))
        total += sum(offsets[p] * shared[p][k : k + 1] for p in range(planes))
        out_ref[:, cut] = (total * inverse + bias[half + k : half + k + 1]).astype(BF)
    logits = jnp.dot(out_ref[:, :out_width], router_ref[...], preferred_element_type=F32)
    lane = lax.broadcasted_iota(jnp.int32, (tokens, LANES), 1)
    expert = lane % experts
    chosen = lane < 0
    for k in range(ids_ref.shape[1]):
        chosen = chosen | (ids_ref[:, k : k + 1] == expert)
    gates = jnp.where(chosen & (lane < 2 * experts), 1.0 / (1.0 + jnp.exp(-logits)), 0.0)
    total = jnp.sum(jnp.where(lane < experts, gates, 0.0), axis=1, keepdims=True)
    weight = route_scale * gates / total
    high, low = pieces(weight, 2)
    out_ref[:, out_width:] = jnp.where(lane < experts, high, low).astype(BF)


def expert_kernel(*refs, experts, cuts):
    *blocks, gate_hbm, up_hbm, down_hbm, own_ref, other_ref, x_ref, gate_ref, up_ref, down_ref, sems = refs
    tokens, width = own_ref.shape[1:]
    half = len(blocks) // 2
    copies = []
    for k, cut in enumerate(cuts):
        for kind, source, target in ((0, gate_hbm, gate_ref), (1, up_hbm, up_ref)):
            copies.append(pltpu.make_async_copy(source.at[0, cut, :], target.at[cut, :], sems.at[2 * k + kind]))
            copies[-1].start()
    last = pltpu.make_async_copy(down_hbm.at[0], down_ref, sems.at[2 * len(cuts)])
    last.start()
    expert = lax.axis_index("wide") // 2
    lane = lax.broadcasted_iota(jnp.int32, (tokens, LANES), 1)
    weights = []
    for k, block in enumerate(blocks):
        x_ref[k * tokens : (k + 1) * tokens, :] = block[:, :width]
        picked = (lane == expert) | (lane == expert + experts)
        picked = jnp.where(picked, block[:, width:].astype(F32), 0.0)
        weights.append(jnp.sum(picked, axis=1, keepdims=True))
    inputs = x_ref[...]
    turned = (((1,), (1,)), ((), ()))
    hidden = []
    for k, cut in enumerate(cuts):
        copies[2 * k].wait()
        gate = lax.dot_general(inputs, gate_ref[cut, :], turned, preferred_element_type=F32)
        copies[2 * k + 1].wait()
        up = lax.dot_general(inputs, up_ref[cut, :], turned, preferred_element_type=F32)
        hidden.append((gate / (1.0 + jnp.exp(-gate)) * up).astype(BF))
    hidden = jnp.concatenate(hidden, 1)
    last.wait()
    step = 4 * LANES
    for begin in range(0, width, step):
        product = jnp.dot(hidden, down_ref[:, begin : begin + step], preferred_element_type=F32)
        for k in range(len(blocks)):
            value = (product[k * tokens : (k + 1) * tokens] * weights[k]).astype(BF)
            out_ref = own_ref if k < half else other_ref
            out_ref[k % half, :, begin : begin + step] = value


def crossed(value, mask):
    pairs = [(source, source ^ mask) for source in range(lax.axis_size("wide"))]
    return lax.ppermute(value, "wide", pairs)


def local(
    qkv, grid, w_out, ln_gain, ln_bias, w_merge, w_router, expert_ids, slot_pos, w_gate, w_up, w_down
):
    devices = lax.axis_size("wide")
    rows = qkv.shape[0]
    vit_width = w_out.shape[0]
    experts = w_router.shape[1]
    out_width = w_merge.shape[1]
    tokens = rows // 4
    peers = devices // CLIPS
    suits = (
        devices == HEADS
        and peers == 8
        and rows == LANES
        and devices == 2 * experts
        and 2 * out_width == tokens * LANES
        and 4 * w_merge.shape[0] == vit_width
    )
    if not suits:
        return general(
            qkv, grid, w_out, ln_gain, ln_bias, w_merge, w_router, expert_ids, slot_pos, w_gate, w_up, w_down
        )
    part = vit_width // peers
    dim = vit_width // HEADS
    packed = pl.pallas_call(
        pack_kernel,
        out_shape=jax.ShapeDtypeStruct((peers, 3 * part, rows), BF),
        in_specs=[VMEM],
        out_specs=VMEM,
        compiler_params=params(8),
    )(qkv)
    clips = [[c * peers + i for i in range(peers)] for c in range(CLIPS)]
    gathered = lax.all_to_all(
        packed, "wide", split_axis=0, concat_axis=0, tiled=True, axis_index_groups=clips
    )
    gathered, held = lax.optimization_barrier((gathered, w_merge))
    held_y = crossed(held, 2)
    attended = pl.pallas_call(
        attend_kernel,
        out_shape=jax.ShapeDtypeStruct((devices, dim, rows), BF),
        in_specs=[VMEM, SMEM],
        out_specs=VMEM,
        compiler_params=params(20),
        cost_estimate=cost(2**32, 2**22, 2**21),
    )(gathered, grid)
    held_c = crossed(held, 1)
    returned = lax.all_to_all(attended, "wide", split_axis=0, concat_axis=0, tiled=True)
    returned, held_y = lax.optimization_barrier((returned, held_y))
    held_yc = crossed(held_y, 1)
    planes = devices // 4
    message = out_width + 2 * LANES
    partial = pl.pallas_call(
        merge_kernel,
        out_shape=jax.ShapeDtypeStruct((planes, tokens, message), BF),
        in_specs=[VMEM, VMEM, VMEM, VMEM, HBM, HBM, HBM, HBM],
        out_specs=VMEM,
        scratch_shapes=[
            pltpu.VMEM((vit_width, rows), BF),
            pltpu.VMEM((vit_width, out_width), BF),
            pltpu.SemaphoreType.DMA((4,)),
        ],
        compiler_params=params(20),
    )(
        returned,
        w_out,
        ln_gain.reshape(1, 4 * vit_width),
        ln_bias.reshape(1, 4 * vit_width),
        held,
        held_c,
        held_y,
        held_yc,
    )
    along = (8, 12, 4)
    arrived = [partial[0]] + [crossed(partial[mask // 4], mask) for mask in along]
    router = jnp.concatenate(
        [w_router, w_router, jnp.zeros((out_width, LANES - 2 * experts), BF)], 1
    )
    routed = pl.pallas_call(
        lambda *refs: route_kernel(*refs, merge_width=4 * vit_width, experts=experts),
        out_shape=jax.ShapeDtypeStruct((tokens, out_width + LANES), BF),
        in_specs=[VMEM] * 6,
        out_specs=VMEM,
        compiler_params=params(6),
    )(*arrived, router, expert_ids)
    near = [routed] + [crossed(routed, mask) for mask in along]
    far = [crossed(block, 2) for block in near]
    *near, far[0] = lax.optimization_barrier((*near, far[0]))
    gate_turned, up_turned = jnp.swapaxes(w_gate, 1, 2), jnp.swapaxes(w_up, 1, 2)

    inner = w_down.shape[1]
    cuts = [slice(k, min(k + 2 * LANES, inner)) for k in range(0, inner, 2 * LANES)]

    def experts_of(blocks):
        return pl.pallas_call(
            lambda *refs: expert_kernel(*refs, experts=experts, cuts=cuts),
            out_shape=[jax.ShapeDtypeStruct((planes, tokens, out_width), BF)] * 2,
            in_specs=[VMEM] * (2 * planes) + [HBM] * 3,
            out_specs=[VMEM, VMEM],
            scratch_shapes=[
                pltpu.VMEM((2 * planes * tokens, out_width), BF),
                pltpu.VMEM((inner, out_width), BF),
                pltpu.VMEM((inner, out_width), BF),
                pltpu.VMEM((inner, out_width), BF),
                pltpu.SemaphoreType.DMA((2 * len(cuts) + 1,)),
            ],
            compiler_params=params(50),
            cost_estimate=cost(2**32, 2**24),
        )(*blocks, *[crossed(block, 1) for block in blocks], gate_turned, up_turned, w_down)

    def scattered(blocks):
        others = [crossed(blocks[1 + along.index(mask)], mask) for mask in along]
        return blocks[0].astype(F32) + sum(block.astype(F32) for block in others)

    def paired(own, other):
        return (own.astype(F32) + crossed(other, 1).astype(F32)).astype(BF)

    near_own, near_other = experts_of(near)
    *far, near_own, near_other = lax.optimization_barrier((*far, near_own, near_other))
    far_own, far_other = experts_of(far)
    near_sum = scattered(paired(near_own, near_other))
    far_out, near_sum = lax.optimization_barrier((paired(far_own, far_other), near_sum))
    across = [crossed(far_out[k], 2 + mask) for k, mask in enumerate(along, 1)]
    across.append(crossed(far_out[0], 2))
    return (near_sum + sum(block.astype(F32) for block in across)).astype(BF)


def solution(mesh):
    placed = (
        P(("grp", "wide"), None),
        P("grp", None),
        P(),
        P(),
        P(),
        P("wide", None),
        P(),
        P(("grp", "wide"), None),
        P(("grp", "wide"), None),
        P("wide", None, None),
        P("wide", None, None),
        P("wide", None, None),
    )
    return jax.shard_map(
        local, mesh=mesh, in_specs=placed, out_specs=P(("grp", "wide"), None), check_vma=False
    )
```

```python
import jax
import jax.numpy as jnp
from jax import lax
from jax.experimental import pallas as pl
from jax.experimental.pallas import tpu as pltpu
from jax.sharding import PartitionSpec as P

HEADS = 16
CLIPS = 2


route_scale = 2.446
norm_eps = 1e-05


def swapped(value, axis, stride):
    mask = 2**stride
    pairs = [(source, source ^ mask) for source in range(lax.axis_size(axis))]
    return lax.ppermute(value, axis, pairs)


def ordered_pair(own_part, partner, upper_bit):
    return jnp.where(
        upper_bit == 1,
        jnp.concatenate([partner, own_part], 0),
        jnp.concatenate([own_part, partner], 0),
    )


def general(
    qkv,
    grid,
    w_out,
    ln_gain,
    ln_bias,
    w_merge,
    w_router,
    expert_ids,
    slot_pos,
    w_gate,
    w_up,
    w_down,
):
    devices = lax.axis_size("wide")
    position_self = lax.axis_index("wide")
    vit_width = w_out.shape[0]
    head_dim = vit_width // HEADS
    groups = devices // HEADS
    local_rows = qkv.shape[0]
    sub_rows = local_rows // groups
    per_clip = devices // CLIPS
    query_send = (
        qkv[:, :vit_width]
        .reshape(groups, sub_rows, HEADS, head_dim)
        .transpose(2, 0, 1, 3)
        .reshape(devices, sub_rows, head_dim)
    )
    key_value = jnp.concatenate(
        [
            qkv[:, vit_width : 2 * vit_width].reshape(local_rows, HEADS, head_dim),
            qkv[:, 2 * vit_width :].reshape(local_rows, HEADS, head_dim),
        ],
        axis=2,
    )
    spread_send = jnp.broadcast_to(
        key_value.transpose(1, 0, 2)[:, None], (HEADS, groups, local_rows, 2 * head_dim)
    ).reshape(devices, local_rows, 2 * head_dim)
    queries, key_rows = (
        lax.all_to_all(query_send, "wide", split_axis=0, concat_axis=0, tiled=True),
        lax.all_to_all(spread_send, "wide", split_axis=0, concat_axis=0, tiled=True),
    )
    key_rows = key_rows[None]
    key_groups = key_rows.shape[0]
    key_count = key_rows.shape[2]
    key_place = (
        jnp.arange(per_clip, dtype=jnp.int32)[None, :, None] * local_rows
        + jnp.arange(key_groups, dtype=jnp.int32)[:, None, None] * local_rows
        + jnp.arange(key_count, dtype=jnp.int32)[None, None, :]
    ).reshape(-1)
    patch_counts = grid[:, 0] * grid[:, 1]
    clip_queries = queries.reshape(CLIPS, per_clip * sub_rows, head_dim)
    query_block_rows = min(512, per_clip * sub_rows)
    score_scale = head_dim ** (-0.5)

    def attend(clip_index):
        key_block = lax.dynamic_slice_in_dim(key_rows, clip_index * per_clip, per_clip, 1).reshape(
            -1, 2 * head_dim
        )
        visible = key_place < lax.dynamic_index_in_dim(patch_counts, clip_index, 0, keepdims=False)
        query_all = lax.dynamic_index_in_dim(clip_queries, clip_index, 0, keepdims=False)

        def one_block(query_block):
            scores = (
                lax.dot_general(
                    query_block,
                    key_block[:, :head_dim],
                    (((1,), (1,)), ((), ())),
                    preferred_element_type=jnp.float32,
                )
                * score_scale
            )
            scores = jnp.where(visible[None, :], scores, -jnp.inf)
            highest = jnp.max(scores, axis=1, keepdims=True)
            weights = jnp.exp(scores - highest)
            running = jnp.sum(weights, axis=1, keepdims=True)
            mixture = jnp.dot(
                weights.astype(jnp.bfloat16),
                key_block[:, head_dim:],
                preferred_element_type=jnp.float32,
            )
            return (mixture / running).astype(jnp.bfloat16)

        return lax.map(one_block, query_all.reshape(-1, query_block_rows, head_dim)).reshape(
            -1, head_dim
        )

    attended = lax.map(attend, jnp.arange(CLIPS, dtype=jnp.int32))
    returned = lax.all_to_all(
        attended.reshape(devices, sub_rows, head_dim),
        "wide",
        split_axis=0,
        concat_axis=0,
        tiled=True,
    )
    attention = (
        returned.reshape(HEADS, groups, sub_rows, head_dim)
        .transpose(1, 2, 0, 3)
        .reshape(local_rows, vit_width)
    )
    projected = jnp.dot(attention, w_out, preferred_element_type=jnp.float32).astype(jnp.bfloat16)
    merged = projected.reshape(local_rows // 4, 4 * vit_width).astype(jnp.float32)
    centre = jnp.mean(merged, axis=1, keepdims=True)
    centered = merged - centre
    spread = jnp.mean(centered * centered, axis=1, keepdims=True)
    normed = (centered * lax.rsqrt(spread + norm_eps) * ln_gain + ln_bias).astype(jnp.bfloat16)
    tok_groups = min(8, devices)
    feat_groups = devices // tok_groups
    merge_rows = w_merge
    for bit_index in range(tok_groups.bit_length() - 1):
        partner = swapped(merge_rows, "wide", bit_index)
        upper_bit = position_self // (1 << bit_index) % 2
        merge_rows = ordered_pair(merge_rows, partner, upper_bit)
    token_count = normed.shape[0]
    part_rows = token_count // tok_groups
    feat_width = normed.shape[1] // feat_groups
    out_width = w_merge.shape[1]
    merge_send = (
        normed.reshape(tok_groups, part_rows, feat_groups, feat_width)
        .transpose(2, 0, 1, 3)
        .reshape(devices, part_rows, feat_width)
    )
    flat_rows = lax.all_to_all(merge_send, "wide", split_axis=0, concat_axis=0, tiled=True).reshape(
        -1, feat_width
    )
    partial_value = jnp.dot(flat_rows, merge_rows, preferred_element_type=jnp.float32).reshape(
        devices, -1, out_width
    )
    summed = lax.all_to_all(partial_value, "wide", split_axis=0, concat_axis=0, tiled=True)
    tokens = (
        jnp.sum(summed.reshape(feat_groups, tok_groups, part_rows, out_width), axis=0)
        .reshape(token_count, out_width)
        .astype(jnp.bfloat16)
    )
    logits = jnp.dot(tokens, w_router, preferred_element_type=jnp.float32)
    experts = w_router.shape[1]
    top_count = expert_ids.shape[1]
    matches = expert_ids[:, :, None] == jnp.arange(experts, dtype=jnp.int32)[None, None, :]
    chosen = jnp.sum(jnp.where(matches, logits[:, None, :], 0.0), axis=2)
    gate_values = jax.nn.sigmoid(chosen)
    route_weight = route_scale * gate_values / jnp.sum(gate_values, axis=1, keepdims=True)
    capacity = min(token_count, 2 * token_count * top_count // experts)
    slot_count = experts * capacity
    target = expert_ids * capacity + slot_pos
    one_hot = jnp.any(
        target[None, :, :] == jnp.arange(slot_count, dtype=jnp.int32)[:, None, None], axis=2
    ).astype(jnp.bfloat16)
    buffer = jnp.dot(one_hot, tokens, preferred_element_type=jnp.float32).astype(jnp.bfloat16)
    gate_half = w_gate[0]
    up_half = w_up[0]
    down_half = w_down[0]
    half_cap = capacity // 2
    dispatch = buffer.reshape(devices, half_cap, out_width)
    portion = lax.all_to_all(dispatch, "wide", split_axis=0, concat_axis=0, tiled=True)
    item_count = portion.shape[1]
    partner_rows = swapped(portion, "wide", 0)
    both_rows = jnp.concatenate([portion, partner_rows], axis=1)
    flat_rows = both_rows.reshape(-1, out_width)
    gate_part = jnp.dot(flat_rows, gate_half, preferred_element_type=jnp.float32)
    up_part = jnp.dot(flat_rows, up_half, preferred_element_type=jnp.float32)
    hidden = (jax.nn.silu(gate_part) * up_part).astype(jnp.bfloat16)
    product = (
        jnp.dot(hidden, down_half, preferred_element_type=jnp.float32)
        .astype(jnp.bfloat16)
        .reshape(devices, 2 * item_count, out_width)
    )
    from_partner = swapped(product[:, item_count:], "wide", 0)
    joined = (
        product[:, :item_count].astype(jnp.float32) + from_partner.astype(jnp.float32)
    ).astype(jnp.bfloat16)
    answers = lax.all_to_all(joined, "wide", split_axis=0, concat_axis=0, tiled=True)
    slot_result = answers.reshape(slot_count, out_width)
    slot_result = lax.optimization_barrier(slot_result)
    picked = jnp.take(slot_result, target.reshape(-1), axis=0).reshape(
        token_count, top_count, out_width
    )
    return jnp.sum(picked.astype(jnp.float32) * route_weight[:, :, None], axis=1).astype(
        jnp.bfloat16
    )


BF = jnp.bfloat16
F32 = jnp.float32
VMEM = pl.BlockSpec(memory_space=pltpu.VMEM)
SMEM = pl.BlockSpec(memory_space=pltpu.SMEM)
HBM = pl.BlockSpec(memory_space=pltpu.HBM)
LANES = 128
MASKED = -1e30
LOG2E = 1.4426950408889634


def params(mib):
    return pltpu.CompilerParams(vmem_limit_bytes=mib * 2**20)


def cost(flops, size, exps=0):
    return pl.CostEstimate(flops=flops, bytes_accessed=size, transcendentals=exps)


def flipped(number, bits):
    low = (number % 2 + bits % 2) % 2
    return 2 * ((number // 2 + bits // 2) % 2) + low


def pieces(value, count):
    out = []
    for _ in range(count):
        piece = value.astype(BF).astype(F32)
        out.append(piece)
        value = value - piece
    return out


def pack_kernel(qkv_ref, merge_ref, out_ref, common_ref, share_ref, sems):
    common, share = common_ref.shape[0], share_ref.shape[0]
    spot = pl.multiple_of(common + share * lax.axis_index("grp"), 16)
    copies = [
        pltpu.make_async_copy(merge_ref.at[pl.ds(spot, share), :], share_ref, sems.at[0]),
        pltpu.make_async_copy(merge_ref.at[pl.ds(0, common), :], common_ref, sems.at[1]),
    ]
    for copy in copies:
        copy.start()
    rows, width = qkv_ref.shape
    tokens = rows // 4
    peers, parts, _ = out_ref.shape
    source = lax.broadcasted_iota(jnp.int32, (rows, rows), 0)
    place = lax.broadcasted_iota(jnp.int32, (rows, rows), 1)
    order = jnp.where(source == 4 * (place % tokens) + place // tokens, 1.0, 0.0).astype(BF)
    part = parts // 3
    third = width // 3
    for kind in range(3):
        turned = lax.dot_general(
            qkv_ref[:, kind * third : (kind + 1) * third],
            order,
            (((0,), (0,)), ((), ())),
            preferred_element_type=F32,
        ).astype(BF)
        for peer in range(peers):
            out_ref[peer, kind * part : (kind + 1) * part, :] = turned[peer * part : (peer + 1) * part]
    for copy in copies:
        copy.wait()


def attend_kernel(x_ref, grid_ref, out_ref):
    peers, parts, lanes = x_ref.shape
    part = parts // 3
    dim = part // 2
    quarters = 4
    sides = peers // quarters
    tokens = lanes // 4
    clip = lax.axis_index("wide") // peers
    count = grid_ref[clip, 0] * grid_ref[clip, 1]
    factor = dim ** (-0.5) * LOG2E
    keys = jnp.concatenate([x_ref[s, part : 2 * part, :] for s in range(peers)], 1)
    lane = lax.broadcasted_iota(jnp.int32, (16, peers * lanes), 1)
    row = lax.broadcasted_iota(jnp.int32, (16, peers * lanes), 0)
    inner = lane % lanes
    place = lane // lanes * lanes + 4 * (inner % tokens) + inner // tokens
    hidden = jnp.where((row == 0) & (place >= count), MASKED, 0.0).astype(BF)
    keys = jnp.concatenate([keys, hidden], 0).T
    values = jnp.concatenate([x_ref[s, 2 * part :, :] for s in range(peers)], 1).astype(F32)
    values = [values[:dim].astype(BF), values[dim:].astype(BF)]
    ones = jnp.where(lax.broadcasted_iota(jnp.int32, (16, sides * lanes), 0) == 0, 1.0, 0.0).astype(BF)
    head_row = lax.broadcasted_iota(jnp.int32, (part, sides * lanes), 0) // dim
    group = lax.broadcasted_iota(jnp.int32, (dim, lanes), 1) // tokens
    for quarter in range(quarters):
        query = jnp.concatenate(
            [x_ref[quarter + quarters * s, :part, :] for s in range(sides)], 1
        ).astype(F32)
        mixed = []
        for head in range(2):
            own = jnp.concatenate([jnp.where(head_row == head, query, 0.0).astype(BF), ones], 0)
            scores = jnp.dot(keys, own, preferred_element_type=F32)
            highest = jnp.max(scores, axis=0, keepdims=True)
            weights = jnp.exp2((scores - highest) * factor)
            total = jnp.sum(weights, axis=0, keepdims=True)
            value = jnp.dot(values[head], weights.astype(BF), preferred_element_type=F32) / total
            mixed += [value[:, s * lanes : (s + 1) * lanes] for s in range(sides)]
        for position in range(4):
            block = mixed[position]
            for g in range(4):
                if g != position:
                    shift = (g - position) * tokens % lanes
                    block = jnp.where(group == g, pltpu.roll(mixed[g], shift, 1), block)
            out_ref[quarters * position + quarter] = block.astype(BF)


def merge_kernel(
    x_ref, w_out_ref, gain_ref, bias_ref, *refs
):
    w0, w1, *rest, out_ref, att_ref, w_ref, sems = refs
    me, group = lax.axis_index("wide"), lax.axis_index("grp")
    position, quarter = me // 4, me % 4
    blocks, dim, lanes = x_ref.shape
    pairs = blocks // 2
    depth = w0.shape[0]
    out_width = w0.shape[1]
    width = w_out_ref.shape[1]
    copies = []
    common, share = rest[0].shape[0], rest[1].shape[0]
    places = [(w0, 0, 0), (w1, 1, 0)]
    for k in (2, 3):
        both, mine, theirs = rest[3 * (k - 2) : 3 * (k - 1)]
        places += [(both, k, 0), (mine, k, common + share * group), (theirs, k, common + share * (1 - group))]
    for n, (source, k, first) in enumerate(places):
        spot = pl.multiple_of(flipped(quarter, k) * depth + first, 16)
        copies.append(pltpu.make_async_copy(source, w_ref.at[pl.ds(spot, source.shape[0]), :], sems.at[n]))
        copies[-1].start()
    left = lax.broadcasted_iota(jnp.int32, (dim, lanes), 1) < lanes // 2
    for pair in range(pairs):
        first, second = x_ref[pair].astype(F32), x_ref[pairs + pair].astype(F32)
        upper = jnp.where(left, first, pltpu.roll(second, lanes // 2, 1))
        lower = jnp.where(left, pltpu.roll(first, lanes // 2, 1), second)
        att_ref[2 * dim * pair : 2 * dim * (pair + 1), :] = jnp.concatenate([upper, lower], 0).astype(BF)
    mixed = lax.dot_general(
        att_ref[...], w_out_ref[...], (((0,), (0,)), ((), ())), preferred_element_type=F32
    )
    mixed = mixed.astype(BF).astype(F32)
    centre = jnp.sum(mixed, axis=1, keepdims=True) / width
    centered = mixed - centre
    square = jnp.sum(centered * centered, axis=1, keepdims=True)
    here = pl.ds(pl.multiple_of(position * width, LANES), width)
    gain, bias = gain_ref[:, here], bias_ref[:, here]
    row = lax.broadcasted_iota(jnp.int32, (16, width), 0)
    extra = jnp.zeros((16, width), F32)
    for k, line in enumerate(pieces(gain, 2) + pieces(bias, 2)):
        extra = jnp.where(row == k, line, extra)
    left_side = jnp.concatenate([(centered * gain).astype(BF), extra.astype(BF)], 0)
    lane = lax.broadcasted_iota(jnp.int32, (lanes, LANES), 1)
    stats = jnp.zeros((lanes, LANES), F32)
    for k, column in enumerate(pieces(centre, 3) + pieces(square, 3)):
        stats = jnp.where(lane == k, column, stats)
    stats = stats.astype(BF)
    for copy in copies:
        copy.wait()
    planes, tokens, _ = out_ref.shape
    half = tokens // 2
    step = 2 * LANES
    shared = [None] * tokens
    for begin in range(0, out_width, step):
        part = jnp.dot(left_side, w_ref[:, begin : begin + step], preferred_element_type=F32)
        for plane in range(planes):
            out_ref[flipped(position, plane), :, begin : begin + step] = part[plane * tokens : (plane + 1) * tokens].astype(BF)
        scale = part[lanes : lanes + 1] + part[lanes + 1 : lanes + 2]
        shift = part[lanes + 2 : lanes + 3] + part[lanes + 3 : lanes + 4]
        for k in range(step // LANES):
            shared[begin // LANES + k] = scale[:, k * LANES : (k + 1) * LANES]
            shared[half + begin // LANES + k] = shift[:, k * LANES : (k + 1) * LANES]
    shared = jnp.concatenate(shared, 0).astype(BF)
    for plane in range(planes):
        out_ref[flipped(position, plane), :, out_width : out_width + LANES] = shared
        out_ref[flipped(position, plane), :, out_width + LANES :] = stats[plane * tokens : (plane + 1) * tokens]


def route_kernel(x0, x1, x2, x3, router_ref, ids_ref, out_ref, *, merge_width, experts):
    blocks = (x0, x1, x2, x3)
    planes, tokens = len(blocks), x0.shape[0]
    out_width = out_ref.shape[1] - LANES
    half = tokens // 2
    stats = [blocks[p][:, out_width + LANES :].astype(F32) for p in range(planes)]
    shared = [blocks[p][:, out_width : out_width + LANES].astype(F32) for p in range(planes)]
    centres = [s[:, 0:1] + s[:, 1:2] + s[:, 2:3] for s in stats]
    squares = [s[:, 3:4] + s[:, 4:5] + s[:, 5:6] for s in stats]
    mean = sum(centres) / planes
    offsets = [c - mean for c in centres]
    spread = sum(q + (merge_width // planes) * (o * o) for q, o in zip(squares, offsets)) / merge_width
    inverse = lax.rsqrt(spread + norm_eps)
    bias = sum(shared)
    for k in range(out_width // LANES):
        cut = slice(k * LANES, (k + 1) * LANES)
        total = sum(blocks[p][:, cut].astype(F32) for p in range(planes))
        total += sum(offsets[p] * shared[p][k : k + 1] for p in range(planes))
        out_ref[:, cut] = (total * inverse + bias[half + k : half + k + 1]).astype(BF)
    logits = jnp.dot(out_ref[:, :out_width], router_ref[...], preferred_element_type=F32)
    lane = lax.broadcasted_iota(jnp.int32, (tokens, LANES), 1)
    expert = lane % experts
    chosen = lane < 0
    for k in range(ids_ref.shape[1]):
        chosen = chosen | (ids_ref[:, k : k + 1] == expert)
    gates = jnp.where(chosen & (lane < 2 * experts), 1.0 / (1.0 + jnp.exp(-logits)), 0.0)
    total = jnp.sum(jnp.where(lane < experts, gates, 0.0), axis=1, keepdims=True)
    weight = route_scale * gates / total
    high, low = pieces(weight, 2)
    out_ref[:, out_width:] = jnp.where(lane < experts, high, low).astype(BF)


def expert_kernel(*refs, experts, cuts):
    *blocks, gate_hbm, up_hbm, down_hbm, own_ref, other_ref, x_ref, gate_ref, up_ref, down_ref, sems = refs
    tokens, width = own_ref.shape[1:]
    half = len(blocks) // 2
    copies = []
    for k, cut in enumerate(cuts):
        for kind, source, target in ((0, gate_hbm, gate_ref), (1, up_hbm, up_ref)):
            copies.append(pltpu.make_async_copy(source.at[0, cut, :], target.at[cut, :], sems.at[2 * k + kind]))
            copies[-1].start()
    last = pltpu.make_async_copy(down_hbm.at[0], down_ref, sems.at[2 * len(cuts)])
    last.start()
    expert = lax.axis_index("wide") // 2
    lane = lax.broadcasted_iota(jnp.int32, (tokens, LANES), 1)
    weights = []
    for k, block in enumerate(blocks):
        x_ref[k * tokens : (k + 1) * tokens, :] = block[:, :width]
        picked = (lane == expert) | (lane == expert + experts)
        picked = jnp.where(picked, block[:, width:].astype(F32), 0.0)
        weights.append(jnp.sum(picked, axis=1, keepdims=True))
    inputs = x_ref[...]
    turned = (((1,), (1,)), ((), ()))
    hidden = []
    for k, cut in enumerate(cuts):
        copies[2 * k].wait()
        gate = lax.dot_general(inputs, gate_ref[cut, :], turned, preferred_element_type=F32)
        copies[2 * k + 1].wait()
        up = lax.dot_general(inputs, up_ref[cut, :], turned, preferred_element_type=F32)
        hidden.append((gate / (1.0 + jnp.exp(-gate)) * up).astype(BF))
    hidden = jnp.concatenate(hidden, 1)
    last.wait()
    step = 4 * LANES
    for begin in range(0, width, step):
        product = jnp.dot(hidden, down_ref[:, begin : begin + step], preferred_element_type=F32)
        for k in range(len(blocks)):
            value = (product[k * tokens : (k + 1) * tokens] * weights[k]).astype(BF)
            out_ref = own_ref if k < half else other_ref
            out_ref[k % half, :, begin : begin + step] = value


def crossed(value, mask):
    pairs = [(source, source ^ mask) for source in range(lax.axis_size("wide"))]
    return lax.ppermute(value, "wide", pairs)


def local(
    qkv, grid, w_out, ln_gain, ln_bias, w_merge, w_router, expert_ids, slot_pos, w_gate, w_up, w_down
):
    devices = lax.axis_size("wide")
    rows = qkv.shape[0]
    vit_width = w_out.shape[0]
    experts = w_router.shape[1]
    out_width = w_merge.shape[1]
    tokens = rows // 4
    peers = devices // CLIPS
    suits = (
        devices == HEADS
        and peers == 8
        and rows == LANES
        and devices == 2 * experts
        and 2 * out_width == tokens * LANES
        and 4 * w_merge.shape[0] == vit_width
        and lax.axis_size("grp") == 2
        and w_merge.shape[0] % 32 == 0
    )
    if not suits:
        return general(
            qkv, grid, w_out, ln_gain, ln_bias, w_merge, w_router, expert_ids, slot_pos, w_gate, w_up, w_down
        )
    part = vit_width // peers
    dim = vit_width // HEADS
    depth = w_merge.shape[0]
    share = depth // 64 * 16
    packed, common, shared = pl.pallas_call(
        pack_kernel,
        out_shape=[
            jax.ShapeDtypeStruct((peers, 3 * part, rows), BF),
            jax.ShapeDtypeStruct((depth - 2 * share, out_width), BF),
            jax.ShapeDtypeStruct((share, out_width), BF),
        ],
        in_specs=[VMEM, HBM],
        out_specs=[VMEM] * 3,
        scratch_shapes=[pltpu.SemaphoreType.DMA((2,))],
        compiler_params=params(56),
    )(qkv, w_merge)
    clips = [[c * peers + i for i in range(peers)] for c in range(CLIPS)]
    gathered = lax.all_to_all(
        packed, "wide", split_axis=0, concat_axis=0, tiled=True, axis_index_groups=clips
    )
    gathered, common, shared, held = lax.optimization_barrier((gathered, common, shared, w_merge))
    mine_y = crossed(shared, 2)
    common_y = crossed(common, 2)
    attended = pl.pallas_call(
        attend_kernel,
        out_shape=jax.ShapeDtypeStruct((devices, dim, rows), BF),
        in_specs=[VMEM, SMEM],
        out_specs=VMEM,
        compiler_params=params(20),
        cost_estimate=cost(2**32, 2**22, 2**21),
    )(gathered, grid)
    held_c = crossed(held, 1)
    attended, mine_y = lax.optimization_barrier((attended, mine_y))
    theirs_y = lax.ppermute(mine_y, "grp", [(0, 1), (1, 0)])
    mine_yc = crossed(mine_y, 1)
    returned = lax.all_to_all(attended, "wide", split_axis=0, concat_axis=0, tiled=True)
    returned, common_y, theirs_y = lax.optimization_barrier((returned, common_y, theirs_y))
    common_yc, theirs_yc = crossed(common_y, 1), crossed(theirs_y, 1)
    planes = devices // 4
    message = out_width + 2 * LANES
    partial = pl.pallas_call(
        merge_kernel,
        out_shape=jax.ShapeDtypeStruct((planes, tokens, message), BF),
        in_specs=[VMEM] * 4 + [pl.BlockSpec(memory_space=pl.ANY)] * 8,
        out_specs=VMEM,
        scratch_shapes=[
            pltpu.VMEM((vit_width, rows), BF),
            pltpu.VMEM((vit_width, out_width), BF),
            pltpu.SemaphoreType.DMA((8,)),
        ],
        compiler_params=params(20),
    )(
        returned,
        w_out,
        ln_gain.reshape(1, 4 * vit_width),
        ln_bias.reshape(1, 4 * vit_width),
        w_merge,
        held_c,
        common_y,
        mine_y,
        theirs_y,
        common_yc,
        mine_yc,
        theirs_yc,
    )
    along = (8, 12, 4)
    arrived = [partial[0]] + [crossed(partial[mask // 4], mask) for mask in along]
    router = jnp.concatenate(
        [w_router, w_router, jnp.zeros((out_width, LANES - 2 * experts), BF)], 1
    )
    routed = pl.pallas_call(
        lambda *refs: route_kernel(*refs, merge_width=4 * vit_width, experts=experts),
        out_shape=jax.ShapeDtypeStruct((tokens, out_width + LANES), BF),
        in_specs=[VMEM] * 6,
        out_specs=VMEM,
        compiler_params=params(6),
    )(*arrived, router, expert_ids)
    near = [routed] + [crossed(routed, mask) for mask in along]
    far = [crossed(block, 2) for block in near]
    *near, far[0] = lax.optimization_barrier((*near, far[0]))
    gate_turned, up_turned = jnp.swapaxes(w_gate, 1, 2), jnp.swapaxes(w_up, 1, 2)

    inner = w_down.shape[1]
    cuts = [slice(k, min(k + 2 * LANES, inner)) for k in range(0, inner, 2 * LANES)]

    def experts_of(blocks):
        return pl.pallas_call(
            lambda *refs: expert_kernel(*refs, experts=experts, cuts=cuts),
            out_shape=[jax.ShapeDtypeStruct((planes, tokens, out_width), BF)] * 2,
            in_specs=[VMEM] * (2 * planes) + [HBM] * 3,
            out_specs=[VMEM, VMEM],
            scratch_shapes=[
                pltpu.VMEM((2 * planes * tokens, out_width), BF),
                pltpu.VMEM((inner, out_width), BF),
                pltpu.VMEM((inner, out_width), BF),
                pltpu.VMEM((inner, out_width), BF),
                pltpu.SemaphoreType.DMA((2 * len(cuts) + 1,)),
            ],
            compiler_params=params(50),
            cost_estimate=cost(2**32, 2**24),
        )(*blocks, *[crossed(block, 1) for block in blocks], gate_turned, up_turned, w_down)

    def scattered(blocks):
        others = [crossed(blocks[1 + along.index(mask)], mask) for mask in along]
        return blocks[0].astype(F32) + sum(block.astype(F32) for block in others)

    def paired(own, other):
        return (own.astype(F32) + crossed(other, 1).astype(F32)).astype(BF)

    near_own, near_other = experts_of(near)
    *far, near_own, near_other = lax.optimization_barrier((*far, near_own, near_other))
    far_own, far_other = experts_of(far)
    near_sum = scattered(paired(near_own, near_other))
    far_out, near_sum = lax.optimization_barrier((paired(far_own, far_other), near_sum))
    across = [crossed(far_out[k], 2 + mask) for k, mask in enumerate(along, 1)]
    across.append(crossed(far_out[0], 2))
    return (near_sum + sum(block.astype(F32) for block in across)).astype(BF)


def solution(mesh):
    placed = (
        P(("grp", "wide"), None),
        P("grp", None),
        P(),
        P(),
        P(),
        P("wide", None),
        P(),
        P(("grp", "wide"), None),
        P(("grp", "wide"), None),
        P("wide", None, None),
        P("wide", None, None),
        P("wide", None, None),
    )
    return jax.shard_map(
        local, mesh=mesh, in_specs=placed, out_specs=P(("grp", "wide"), None), check_vma=False
    )
```

```python
import jax
import jax.numpy as jnp
from jax import lax
from jax.experimental import pallas as pl
from jax.experimental.pallas import tpu as pltpu
from jax.sharding import PartitionSpec as P

HEADS = 16
CLIPS = 2


route_scale = 2.446
norm_eps = 1e-05


def swapped(value, axis, stride):
    mask = 2**stride
    pairs = [(source, source ^ mask) for source in range(lax.axis_size(axis))]
    return lax.ppermute(value, axis, pairs)


def ordered_pair(own_part, partner, upper_bit):
    return jnp.where(
        upper_bit == 1,
        jnp.concatenate([partner, own_part], 0),
        jnp.concatenate([own_part, partner], 0),
    )


def general(
    qkv,
    grid,
    w_out,
    ln_gain,
    ln_bias,
    w_merge,
    w_router,
    expert_ids,
    slot_pos,
    w_gate,
    w_up,
    w_down,
):
    devices = lax.axis_size("wide")
    position_self = lax.axis_index("wide")
    vit_width = w_out.shape[0]
    head_dim = vit_width // HEADS
    groups = devices // HEADS
    local_rows = qkv.shape[0]
    sub_rows = local_rows // groups
    per_clip = devices // CLIPS
    query_send = (
        qkv[:, :vit_width]
        .reshape(groups, sub_rows, HEADS, head_dim)
        .transpose(2, 0, 1, 3)
        .reshape(devices, sub_rows, head_dim)
    )
    key_value = jnp.concatenate(
        [
            qkv[:, vit_width : 2 * vit_width].reshape(local_rows, HEADS, head_dim),
            qkv[:, 2 * vit_width :].reshape(local_rows, HEADS, head_dim),
        ],
        axis=2,
    )
    spread_send = jnp.broadcast_to(
        key_value.transpose(1, 0, 2)[:, None], (HEADS, groups, local_rows, 2 * head_dim)
    ).reshape(devices, local_rows, 2 * head_dim)
    queries, key_rows = (
        lax.all_to_all(query_send, "wide", split_axis=0, concat_axis=0, tiled=True),
        lax.all_to_all(spread_send, "wide", split_axis=0, concat_axis=0, tiled=True),
    )
    key_rows = key_rows[None]
    key_groups = key_rows.shape[0]
    key_count = key_rows.shape[2]
    key_place = (
        jnp.arange(per_clip, dtype=jnp.int32)[None, :, None] * local_rows
        + jnp.arange(key_groups, dtype=jnp.int32)[:, None, None] * local_rows
        + jnp.arange(key_count, dtype=jnp.int32)[None, None, :]
    ).reshape(-1)
    patch_counts = grid[:, 0] * grid[:, 1]
    clip_queries = queries.reshape(CLIPS, per_clip * sub_rows, head_dim)
    query_block_rows = min(512, per_clip * sub_rows)
    score_scale = head_dim ** (-0.5)

    def attend(clip_index):
        key_block = lax.dynamic_slice_in_dim(key_rows, clip_index * per_clip, per_clip, 1).reshape(
            -1, 2 * head_dim
        )
        visible = key_place < lax.dynamic_index_in_dim(patch_counts, clip_index, 0, keepdims=False)
        query_all = lax.dynamic_index_in_dim(clip_queries, clip_index, 0, keepdims=False)

        def one_block(query_block):
            scores = (
                lax.dot_general(
                    query_block,
                    key_block[:, :head_dim],
                    (((1,), (1,)), ((), ())),
                    preferred_element_type=jnp.float32,
                )
                * score_scale
            )
            scores = jnp.where(visible[None, :], scores, -jnp.inf)
            highest = jnp.max(scores, axis=1, keepdims=True)
            weights = jnp.exp(scores - highest)
            running = jnp.sum(weights, axis=1, keepdims=True)
            mixture = jnp.dot(
                weights.astype(jnp.bfloat16),
                key_block[:, head_dim:],
                preferred_element_type=jnp.float32,
            )
            return (mixture / running).astype(jnp.bfloat16)

        return lax.map(one_block, query_all.reshape(-1, query_block_rows, head_dim)).reshape(
            -1, head_dim
        )

    attended = lax.map(attend, jnp.arange(CLIPS, dtype=jnp.int32))
    returned = lax.all_to_all(
        attended.reshape(devices, sub_rows, head_dim),
        "wide",
        split_axis=0,
        concat_axis=0,
        tiled=True,
    )
    attention = (
        returned.reshape(HEADS, groups, sub_rows, head_dim)
        .transpose(1, 2, 0, 3)
        .reshape(local_rows, vit_width)
    )
    projected = jnp.dot(attention, w_out, preferred_element_type=jnp.float32).astype(jnp.bfloat16)
    merged = projected.reshape(local_rows // 4, 4 * vit_width).astype(jnp.float32)
    centre = jnp.mean(merged, axis=1, keepdims=True)
    centered = merged - centre
    spread = jnp.mean(centered * centered, axis=1, keepdims=True)
    normed = (centered * lax.rsqrt(spread + norm_eps) * ln_gain + ln_bias).astype(jnp.bfloat16)
    tok_groups = min(8, devices)
    feat_groups = devices // tok_groups
    merge_rows = w_merge
    for bit_index in range(tok_groups.bit_length() - 1):
        partner = swapped(merge_rows, "wide", bit_index)
        upper_bit = position_self // (1 << bit_index) % 2
        merge_rows = ordered_pair(merge_rows, partner, upper_bit)
    token_count = normed.shape[0]
    part_rows = token_count // tok_groups
    feat_width = normed.shape[1] // feat_groups
    out_width = w_merge.shape[1]
    merge_send = (
        normed.reshape(tok_groups, part_rows, feat_groups, feat_width)
        .transpose(2, 0, 1, 3)
        .reshape(devices, part_rows, feat_width)
    )
    flat_rows = lax.all_to_all(merge_send, "wide", split_axis=0, concat_axis=0, tiled=True).reshape(
        -1, feat_width
    )
    partial_value = jnp.dot(flat_rows, merge_rows, preferred_element_type=jnp.float32).reshape(
        devices, -1, out_width
    )
    summed = lax.all_to_all(partial_value, "wide", split_axis=0, concat_axis=0, tiled=True)
    tokens = (
        jnp.sum(summed.reshape(feat_groups, tok_groups, part_rows, out_width), axis=0)
        .reshape(token_count, out_width)
        .astype(jnp.bfloat16)
    )
    logits = jnp.dot(tokens, w_router, preferred_element_type=jnp.float32)
    experts = w_router.shape[1]
    top_count = expert_ids.shape[1]
    matches = expert_ids[:, :, None] == jnp.arange(experts, dtype=jnp.int32)[None, None, :]
    chosen = jnp.sum(jnp.where(matches, logits[:, None, :], 0.0), axis=2)
    gate_values = jax.nn.sigmoid(chosen)
    route_weight = route_scale * gate_values / jnp.sum(gate_values, axis=1, keepdims=True)
    capacity = min(token_count, 2 * token_count * top_count // experts)
    slot_count = experts * capacity
    target = expert_ids * capacity + slot_pos
    one_hot = jnp.any(
        target[None, :, :] == jnp.arange(slot_count, dtype=jnp.int32)[:, None, None], axis=2
    ).astype(jnp.bfloat16)
    buffer = jnp.dot(one_hot, tokens, preferred_element_type=jnp.float32).astype(jnp.bfloat16)
    gate_half = w_gate[0]
    up_half = w_up[0]
    down_half = w_down[0]
    half_cap = capacity // 2
    dispatch = buffer.reshape(devices, half_cap, out_width)
    portion = lax.all_to_all(dispatch, "wide", split_axis=0, concat_axis=0, tiled=True)
    item_count = portion.shape[1]
    partner_rows = swapped(portion, "wide", 0)
    both_rows = jnp.concatenate([portion, partner_rows], axis=1)
    flat_rows = both_rows.reshape(-1, out_width)
    gate_part = jnp.dot(flat_rows, gate_half, preferred_element_type=jnp.float32)
    up_part = jnp.dot(flat_rows, up_half, preferred_element_type=jnp.float32)
    hidden = (jax.nn.silu(gate_part) * up_part).astype(jnp.bfloat16)
    product = (
        jnp.dot(hidden, down_half, preferred_element_type=jnp.float32)
        .astype(jnp.bfloat16)
        .reshape(devices, 2 * item_count, out_width)
    )
    from_partner = swapped(product[:, item_count:], "wide", 0)
    joined = (
        product[:, :item_count].astype(jnp.float32) + from_partner.astype(jnp.float32)
    ).astype(jnp.bfloat16)
    answers = lax.all_to_all(joined, "wide", split_axis=0, concat_axis=0, tiled=True)
    slot_result = answers.reshape(slot_count, out_width)
    slot_result = lax.optimization_barrier(slot_result)
    picked = jnp.take(slot_result, target.reshape(-1), axis=0).reshape(
        token_count, top_count, out_width
    )
    return jnp.sum(picked.astype(jnp.float32) * route_weight[:, :, None], axis=1).astype(
        jnp.bfloat16
    )


BF = jnp.bfloat16
F32 = jnp.float32
VMEM = pl.BlockSpec(memory_space=pltpu.VMEM)
SMEM = pl.BlockSpec(memory_space=pltpu.SMEM)
HBM = pl.BlockSpec(memory_space=pltpu.HBM)
LANES = 128
MASKED = -1e30
LOG2E = 1.4426950408889634


def params(mib):
    return pltpu.CompilerParams(vmem_limit_bytes=mib * 2**20)


def cost(flops, size, exps=0):
    return pl.CostEstimate(flops=flops, bytes_accessed=size, transcendentals=exps)


def flipped(number, bits):
    low = (number % 2 + bits % 2) % 2
    return 2 * ((number // 2 + bits // 2) % 2) + low


def pieces(value, count):
    out = []
    for _ in range(count):
        piece = value.astype(BF).astype(F32)
        out.append(piece)
        value = value - piece
    return out


def pack_kernel(qkv_hbm, merge_ref, out_ref, common_ref, share_ref, qkv_ref, sems):
    common, share = common_ref.shape[0], share_ref.shape[0]
    spot = pl.multiple_of(common + share * lax.axis_index("grp"), 16)
    third = qkv_hbm.shape[1] // 3
    loads = []
    for kind in range(3):
        cut = slice(kind * third, (kind + 1) * third)
        loads.append(pltpu.make_async_copy(qkv_hbm.at[:, cut], qkv_ref.at[:, cut], sems.at[2 + kind]))
        loads[-1].start()
    copies = [
        pltpu.make_async_copy(merge_ref.at[pl.ds(spot, share), :], share_ref, sems.at[0]),
        pltpu.make_async_copy(merge_ref.at[pl.ds(0, common), :], common_ref, sems.at[1]),
    ]
    for copy in copies:
        copy.start()
    rows, width = qkv_ref.shape
    tokens = rows // 4
    peers, parts, _ = out_ref.shape
    source = lax.broadcasted_iota(jnp.int32, (rows, rows), 0)
    place = lax.broadcasted_iota(jnp.int32, (rows, rows), 1)
    order = jnp.where(source == 4 * (place % tokens) + place // tokens, 1.0, 0.0).astype(BF)
    part = parts // 3
    for kind in range(3):
        loads[kind].wait()
        turned = lax.dot_general(
            qkv_ref[:, kind * third : (kind + 1) * third],
            order,
            (((0,), (0,)), ((), ())),
            preferred_element_type=F32,
        ).astype(BF)
        for peer in range(peers):
            out_ref[peer, kind * part : (kind + 1) * part, :] = turned[peer * part : (peer + 1) * part]
    for copy in copies:
        copy.wait()


def attend_kernel(x_ref, grid_ref, out_ref):
    peers, parts, lanes = x_ref.shape
    part = parts // 3
    dim = part // 2
    quarters = 4
    sides = peers // quarters
    tokens = lanes // 4
    clip = lax.axis_index("wide") // peers
    count = grid_ref[clip, 0] * grid_ref[clip, 1]
    factor = dim ** (-0.5) * LOG2E
    keys = jnp.concatenate([x_ref[s, part : 2 * part, :] for s in range(peers)], 1)
    lane = lax.broadcasted_iota(jnp.int32, (16, peers * lanes), 1)
    row = lax.broadcasted_iota(jnp.int32, (16, peers * lanes), 0)
    inner = lane % lanes
    place = lane // lanes * lanes + 4 * (inner % tokens) + inner // tokens
    hidden = jnp.where((row == 0) & (place >= count), MASKED, 0.0).astype(BF)
    keys = jnp.concatenate([keys, hidden], 0).T
    values = jnp.concatenate([x_ref[s, 2 * part :, :] for s in range(peers)], 1).astype(F32)
    values = [values[:dim].astype(BF), values[dim:].astype(BF)]
    ones = jnp.where(lax.broadcasted_iota(jnp.int32, (16, sides * lanes), 0) == 0, 1.0, 0.0).astype(BF)
    head_row = lax.broadcasted_iota(jnp.int32, (part, sides * lanes), 0) // dim
    group = lax.broadcasted_iota(jnp.int32, (dim, lanes), 1) // tokens
    for quarter in range(quarters):
        query = jnp.concatenate(
            [x_ref[quarter + quarters * s, :part, :] for s in range(sides)], 1
        ).astype(F32)
        mixed = []
        for head in range(2):
            own = jnp.concatenate([jnp.where(head_row == head, query, 0.0).astype(BF), ones], 0)
            scores = jnp.dot(keys, own, preferred_element_type=F32)
            highest = jnp.max(scores, axis=0, keepdims=True)
            weights = jnp.exp2((scores - highest) * factor)
            total = jnp.sum(weights, axis=0, keepdims=True)
            value = jnp.dot(values[head], weights.astype(BF), preferred_element_type=F32) / total
            mixed += [value[:, s * lanes : (s + 1) * lanes] for s in range(sides)]
        for position in range(4):
            block = mixed[position]
            for g in range(4):
                if g != position:
                    shift = (g - position) * tokens % lanes
                    block = jnp.where(group == g, pltpu.roll(mixed[g], shift, 1), block)
            out_ref[quarters * position + quarter] = block.astype(BF)


def merge_kernel(
    x_ref, w_out_hbm, gain_ref, bias_ref, *refs
):
    w0, w1, *rest, out_ref, att_ref, w_ref, w_out_ref, sems = refs
    me, group = lax.axis_index("wide"), lax.axis_index("grp")
    position, quarter = me // 4, me % 4
    blocks, dim, lanes = x_ref.shape
    pairs = blocks // 2
    depth = w0.shape[0]
    out_width = w0.shape[1]
    width = w_out_ref.shape[1]
    first_copy = pltpu.make_async_copy(w_out_hbm, w_out_ref, sems.at[8])
    first_copy.start()
    copies = []
    common, share = rest[0].shape[0], rest[1].shape[0]
    places = [(w0, 0, 0), (w1, 1, 0)]
    for k in (2, 3):
        both, mine, theirs = rest[3 * (k - 2) : 3 * (k - 1)]
        places += [(both, k, 0), (mine, k, common + share * group), (theirs, k, common + share * (1 - group))]
    for n, (source, k, first) in enumerate(places):
        spot = pl.multiple_of(flipped(quarter, k) * depth + first, 16)
        copies.append(pltpu.make_async_copy(source, w_ref.at[pl.ds(spot, source.shape[0]), :], sems.at[n]))
        copies[-1].start()
    left = lax.broadcasted_iota(jnp.int32, (dim, lanes), 1) < lanes // 2
    for pair in range(pairs):
        first, second = x_ref[pair].astype(F32), x_ref[pairs + pair].astype(F32)
        upper = jnp.where(left, first, pltpu.roll(second, lanes // 2, 1))
        lower = jnp.where(left, pltpu.roll(first, lanes // 2, 1), second)
        att_ref[2 * dim * pair : 2 * dim * (pair + 1), :] = jnp.concatenate([upper, lower], 0).astype(BF)
    first_copy.wait()
    mixed = lax.dot_general(
        att_ref[...], w_out_ref[...], (((0,), (0,)), ((), ())), preferred_element_type=F32
    )
    mixed = mixed.astype(BF).astype(F32)
    centre = jnp.sum(mixed, axis=1, keepdims=True) / width
    centered = mixed - centre
    square = jnp.sum(centered * centered, axis=1, keepdims=True)
    here = pl.ds(pl.multiple_of(position * width, LANES), width)
    gain, bias = gain_ref[:, here], bias_ref[:, here]
    row = lax.broadcasted_iota(jnp.int32, (16, width), 0)
    extra = jnp.zeros((16, width), F32)
    for k, line in enumerate(pieces(gain, 2) + pieces(bias, 2)):
        extra = jnp.where(row == k, line, extra)
    left_side = jnp.concatenate([(centered * gain).astype(BF), extra.astype(BF)], 0)
    lane = lax.broadcasted_iota(jnp.int32, (lanes, LANES), 1)
    stats = jnp.zeros((lanes, LANES), F32)
    for k, column in enumerate(pieces(centre, 3) + pieces(square, 3)):
        stats = jnp.where(lane == k, column, stats)
    stats = stats.astype(BF)
    for copy in copies:
        copy.wait()
    planes, tokens, _ = out_ref.shape
    half = tokens // 2
    step = 2 * LANES
    shared = [None] * tokens
    for begin in range(0, out_width, step):
        part = jnp.dot(left_side, w_ref[:, begin : begin + step], preferred_element_type=F32)
        for plane in range(planes):
            out_ref[flipped(position, plane), :, begin : begin + step] = part[plane * tokens : (plane + 1) * tokens].astype(BF)
        scale = part[lanes : lanes + 1] + part[lanes + 1 : lanes + 2]
        shift = part[lanes + 2 : lanes + 3] + part[lanes + 3 : lanes + 4]
        for k in range(step // LANES):
            shared[begin // LANES + k] = scale[:, k * LANES : (k + 1) * LANES]
            shared[half + begin // LANES + k] = shift[:, k * LANES : (k + 1) * LANES]
    shared = jnp.concatenate(shared, 0).astype(BF)
    for plane in range(planes):
        out_ref[flipped(position, plane), :, out_width : out_width + LANES] = shared
        out_ref[flipped(position, plane), :, out_width + LANES :] = stats[plane * tokens : (plane + 1) * tokens]


def route_kernel(x0, x1, x2, x3, router_ref, ids_ref, out_ref, *, merge_width, experts):
    blocks = (x0, x1, x2, x3)
    planes, tokens = len(blocks), x0.shape[0]
    out_width = out_ref.shape[1] - LANES
    half = tokens // 2
    stats = [blocks[p][:, out_width + LANES :].astype(F32) for p in range(planes)]
    shared = [blocks[p][:, out_width : out_width + LANES].astype(F32) for p in range(planes)]
    centres = [s[:, 0:1] + s[:, 1:2] + s[:, 2:3] for s in stats]
    squares = [s[:, 3:4] + s[:, 4:5] + s[:, 5:6] for s in stats]
    mean = sum(centres) / planes
    offsets = [c - mean for c in centres]
    spread = sum(q + (merge_width // planes) * (o * o) for q, o in zip(squares, offsets)) / merge_width
    inverse = lax.rsqrt(spread + norm_eps)
    bias = sum(shared)
    for k in range(out_width // LANES):
        cut = slice(k * LANES, (k + 1) * LANES)
        total = sum(blocks[p][:, cut].astype(F32) for p in range(planes))
        total += sum(offsets[p] * shared[p][k : k + 1] for p in range(planes))
        out_ref[:, cut] = (total * inverse + bias[half + k : half + k + 1]).astype(BF)
    logits = jnp.dot(out_ref[:, :out_width], router_ref[...], preferred_element_type=F32)
    lane = lax.broadcasted_iota(jnp.int32, (tokens, LANES), 1)
    expert = lane % experts
    chosen = lane < 0
    for k in range(ids_ref.shape[1]):
        chosen = chosen | (ids_ref[:, k : k + 1] == expert)
    gates = jnp.where(chosen & (lane < 2 * experts), 1.0 / (1.0 + jnp.exp(-logits)), 0.0)
    total = jnp.sum(jnp.where(lane < experts, gates, 0.0), axis=1, keepdims=True)
    weight = route_scale * gates / total
    high, low = pieces(weight, 2)
    out_ref[:, out_width:] = jnp.where(lane < experts, high, low).astype(BF)


def expert_kernel(*refs, experts, cuts):
    *blocks, gate_hbm, up_hbm, down_hbm, own_ref, other_ref, x_ref, gate_ref, up_ref, down_ref, sems = refs
    tokens, width = own_ref.shape[1:]
    half = len(blocks) // 2
    copies = []
    for k, cut in enumerate(cuts):
        for kind, source, target in ((0, gate_hbm, gate_ref), (1, up_hbm, up_ref)):
            copies.append(pltpu.make_async_copy(source.at[0, cut, :], target.at[cut, :], sems.at[2 * k + kind]))
            copies[-1].start()
    last = pltpu.make_async_copy(down_hbm.at[0], down_ref, sems.at[2 * len(cuts)])
    last.start()
    expert = lax.axis_index("wide") // 2
    lane = lax.broadcasted_iota(jnp.int32, (tokens, LANES), 1)
    weights = []
    for k, block in enumerate(blocks):
        x_ref[k * tokens : (k + 1) * tokens, :] = block[:, :width]
        picked = (lane == expert) | (lane == expert + experts)
        picked = jnp.where(picked, block[:, width:].astype(F32), 0.0)
        weights.append(jnp.sum(picked, axis=1, keepdims=True))
    inputs = x_ref[...]
    turned = (((1,), (1,)), ((), ()))
    hidden = []
    for k, cut in enumerate(cuts):
        copies[2 * k].wait()
        gate = lax.dot_general(inputs, gate_ref[cut, :], turned, preferred_element_type=F32)
        copies[2 * k + 1].wait()
        up = lax.dot_general(inputs, up_ref[cut, :], turned, preferred_element_type=F32)
        hidden.append((gate / (1.0 + jnp.exp(-gate)) * up).astype(BF))
    hidden = jnp.concatenate(hidden, 1)
    last.wait()
    step = 4 * LANES
    for begin in range(0, width, step):
        product = jnp.dot(hidden, down_ref[:, begin : begin + step], preferred_element_type=F32)
        for k in range(len(blocks)):
            value = (product[k * tokens : (k + 1) * tokens] * weights[k]).astype(BF)
            out_ref = own_ref if k < half else other_ref
            out_ref[k % half, :, begin : begin + step] = value


def crossed(value, mask):
    pairs = [(source, source ^ mask) for source in range(lax.axis_size("wide"))]
    return lax.ppermute(value, "wide", pairs)


def local(
    qkv, grid, w_out, ln_gain, ln_bias, w_merge, w_router, expert_ids, slot_pos, w_gate, w_up, w_down
):
    devices = lax.axis_size("wide")
    rows = qkv.shape[0]
    vit_width = w_out.shape[0]
    experts = w_router.shape[1]
    out_width = w_merge.shape[1]
    tokens = rows // 4
    peers = devices // CLIPS
    suits = (
        devices == HEADS
        and peers == 8
        and rows == LANES
        and devices == 2 * experts
        and 2 * out_width == tokens * LANES
        and 4 * w_merge.shape[0] == vit_width
        and lax.axis_size("grp") == 2
        and w_merge.shape[0] % 32 == 0
    )
    if not suits:
        return general(
            qkv, grid, w_out, ln_gain, ln_bias, w_merge, w_router, expert_ids, slot_pos, w_gate, w_up, w_down
        )
    part = vit_width // peers
    dim = vit_width // HEADS
    depth = w_merge.shape[0]
    share = depth // 64 * 16
    packed, common, shared = pl.pallas_call(
        pack_kernel,
        out_shape=[
            jax.ShapeDtypeStruct((peers, 3 * part, rows), BF),
            jax.ShapeDtypeStruct((depth - 2 * share, out_width), BF),
            jax.ShapeDtypeStruct((share, out_width), BF),
        ],
        in_specs=[HBM, HBM],
        out_specs=[VMEM, HBM, HBM],
        scratch_shapes=[pltpu.VMEM(qkv.shape, BF), pltpu.SemaphoreType.DMA((5,))],
        compiler_params=params(56),
    )(qkv, w_merge)
    clips = [[c * peers + i for i in range(peers)] for c in range(CLIPS)]
    gathered = lax.all_to_all(
        packed, "wide", split_axis=0, concat_axis=0, tiled=True, axis_index_groups=clips
    )
    gathered, common, shared, held = lax.optimization_barrier((gathered, common, shared, w_merge))
    mine_y = crossed(shared, 2)
    common_y = crossed(common, 2)
    attended = pl.pallas_call(
        attend_kernel,
        out_shape=jax.ShapeDtypeStruct((devices, dim, rows), BF),
        in_specs=[VMEM, SMEM],
        out_specs=VMEM,
        compiler_params=params(20),
        cost_estimate=cost(2**32, 2**22, 2**21),
    )(gathered, grid)
    held_c = crossed(held, 1)
    attended, mine_y = lax.optimization_barrier((attended, mine_y))
    theirs_y = lax.ppermute(mine_y, "grp", [(0, 1), (1, 0)])
    mine_yc = crossed(mine_y, 1)
    returned = lax.all_to_all(attended, "wide", split_axis=0, concat_axis=0, tiled=True)
    returned, common_y, theirs_y = lax.optimization_barrier((returned, common_y, theirs_y))
    common_yc, theirs_yc = crossed(common_y, 1), crossed(theirs_y, 1)
    planes = devices // 4
    message = out_width + 2 * LANES
    partial = pl.pallas_call(
        merge_kernel,
        out_shape=jax.ShapeDtypeStruct((planes, tokens, message), BF),
        in_specs=[VMEM, HBM, VMEM, VMEM] + [pl.BlockSpec(memory_space=pl.ANY)] * 8,
        out_specs=VMEM,
        scratch_shapes=[
            pltpu.VMEM((vit_width, rows), BF),
            pltpu.VMEM((vit_width, out_width), BF),
            pltpu.VMEM((vit_width, vit_width), BF),
            pltpu.SemaphoreType.DMA((9,)),
        ],
        compiler_params=params(50),
    )(
        returned,
        w_out,
        ln_gain.reshape(1, 4 * vit_width),
        ln_bias.reshape(1, 4 * vit_width),
        w_merge,
        held_c,
        common_y,
        mine_y,
        theirs_y,
        common_yc,
        mine_yc,
        theirs_yc,
    )
    along = (8, 12, 4)
    arrived = [partial[0]] + [crossed(partial[mask // 4], mask) for mask in along]
    router = jnp.concatenate(
        [w_router, w_router, jnp.zeros((out_width, LANES - 2 * experts), BF)], 1
    )
    routed = pl.pallas_call(
        lambda *refs: route_kernel(*refs, merge_width=4 * vit_width, experts=experts),
        out_shape=jax.ShapeDtypeStruct((tokens, out_width + LANES), BF),
        in_specs=[VMEM] * 6,
        out_specs=VMEM,
        compiler_params=params(6),
    )(*arrived, router, expert_ids)
    near = [routed] + [crossed(routed, mask) for mask in along]
    far = [crossed(block, 2) for block in near]
    *near, far[0] = lax.optimization_barrier((*near, far[0]))
    gate_turned, up_turned = jnp.swapaxes(w_gate, 1, 2), jnp.swapaxes(w_up, 1, 2)

    inner = w_down.shape[1]
    cuts = [slice(k, min(k + 2 * LANES, inner)) for k in range(0, inner, 2 * LANES)]

    def experts_of(blocks):
        return pl.pallas_call(
            lambda *refs: expert_kernel(*refs, experts=experts, cuts=cuts),
            out_shape=[jax.ShapeDtypeStruct((planes, tokens, out_width), BF)] * 2,
            in_specs=[VMEM] * (2 * planes) + [HBM] * 3,
            out_specs=[VMEM, VMEM],
            scratch_shapes=[
                pltpu.VMEM((2 * planes * tokens, out_width), BF),
                pltpu.VMEM((inner, out_width), BF),
                pltpu.VMEM((inner, out_width), BF),
                pltpu.VMEM((inner, out_width), BF),
                pltpu.SemaphoreType.DMA((2 * len(cuts) + 1,)),
            ],
            compiler_params=params(50),
            cost_estimate=cost(2**32, 2**24),
        )(*blocks, *[crossed(block, 1) for block in blocks], gate_turned, up_turned, w_down)

    def scattered(blocks):
        others = [crossed(blocks[1 + along.index(mask)], mask) for mask in along]
        return blocks[0].astype(F32) + sum(block.astype(F32) for block in others)

    def paired(own, other):
        return (own.astype(F32) + crossed(other, 1).astype(F32)).astype(BF)

    near_own, near_other = experts_of(near)
    *far, near_own, near_other = lax.optimization_barrier((*far, near_own, near_other))
    far_own, far_other = experts_of(far)
    near_sum = scattered(paired(near_own, near_other))
    far_out, near_sum = lax.optimization_barrier((paired(far_own, far_other), near_sum))
    across = [crossed(far_out[k], 2 + mask) for k, mask in enumerate(along, 1)]
    across.append(crossed(far_out[0], 2))
    return (near_sum + sum(block.astype(F32) for block in across)).astype(BF)


def solution(mesh):
    placed = (
        P(("grp", "wide"), None),
        P("grp", None),
        P(),
        P(),
        P(),
        P("wide", None),
        P(),
        P(("grp", "wide"), None),
        P(("grp", "wide"), None),
        P("wide", None, None),
        P("wide", None, None),
        P("wide", None, None),
    )
    return jax.shard_map(
        local, mesh=mesh, in_specs=placed, out_specs=P(("grp", "wide"), None), check_vma=False
    )
```

```python
import jax
import jax.numpy as jnp
from jax import lax
from jax.experimental import pallas as pl
from jax.experimental.pallas import tpu as pltpu
from jax.sharding import PartitionSpec as P

HEADS = 16
CLIPS = 2


route_scale = 2.446
norm_eps = 1e-05


def swapped(value, axis, stride):
    mask = 2**stride
    pairs = [(source, source ^ mask) for source in range(lax.axis_size(axis))]
    return lax.ppermute(value, axis, pairs)


def ordered_pair(own_part, partner, upper_bit):
    return jnp.where(
        upper_bit == 1,
        jnp.concatenate([partner, own_part], 0),
        jnp.concatenate([own_part, partner], 0),
    )


def general(
    qkv,
    grid,
    w_out,
    ln_gain,
    ln_bias,
    w_merge,
    w_router,
    expert_ids,
    slot_pos,
    w_gate,
    w_up,
    w_down,
):
    devices = lax.axis_size("wide")
    position_self = lax.axis_index("wide")
    vit_width = w_out.shape[0]
    head_dim = vit_width // HEADS
    groups = devices // HEADS
    local_rows = qkv.shape[0]
    sub_rows = local_rows // groups
    per_clip = devices // CLIPS
    query_send = (
        qkv[:, :vit_width]
        .reshape(groups, sub_rows, HEADS, head_dim)
        .transpose(2, 0, 1, 3)
        .reshape(devices, sub_rows, head_dim)
    )
    key_value = jnp.concatenate(
        [
            qkv[:, vit_width : 2 * vit_width].reshape(local_rows, HEADS, head_dim),
            qkv[:, 2 * vit_width :].reshape(local_rows, HEADS, head_dim),
        ],
        axis=2,
    )
    spread_send = jnp.broadcast_to(
        key_value.transpose(1, 0, 2)[:, None], (HEADS, groups, local_rows, 2 * head_dim)
    ).reshape(devices, local_rows, 2 * head_dim)
    queries, key_rows = (
        lax.all_to_all(query_send, "wide", split_axis=0, concat_axis=0, tiled=True),
        lax.all_to_all(spread_send, "wide", split_axis=0, concat_axis=0, tiled=True),
    )
    key_rows = key_rows[None]
    key_groups = key_rows.shape[0]
    key_count = key_rows.shape[2]
    key_place = (
        jnp.arange(per_clip, dtype=jnp.int32)[None, :, None] * local_rows
        + jnp.arange(key_groups, dtype=jnp.int32)[:, None, None] * local_rows
        + jnp.arange(key_count, dtype=jnp.int32)[None, None, :]
    ).reshape(-1)
    patch_counts = grid[:, 0] * grid[:, 1]
    clip_queries = queries.reshape(CLIPS, per_clip * sub_rows, head_dim)
    query_block_rows = min(512, per_clip * sub_rows)
    score_scale = head_dim ** (-0.5)

    def attend(clip_index):
        key_block = lax.dynamic_slice_in_dim(key_rows, clip_index * per_clip, per_clip, 1).reshape(
            -1, 2 * head_dim
        )
        visible = key_place < lax.dynamic_index_in_dim(patch_counts, clip_index, 0, keepdims=False)
        query_all = lax.dynamic_index_in_dim(clip_queries, clip_index, 0, keepdims=False)

        def one_block(query_block):
            scores = (
                lax.dot_general(
                    query_block,
                    key_block[:, :head_dim],
                    (((1,), (1,)), ((), ())),
                    preferred_element_type=jnp.float32,
                )
                * score_scale
            )
            scores = jnp.where(visible[None, :], scores, -jnp.inf)
            highest = jnp.max(scores, axis=1, keepdims=True)
            weights = jnp.exp(scores - highest)
            running = jnp.sum(weights, axis=1, keepdims=True)
            mixture = jnp.dot(
                weights.astype(jnp.bfloat16),
                key_block[:, head_dim:],
                preferred_element_type=jnp.float32,
            )
            return (mixture / running).astype(jnp.bfloat16)

        return lax.map(one_block, query_all.reshape(-1, query_block_rows, head_dim)).reshape(
            -1, head_dim
        )

    attended = lax.map(attend, jnp.arange(CLIPS, dtype=jnp.int32))
    returned = lax.all_to_all(
        attended.reshape(devices, sub_rows, head_dim),
        "wide",
        split_axis=0,
        concat_axis=0,
        tiled=True,
    )
    attention = (
        returned.reshape(HEADS, groups, sub_rows, head_dim)
        .transpose(1, 2, 0, 3)
        .reshape(local_rows, vit_width)
    )
    projected = jnp.dot(attention, w_out, preferred_element_type=jnp.float32).astype(jnp.bfloat16)
    merged = projected.reshape(local_rows // 4, 4 * vit_width).astype(jnp.float32)
    centre = jnp.mean(merged, axis=1, keepdims=True)
    centered = merged - centre
    spread = jnp.mean(centered * centered, axis=1, keepdims=True)
    normed = (centered * lax.rsqrt(spread + norm_eps) * ln_gain + ln_bias).astype(jnp.bfloat16)
    tok_groups = min(8, devices)
    feat_groups = devices // tok_groups
    merge_rows = w_merge
    for bit_index in range(tok_groups.bit_length() - 1):
        partner = swapped(merge_rows, "wide", bit_index)
        upper_bit = position_self // (1 << bit_index) % 2
        merge_rows = ordered_pair(merge_rows, partner, upper_bit)
    token_count = normed.shape[0]
    part_rows = token_count // tok_groups
    feat_width = normed.shape[1] // feat_groups
    out_width = w_merge.shape[1]
    merge_send = (
        normed.reshape(tok_groups, part_rows, feat_groups, feat_width)
        .transpose(2, 0, 1, 3)
        .reshape(devices, part_rows, feat_width)
    )
    flat_rows = lax.all_to_all(merge_send, "wide", split_axis=0, concat_axis=0, tiled=True).reshape(
        -1, feat_width
    )
    partial_value = jnp.dot(flat_rows, merge_rows, preferred_element_type=jnp.float32).reshape(
        devices, -1, out_width
    )
    summed = lax.all_to_all(partial_value, "wide", split_axis=0, concat_axis=0, tiled=True)
    tokens = (
        jnp.sum(summed.reshape(feat_groups, tok_groups, part_rows, out_width), axis=0)
        .reshape(token_count, out_width)
        .astype(jnp.bfloat16)
    )
    logits = jnp.dot(tokens, w_router, preferred_element_type=jnp.float32)
    experts = w_router.shape[1]
    top_count = expert_ids.shape[1]
    matches = expert_ids[:, :, None] == jnp.arange(experts, dtype=jnp.int32)[None, None, :]
    chosen = jnp.sum(jnp.where(matches, logits[:, None, :], 0.0), axis=2)
    gate_values = jax.nn.sigmoid(chosen)
    route_weight = route_scale * gate_values / jnp.sum(gate_values, axis=1, keepdims=True)
    capacity = min(token_count, 2 * token_count * top_count // experts)
    slot_count = experts * capacity
    target = expert_ids * capacity + slot_pos
    one_hot = jnp.any(
        target[None, :, :] == jnp.arange(slot_count, dtype=jnp.int32)[:, None, None], axis=2
    ).astype(jnp.bfloat16)
    buffer = jnp.dot(one_hot, tokens, preferred_element_type=jnp.float32).astype(jnp.bfloat16)
    gate_half = w_gate[0]
    up_half = w_up[0]
    down_half = w_down[0]
    half_cap = capacity // 2
    dispatch = buffer.reshape(devices, half_cap, out_width)
    portion = lax.all_to_all(dispatch, "wide", split_axis=0, concat_axis=0, tiled=True)
    item_count = portion.shape[1]
    partner_rows = swapped(portion, "wide", 0)
    both_rows = jnp.concatenate([portion, partner_rows], axis=1)
    flat_rows = both_rows.reshape(-1, out_width)
    gate_part = jnp.dot(flat_rows, gate_half, preferred_element_type=jnp.float32)
    up_part = jnp.dot(flat_rows, up_half, preferred_element_type=jnp.float32)
    hidden = (jax.nn.silu(gate_part) * up_part).astype(jnp.bfloat16)
    product = (
        jnp.dot(hidden, down_half, preferred_element_type=jnp.float32)
        .astype(jnp.bfloat16)
        .reshape(devices, 2 * item_count, out_width)
    )
    from_partner = swapped(product[:, item_count:], "wide", 0)
    joined = (
        product[:, :item_count].astype(jnp.float32) + from_partner.astype(jnp.float32)
    ).astype(jnp.bfloat16)
    answers = lax.all_to_all(joined, "wide", split_axis=0, concat_axis=0, tiled=True)
    slot_result = answers.reshape(slot_count, out_width)
    slot_result = lax.optimization_barrier(slot_result)
    picked = jnp.take(slot_result, target.reshape(-1), axis=0).reshape(
        token_count, top_count, out_width
    )
    return jnp.sum(picked.astype(jnp.float32) * route_weight[:, :, None], axis=1).astype(
        jnp.bfloat16
    )


BF = jnp.bfloat16
F32 = jnp.float32
VMEM = pl.BlockSpec(memory_space=pltpu.VMEM)
SMEM = pl.BlockSpec(memory_space=pltpu.SMEM)
HBM = pl.BlockSpec(memory_space=pltpu.HBM)
LANES = 128
MASKED = -1e30
LOG2E = 1.4426950408889634


def params(mib):
    return pltpu.CompilerParams(vmem_limit_bytes=mib * 2**20)


def cost(flops, size, exps=0):
    return pl.CostEstimate(flops=flops, bytes_accessed=size, transcendentals=exps)


def flipped(number, bits):
    low = (number % 2 + bits % 2) % 2
    return 2 * ((number // 2 + bits // 2) % 2) + low


def pieces(value, count):
    out = []
    for _ in range(count):
        piece = value.astype(BF).astype(F32)
        out.append(piece)
        value = value - piece
    return out


def pack_kernel(qkv_ref, out_ref):
    rows, width = qkv_ref.shape
    tokens = rows // 4
    peers, parts, _ = out_ref.shape
    source = lax.broadcasted_iota(jnp.int32, (rows, rows), 0)
    place = lax.broadcasted_iota(jnp.int32, (rows, rows), 1)
    order = jnp.where(source == 4 * (place % tokens) + place // tokens, 1.0, 0.0).astype(BF)
    part = parts // 3
    third = width // 3
    for kind in range(3):
        turned = lax.dot_general(
            qkv_ref[:, kind * third : (kind + 1) * third],
            order,
            (((0,), (0,)), ((), ())),
            preferred_element_type=F32,
        ).astype(BF)
        for peer in range(peers):
            out_ref[peer, kind * part : (kind + 1) * part, :] = turned[peer * part : (peer + 1) * part]


def share_kernel(merge_ref, common_ref, share_ref, sems):
    common, share = common_ref.shape[0], share_ref.shape[0]
    spot = pl.multiple_of(common + share * lax.axis_index("grp"), 16)
    copies = [
        pltpu.make_async_copy(merge_ref.at[pl.ds(spot, share), :], share_ref, sems.at[0]),
        pltpu.make_async_copy(merge_ref.at[pl.ds(0, common), :], common_ref, sems.at[1]),
    ]
    for copy in copies:
        copy.start()
    for copy in copies:
        copy.wait()


def attend_kernel(x_ref, grid_ref, out_ref):
    peers, parts, lanes = x_ref.shape
    part = parts // 3
    dim = part // 2
    quarters = 4
    sides = peers // quarters
    tokens = lanes // 4
    clip = lax.axis_index("wide") // peers
    count = grid_ref[clip, 0] * grid_ref[clip, 1]
    factor = dim ** (-0.5) * LOG2E
    keys = jnp.concatenate([x_ref[s, part : 2 * part, :] for s in range(peers)], 1)
    lane = lax.broadcasted_iota(jnp.int32, (16, peers * lanes), 1)
    row = lax.broadcasted_iota(jnp.int32, (16, peers * lanes), 0)
    inner = lane % lanes
    place = lane // lanes * lanes + 4 * (inner % tokens) + inner // tokens
    hidden = jnp.where((row == 0) & (place >= count), MASKED, 0.0).astype(BF)
    keys = jnp.concatenate([keys, hidden], 0).T
    values = jnp.concatenate([x_ref[s, 2 * part :, :] for s in range(peers)], 1).astype(F32)
    values = [values[:dim].astype(BF), values[dim:].astype(BF)]
    ones = jnp.where(lax.broadcasted_iota(jnp.int32, (16, sides * lanes), 0) == 0, 1.0, 0.0).astype(BF)
    head_row = lax.broadcasted_iota(jnp.int32, (part, sides * lanes), 0) // dim
    group = lax.broadcasted_iota(jnp.int32, (dim, lanes), 1) // tokens
    for quarter in range(quarters):
        query = jnp.concatenate(
            [x_ref[quarter + quarters * s, :part, :] for s in range(sides)], 1
        ).astype(F32)
        mixed = []
        for head in range(2):
            own = jnp.concatenate([jnp.where(head_row == head, query, 0.0).astype(BF), ones], 0)
            scores = jnp.dot(keys, own, preferred_element_type=F32)
            highest = jnp.max(scores, axis=0, keepdims=True)
            weights = jnp.exp2((scores - highest) * factor)
            total = jnp.sum(weights, axis=0, keepdims=True)
            value = jnp.dot(values[head], weights.astype(BF), preferred_element_type=F32) / total
            mixed += [value[:, s * lanes : (s + 1) * lanes] for s in range(sides)]
        for position in range(4):
            block = mixed[position]
            for g in range(4):
                if g != position:
                    shift = (g - position) * tokens % lanes
                    block = jnp.where(group == g, pltpu.roll(mixed[g], shift, 1), block)
            out_ref[quarters * position + quarter] = block.astype(BF)


def merge_kernel(
    x_ref, w_out_hbm, gain_ref, bias_ref, *refs
):
    w0, w1, *rest, out_ref, att_ref, w_ref, w_out_ref, sems = refs
    me, group = lax.axis_index("wide"), lax.axis_index("grp")
    position, quarter = me // 4, me % 4
    blocks, dim, lanes = x_ref.shape
    pairs = blocks // 2
    depth = w0.shape[0]
    out_width = w0.shape[1]
    width = w_out_ref.shape[1]
    first_copy = pltpu.make_async_copy(w_out_hbm, w_out_ref, sems.at[8])
    first_copy.start()
    copies = []
    common, share = rest[0].shape[0], rest[1].shape[0]
    places = [(w0, 0, 0), (w1, 1, 0)]
    for k in (2, 3):
        both, mine, theirs = rest[3 * (k - 2) : 3 * (k - 1)]
        places += [(both, k, 0), (mine, k, common + share * group), (theirs, k, common + share * (1 - group))]
    for n, (source, k, first) in enumerate(places):
        spot = pl.multiple_of(flipped(quarter, k) * depth + first, 16)
        copies.append(pltpu.make_async_copy(source, w_ref.at[pl.ds(spot, source.shape[0]), :], sems.at[n]))
        copies[-1].start()
    left = lax.broadcasted_iota(jnp.int32, (dim, lanes), 1) < lanes // 2
    for pair in range(pairs):
        first, second = x_ref[pair].astype(F32), x_ref[pairs + pair].astype(F32)
        upper = jnp.where(left, first, pltpu.roll(second, lanes // 2, 1))
        lower = jnp.where(left, pltpu.roll(first, lanes // 2, 1), second)
        att_ref[2 * dim * pair : 2 * dim * (pair + 1), :] = jnp.concatenate([upper, lower], 0).astype(BF)
    first_copy.wait()
    mixed = lax.dot_general(
        att_ref[...], w_out_ref[...], (((0,), (0,)), ((), ())), preferred_element_type=F32
    )
    mixed = mixed.astype(BF).astype(F32)
    centre = jnp.sum(mixed, axis=1, keepdims=True) / width
    centered = mixed - centre
    square = jnp.sum(centered * centered, axis=1, keepdims=True)
    here = pl.ds(pl.multiple_of(position * width, LANES), width)
    gain, bias = gain_ref[:, here], bias_ref[:, here]
    row = lax.broadcasted_iota(jnp.int32, (16, width), 0)
    extra = jnp.zeros((16, width), F32)
    for k, line in enumerate(pieces(gain, 2) + pieces(bias, 2)):
        extra = jnp.where(row == k, line, extra)
    left_side = jnp.concatenate([(centered * gain).astype(BF), extra.astype(BF)], 0)
    lane = lax.broadcasted_iota(jnp.int32, (lanes, LANES), 1)
    stats = jnp.zeros((lanes, LANES), F32)
    for k, column in enumerate(pieces(centre, 3) + pieces(square, 3)):
        stats = jnp.where(lane == k, column, stats)
    stats = stats.astype(BF)
    for copy in copies:
        copy.wait()
    planes, tokens, _ = out_ref.shape
    half = tokens // 2
    step = 2 * LANES
    shared = [None] * tokens
    for begin in range(0, out_width, step):
        part = jnp.dot(left_side, w_ref[:, begin : begin + step], preferred_element_type=F32)
        for plane in range(planes):
            out_ref[flipped(position, plane), :, begin : begin + step] = part[plane * tokens : (plane + 1) * tokens].astype(BF)
        scale = part[lanes : lanes + 1] + part[lanes + 1 : lanes + 2]
        shift = part[lanes + 2 : lanes + 3] + part[lanes + 3 : lanes + 4]
        for k in range(step // LANES):
            shared[begin // LANES + k] = scale[:, k * LANES : (k + 1) * LANES]
            shared[half + begin // LANES + k] = shift[:, k * LANES : (k + 1) * LANES]
    shared = jnp.concatenate(shared, 0).astype(BF)
    for plane in range(planes):
        out_ref[flipped(position, plane), :, out_width : out_width + LANES] = shared
        out_ref[flipped(position, plane), :, out_width + LANES :] = stats[plane * tokens : (plane + 1) * tokens]


def route_kernel(x0, x1, x2, x3, router_ref, ids_ref, out_ref, *, merge_width, experts):
    blocks = (x0, x1, x2, x3)
    planes, tokens = len(blocks), x0.shape[0]
    out_width = out_ref.shape[1] - LANES
    half = tokens // 2
    stats = [blocks[p][:, out_width + LANES :].astype(F32) for p in range(planes)]
    shared = [blocks[p][:, out_width : out_width + LANES].astype(F32) for p in range(planes)]
    centres = [s[:, 0:1] + s[:, 1:2] + s[:, 2:3] for s in stats]
    squares = [s[:, 3:4] + s[:, 4:5] + s[:, 5:6] for s in stats]
    mean = sum(centres) / planes
    offsets = [c - mean for c in centres]
    spread = sum(q + (merge_width // planes) * (o * o) for q, o in zip(squares, offsets)) / merge_width
    inverse = lax.rsqrt(spread + norm_eps)
    bias = sum(shared)
    for k in range(out_width // LANES):
        cut = slice(k * LANES, (k + 1) * LANES)
        total = sum(blocks[p][:, cut].astype(F32) for p in range(planes))
        total += sum(offsets[p] * shared[p][k : k + 1] for p in range(planes))
        out_ref[:, cut] = (total * inverse + bias[half + k : half + k + 1]).astype(BF)
    logits = jnp.dot(out_ref[:, :out_width], router_ref[...], preferred_element_type=F32)
    lane = lax.broadcasted_iota(jnp.int32, (tokens, LANES), 1)
    expert = lane % experts
    chosen = lane < 0
    for k in range(ids_ref.shape[1]):
        chosen = chosen | (ids_ref[:, k : k + 1] == expert)
    gates = jnp.where(chosen & (lane < 2 * experts), 1.0 / (1.0 + jnp.exp(-logits)), 0.0)
    total = jnp.sum(jnp.where(lane < experts, gates, 0.0), axis=1, keepdims=True)
    weight = route_scale * gates / total
    high, low = pieces(weight, 2)
    out_ref[:, out_width:] = jnp.where(lane < experts, high, low).astype(BF)


def expert_kernel(*refs, experts, cuts):
    *blocks, gate_hbm, up_hbm, down_hbm, own_ref, other_ref, x_ref, gate_ref, up_ref, down_ref, sems = refs
    tokens, width = own_ref.shape[1:]
    half = len(blocks) // 2
    copies = []
    for k, cut in enumerate(cuts):
        for kind, source, target in ((0, gate_hbm, gate_ref), (1, up_hbm, up_ref)):
            copies.append(pltpu.make_async_copy(source.at[0, cut, :], target.at[cut, :], sems.at[2 * k + kind]))
            copies[-1].start()
    last = pltpu.make_async_copy(down_hbm.at[0], down_ref, sems.at[2 * len(cuts)])
    last.start()
    expert = lax.axis_index("wide") // 2
    lane = lax.broadcasted_iota(jnp.int32, (tokens, LANES), 1)
    weights = []
    for k, block in enumerate(blocks):
        x_ref[k * tokens : (k + 1) * tokens, :] = block[:, :width]
        picked = (lane == expert) | (lane == expert + experts)
        picked = jnp.where(picked, block[:, width:].astype(F32), 0.0)
        weights.append(jnp.sum(picked, axis=1, keepdims=True))
    inputs = x_ref[...]
    turned = (((1,), (1,)), ((), ()))
    hidden = []
    for k, cut in enumerate(cuts):
        copies[2 * k].wait()
        gate = lax.dot_general(inputs, gate_ref[cut, :], turned, preferred_element_type=F32)
        copies[2 * k + 1].wait()
        up = lax.dot_general(inputs, up_ref[cut, :], turned, preferred_element_type=F32)
        hidden.append((gate / (1.0 + jnp.exp(-gate)) * up).astype(BF))
    hidden = jnp.concatenate(hidden, 1)
    last.wait()
    step = 4 * LANES
    for begin in range(0, width, step):
        product = jnp.dot(hidden, down_ref[:, begin : begin + step], preferred_element_type=F32)
        for k in range(len(blocks)):
            value = (product[k * tokens : (k + 1) * tokens] * weights[k]).astype(BF)
            out_ref = own_ref if k < half else other_ref
            out_ref[k % half, :, begin : begin + step] = value


def crossed(value, mask):
    pairs = [(source, source ^ mask) for source in range(lax.axis_size("wide"))]
    return lax.ppermute(value, "wide", pairs)


def local(
    qkv, grid, w_out, ln_gain, ln_bias, w_merge, w_router, expert_ids, slot_pos, w_gate, w_up, w_down
):
    devices = lax.axis_size("wide")
    rows = qkv.shape[0]
    vit_width = w_out.shape[0]
    experts = w_router.shape[1]
    out_width = w_merge.shape[1]
    tokens = rows // 4
    peers = devices // CLIPS
    suits = (
        devices == HEADS
        and peers == 8
        and rows == LANES
        and devices == 2 * experts
        and 2 * out_width == tokens * LANES
        and 4 * w_merge.shape[0] == vit_width
        and lax.axis_size("grp") == 2
        and w_merge.shape[0] % 32 == 0
    )
    if not suits:
        return general(
            qkv, grid, w_out, ln_gain, ln_bias, w_merge, w_router, expert_ids, slot_pos, w_gate, w_up, w_down
        )
    part = vit_width // peers
    dim = vit_width // HEADS
    depth = w_merge.shape[0]
    share = depth // 64 * 16
    packed = pl.pallas_call(
        pack_kernel,
        out_shape=jax.ShapeDtypeStruct((peers, 3 * part, rows), BF),
        in_specs=[VMEM],
        out_specs=VMEM,
        compiler_params=params(8),
    )(qkv)
    common, shared = pl.pallas_call(
        share_kernel,
        out_shape=[
            jax.ShapeDtypeStruct((depth - 2 * share, out_width), BF),
            jax.ShapeDtypeStruct((share, out_width), BF),
        ],
        in_specs=[HBM],
        out_specs=[VMEM] * 2,
        scratch_shapes=[pltpu.SemaphoreType.DMA((2,))],
        compiler_params=params(8),
        cost_estimate=cost(2**31, 2**24),
    )(w_merge)
    clips = [[c * peers + i for i in range(peers)] for c in range(CLIPS)]
    gathered = lax.all_to_all(
        packed, "wide", split_axis=0, concat_axis=0, tiled=True, axis_index_groups=clips
    )
    gathered, common, shared, held = lax.optimization_barrier((gathered, common, shared, w_merge))
    mine_y = crossed(shared, 2)
    common_y = crossed(common, 2)
    attended = pl.pallas_call(
        attend_kernel,
        out_shape=jax.ShapeDtypeStruct((devices, dim, rows), BF),
        in_specs=[VMEM, SMEM],
        out_specs=VMEM,
        compiler_params=params(20),
        cost_estimate=cost(2**32, 2**22, 2**21),
    )(gathered, grid)
    held_c = crossed(held, 1)
    attended, mine_y = lax.optimization_barrier((attended, mine_y))
    theirs_y = lax.ppermute(mine_y, "grp", [(0, 1), (1, 0)])
    mine_yc = crossed(mine_y, 1)
    returned = lax.all_to_all(attended, "wide", split_axis=0, concat_axis=0, tiled=True)
    returned, common_y, theirs_y = lax.optimization_barrier((returned, common_y, theirs_y))
    common_yc, theirs_yc = crossed(common_y, 1), crossed(theirs_y, 1)
    planes = devices // 4
    message = out_width + 2 * LANES
    partial = pl.pallas_call(
        merge_kernel,
        out_shape=jax.ShapeDtypeStruct((planes, tokens, message), BF),
        in_specs=[VMEM, HBM, VMEM, VMEM] + [pl.BlockSpec(memory_space=pl.ANY)] * 8,
        out_specs=VMEM,
        scratch_shapes=[
            pltpu.VMEM((vit_width, rows), BF),
            pltpu.VMEM((vit_width, out_width), BF),
            pltpu.VMEM((vit_width, vit_width), BF),
            pltpu.SemaphoreType.DMA((9,)),
        ],
        compiler_params=params(50),
    )(
        returned,
        w_out,
        ln_gain.reshape(1, 4 * vit_width),
        ln_bias.reshape(1, 4 * vit_width),
        w_merge,
        held_c,
        common_y,
        mine_y,
        theirs_y,
        common_yc,
        mine_yc,
        theirs_yc,
    )
    along = (8, 12, 4)
    arrived = [partial[0]] + [crossed(partial[mask // 4], mask) for mask in along]
    router = jnp.concatenate(
        [w_router, w_router, jnp.zeros((out_width, LANES - 2 * experts), BF)], 1
    )
    routed = pl.pallas_call(
        lambda *refs: route_kernel(*refs, merge_width=4 * vit_width, experts=experts),
        out_shape=jax.ShapeDtypeStruct((tokens, out_width + LANES), BF),
        in_specs=[VMEM] * 6,
        out_specs=VMEM,
        compiler_params=params(6),
    )(*arrived, router, expert_ids)
    near = [routed] + [crossed(routed, mask) for mask in along]
    far = [crossed(block, 2) for block in near]
    *near, far[0] = lax.optimization_barrier((*near, far[0]))
    gate_turned, up_turned = jnp.swapaxes(w_gate, 1, 2), jnp.swapaxes(w_up, 1, 2)

    inner = w_down.shape[1]
    cuts = [slice(k, min(k + 2 * LANES, inner)) for k in range(0, inner, 2 * LANES)]

    def experts_of(blocks):
        return pl.pallas_call(
            lambda *refs: expert_kernel(*refs, experts=experts, cuts=cuts),
            out_shape=[jax.ShapeDtypeStruct((planes, tokens, out_width), BF)] * 2,
            in_specs=[VMEM] * (2 * planes) + [HBM] * 3,
            out_specs=[VMEM, VMEM],
            scratch_shapes=[
                pltpu.VMEM((2 * planes * tokens, out_width), BF),
                pltpu.VMEM((inner, out_width), BF),
                pltpu.VMEM((inner, out_width), BF),
                pltpu.VMEM((inner, out_width), BF),
                pltpu.SemaphoreType.DMA((2 * len(cuts) + 1,)),
            ],
            compiler_params=params(50),
            cost_estimate=cost(2**32, 2**24),
        )(*blocks, *[crossed(block, 1) for block in blocks], gate_turned, up_turned, w_down)

    def scattered(blocks):
        others = [crossed(blocks[1 + along.index(mask)], mask) for mask in along]
        return blocks[0].astype(F32) + sum(block.astype(F32) for block in others)

    def paired(own, other):
        return (own.astype(F32) + crossed(other, 1).astype(F32)).astype(BF)

    near_own, near_other = experts_of(near)
    *far, near_own, near_other = lax.optimization_barrier((*far, near_own, near_other))
    far_own, far_other = experts_of(far)
    near_sum = scattered(paired(near_own, near_other))
    far_out, near_sum = lax.optimization_barrier((paired(far_own, far_other), near_sum))
    across = [crossed(far_out[k], 2 + mask) for k, mask in enumerate(along, 1)]
    across.append(crossed(far_out[0], 2))
    return (near_sum + sum(block.astype(F32) for block in across)).astype(BF)


def solution(mesh):
    placed = (
        P(("grp", "wide"), None),
        P("grp", None),
        P(),
        P(),
        P(),
        P("wide", None),
        P(),
        P(("grp", "wide"), None),
        P(("grp", "wide"), None),
        P("wide", None, None),
        P("wide", None, None),
        P("wide", None, None),
    )
    return jax.shard_map(
        local, mesh=mesh, in_specs=placed, out_specs=P(("grp", "wide"), None), check_vma=False
    )
```

```python
import jax
import jax.numpy as jnp
from jax import lax
from jax.experimental import pallas as pl
from jax.experimental.pallas import tpu as pltpu
from jax.sharding import PartitionSpec as P

HEADS = 16
CLIPS = 2


route_scale = 2.446
norm_eps = 1e-05


def swapped(value, axis, stride):
    mask = 2**stride
    pairs = [(source, source ^ mask) for source in range(lax.axis_size(axis))]
    return lax.ppermute(value, axis, pairs)


def ordered_pair(own_part, partner, upper_bit):
    return jnp.where(
        upper_bit == 1,
        jnp.concatenate([partner, own_part], 0),
        jnp.concatenate([own_part, partner], 0),
    )


def general(
    qkv,
    grid,
    w_out,
    ln_gain,
    ln_bias,
    w_merge,
    w_router,
    expert_ids,
    slot_pos,
    w_gate,
    w_up,
    w_down,
):
    devices = lax.axis_size("wide")
    position_self = lax.axis_index("wide")
    vit_width = w_out.shape[0]
    head_dim = vit_width // HEADS
    groups = devices // HEADS
    local_rows = qkv.shape[0]
    sub_rows = local_rows // groups
    per_clip = devices // CLIPS
    query_send = (
        qkv[:, :vit_width]
        .reshape(groups, sub_rows, HEADS, head_dim)
        .transpose(2, 0, 1, 3)
        .reshape(devices, sub_rows, head_dim)
    )
    key_value = jnp.concatenate(
        [
            qkv[:, vit_width : 2 * vit_width].reshape(local_rows, HEADS, head_dim),
            qkv[:, 2 * vit_width :].reshape(local_rows, HEADS, head_dim),
        ],
        axis=2,
    )
    spread_send = jnp.broadcast_to(
        key_value.transpose(1, 0, 2)[:, None], (HEADS, groups, local_rows, 2 * head_dim)
    ).reshape(devices, local_rows, 2 * head_dim)
    queries, key_rows = (
        lax.all_to_all(query_send, "wide", split_axis=0, concat_axis=0, tiled=True),
        lax.all_to_all(spread_send, "wide", split_axis=0, concat_axis=0, tiled=True),
    )
    key_rows = key_rows[None]
    key_groups = key_rows.shape[0]
    key_count = key_rows.shape[2]
    key_place = (
        jnp.arange(per_clip, dtype=jnp.int32)[None, :, None] * local_rows
        + jnp.arange(key_groups, dtype=jnp.int32)[:, None, None] * local_rows
        + jnp.arange(key_count, dtype=jnp.int32)[None, None, :]
    ).reshape(-1)
    patch_counts = grid[:, 0] * grid[:, 1]
    clip_queries = queries.reshape(CLIPS, per_clip * sub_rows, head_dim)
    query_block_rows = min(512, per_clip * sub_rows)
    score_scale = head_dim ** (-0.5)

    def attend(clip_index):
        key_block = lax.dynamic_slice_in_dim(key_rows, clip_index * per_clip, per_clip, 1).reshape(
            -1, 2 * head_dim
        )
        visible = key_place < lax.dynamic_index_in_dim(patch_counts, clip_index, 0, keepdims=False)
        query_all = lax.dynamic_index_in_dim(clip_queries, clip_index, 0, keepdims=False)

        def one_block(query_block):
            scores = (
                lax.dot_general(
                    query_block,
                    key_block[:, :head_dim],
                    (((1,), (1,)), ((), ())),
                    preferred_element_type=jnp.float32,
                )
                * score_scale
            )
            scores = jnp.where(visible[None, :], scores, -jnp.inf)
            highest = jnp.max(scores, axis=1, keepdims=True)
            weights = jnp.exp(scores - highest)
            running = jnp.sum(weights, axis=1, keepdims=True)
            mixture = jnp.dot(
                weights.astype(jnp.bfloat16),
                key_block[:, head_dim:],
                preferred_element_type=jnp.float32,
            )
            return (mixture / running).astype(jnp.bfloat16)

        return lax.map(one_block, query_all.reshape(-1, query_block_rows, head_dim)).reshape(
            -1, head_dim
        )

    attended = lax.map(attend, jnp.arange(CLIPS, dtype=jnp.int32))
    returned = lax.all_to_all(
        attended.reshape(devices, sub_rows, head_dim),
        "wide",
        split_axis=0,
        concat_axis=0,
        tiled=True,
    )
    attention = (
        returned.reshape(HEADS, groups, sub_rows, head_dim)
        .transpose(1, 2, 0, 3)
        .reshape(local_rows, vit_width)
    )
    projected = jnp.dot(attention, w_out, preferred_element_type=jnp.float32).astype(jnp.bfloat16)
    merged = projected.reshape(local_rows // 4, 4 * vit_width).astype(jnp.float32)
    centre = jnp.mean(merged, axis=1, keepdims=True)
    centered = merged - centre
    spread = jnp.mean(centered * centered, axis=1, keepdims=True)
    normed = (centered * lax.rsqrt(spread + norm_eps) * ln_gain + ln_bias).astype(jnp.bfloat16)
    tok_groups = min(8, devices)
    feat_groups = devices // tok_groups
    merge_rows = w_merge
    for bit_index in range(tok_groups.bit_length() - 1):
        partner = swapped(merge_rows, "wide", bit_index)
        upper_bit = position_self // (1 << bit_index) % 2
        merge_rows = ordered_pair(merge_rows, partner, upper_bit)
    token_count = normed.shape[0]
    part_rows = token_count // tok_groups
    feat_width = normed.shape[1] // feat_groups
    out_width = w_merge.shape[1]
    merge_send = (
        normed.reshape(tok_groups, part_rows, feat_groups, feat_width)
        .transpose(2, 0, 1, 3)
        .reshape(devices, part_rows, feat_width)
    )
    flat_rows = lax.all_to_all(merge_send, "wide", split_axis=0, concat_axis=0, tiled=True).reshape(
        -1, feat_width
    )
    partial_value = jnp.dot(flat_rows, merge_rows, preferred_element_type=jnp.float32).reshape(
        devices, -1, out_width
    )
    summed = lax.all_to_all(partial_value, "wide", split_axis=0, concat_axis=0, tiled=True)
    tokens = (
        jnp.sum(summed.reshape(feat_groups, tok_groups, part_rows, out_width), axis=0)
        .reshape(token_count, out_width)
        .astype(jnp.bfloat16)
    )
    logits = jnp.dot(tokens, w_router, preferred_element_type=jnp.float32)
    experts = w_router.shape[1]
    top_count = expert_ids.shape[1]
    matches = expert_ids[:, :, None] == jnp.arange(experts, dtype=jnp.int32)[None, None, :]
    chosen = jnp.sum(jnp.where(matches, logits[:, None, :], 0.0), axis=2)
    gate_values = jax.nn.sigmoid(chosen)
    route_weight = route_scale * gate_values / jnp.sum(gate_values, axis=1, keepdims=True)
    capacity = min(token_count, 2 * token_count * top_count // experts)
    slot_count = experts * capacity
    target = expert_ids * capacity + slot_pos
    one_hot = jnp.any(
        target[None, :, :] == jnp.arange(slot_count, dtype=jnp.int32)[:, None, None], axis=2
    ).astype(jnp.bfloat16)
    buffer = jnp.dot(one_hot, tokens, preferred_element_type=jnp.float32).astype(jnp.bfloat16)
    gate_half = w_gate[0]
    up_half = w_up[0]
    down_half = w_down[0]
    half_cap = capacity // 2
    dispatch = buffer.reshape(devices, half_cap, out_width)
    portion = lax.all_to_all(dispatch, "wide", split_axis=0, concat_axis=0, tiled=True)
    item_count = portion.shape[1]
    partner_rows = swapped(portion, "wide", 0)
    both_rows = jnp.concatenate([portion, partner_rows], axis=1)
    flat_rows = both_rows.reshape(-1, out_width)
    gate_part = jnp.dot(flat_rows, gate_half, preferred_element_type=jnp.float32)
    up_part = jnp.dot(flat_rows, up_half, preferred_element_type=jnp.float32)
    hidden = (jax.nn.silu(gate_part) * up_part).astype(jnp.bfloat16)
    product = (
        jnp.dot(hidden, down_half, preferred_element_type=jnp.float32)
        .astype(jnp.bfloat16)
        .reshape(devices, 2 * item_count, out_width)
    )
    from_partner = swapped(product[:, item_count:], "wide", 0)
    joined = (
        product[:, :item_count].astype(jnp.float32) + from_partner.astype(jnp.float32)
    ).astype(jnp.bfloat16)
    answers = lax.all_to_all(joined, "wide", split_axis=0, concat_axis=0, tiled=True)
    slot_result = answers.reshape(slot_count, out_width)
    slot_result = lax.optimization_barrier(slot_result)
    picked = jnp.take(slot_result, target.reshape(-1), axis=0).reshape(
        token_count, top_count, out_width
    )
    return jnp.sum(picked.astype(jnp.float32) * route_weight[:, :, None], axis=1).astype(
        jnp.bfloat16
    )


BF = jnp.bfloat16
F32 = jnp.float32
VMEM = pl.BlockSpec(memory_space=pltpu.VMEM)
SMEM = pl.BlockSpec(memory_space=pltpu.SMEM)
HBM = pl.BlockSpec(memory_space=pltpu.HBM)
LANES = 128
MASKED = -1e30
LOG2E = 1.4426950408889634


def params(mib):
    return pltpu.CompilerParams(vmem_limit_bytes=mib * 2**20)


def cost(flops, size, exps=0):
    return pl.CostEstimate(flops=flops, bytes_accessed=size, transcendentals=exps)


def flipped(number, bits):
    low = (number % 2 + bits % 2) % 2
    return 2 * ((number // 2 + bits // 2) % 2) + low


def pieces(value, count):
    out = []
    for _ in range(count):
        piece = value.astype(BF).astype(F32)
        out.append(piece)
        value = value - piece
    return out


def pack_kernel(qkv_ref, out_ref):
    rows, width = qkv_ref.shape
    tokens = rows // 4
    peers, parts, _ = out_ref.shape
    source = lax.broadcasted_iota(jnp.int32, (rows, rows), 0)
    place = lax.broadcasted_iota(jnp.int32, (rows, rows), 1)
    order = jnp.where(source == 4 * (place % tokens) + place // tokens, 1.0, 0.0).astype(BF)
    part = parts // 3
    third = width // 3
    for kind in range(3):
        turned = lax.dot_general(
            qkv_ref[:, kind * third : (kind + 1) * third],
            order,
            (((0,), (0,)), ((), ())),
            preferred_element_type=F32,
        ).astype(BF)
        for peer in range(peers):
            out_ref[peer, kind * part : (kind + 1) * part, :] = turned[peer * part : (peer + 1) * part]


def share_kernel(merge_ref, common_ref, share_ref, sems):
    common, share = common_ref.shape[0], share_ref.shape[0]
    spot = pl.multiple_of(common + share * lax.axis_index("grp"), 16)
    copies = [
        pltpu.make_async_copy(merge_ref.at[pl.ds(spot, share), :], share_ref, sems.at[0]),
        pltpu.make_async_copy(merge_ref.at[pl.ds(0, common), :], common_ref, sems.at[1]),
    ]
    for copy in copies:
        copy.start()
    for copy in copies:
        copy.wait()


def attend_kernel(x_ref, grid_ref, out_ref):
    peers, parts, lanes = x_ref.shape
    part = parts // 3
    dim = part // 2
    quarters = 4
    sides = peers // quarters
    tokens = lanes // 4
    clip = lax.axis_index("wide") // peers
    count = grid_ref[clip, 0] * grid_ref[clip, 1]
    factor = dim ** (-0.5) * LOG2E
    keys = jnp.concatenate([x_ref[s, part : 2 * part, :] for s in range(peers)], 1)
    lane = lax.broadcasted_iota(jnp.int32, (16, peers * lanes), 1)
    row = lax.broadcasted_iota(jnp.int32, (16, peers * lanes), 0)
    inner = lane % lanes
    place = lane // lanes * lanes + 4 * (inner % tokens) + inner // tokens
    hidden = jnp.where((row == 0) & (place >= count), MASKED, 0.0).astype(BF)
    keys = jnp.concatenate([keys, hidden], 0).T
    values = jnp.concatenate([x_ref[s, 2 * part :, :] for s in range(peers)], 1).astype(F32)
    values = [values[:dim].astype(BF), values[dim:].astype(BF)]
    ones = jnp.where(lax.broadcasted_iota(jnp.int32, (16, sides * lanes), 0) == 0, 1.0, 0.0).astype(BF)
    head_row = lax.broadcasted_iota(jnp.int32, (part, sides * lanes), 0) // dim
    group = lax.broadcasted_iota(jnp.int32, (dim, lanes), 1) // tokens
    def scores_of(item):
        quarter, head = item // 2, item % 2
        query = jnp.concatenate(
            [x_ref[quarter + quarters * s, :part, :] for s in range(sides)], 1
        ).astype(F32)
        own = jnp.concatenate([jnp.where(head_row == head, query, 0.0).astype(BF), ones], 0)
        return jnp.dot(keys, own, preferred_element_type=F32)

    scores = scores_of(0)
    for item in range(2 * quarters):
        quarter, head = item // 2, item % 2
        following = scores_of(item + 1) if item + 1 < 2 * quarters else None
        highest = jnp.max(scores, axis=0, keepdims=True)
        weights = jnp.exp2((scores - highest) * factor)
        total = jnp.sum(weights, axis=0, keepdims=True)
        value = jnp.dot(values[head], weights.astype(BF), preferred_element_type=F32) / total
        mixed = [] if head == 0 else mixed
        mixed += [value[:, s * lanes : (s + 1) * lanes] for s in range(sides)]
        scores = following
        if head == 0:
            continue
        for position in range(4):
            block = mixed[position]
            for g in range(4):
                if g != position:
                    shift = (g - position) * tokens % lanes
                    block = jnp.where(group == g, pltpu.roll(mixed[g], shift, 1), block)
            out_ref[quarters * position + quarter] = block.astype(BF)


def merge_kernel(
    x_ref, w_out_hbm, gain_ref, bias_ref, *refs
):
    w0, w1, *rest, out_ref, att_ref, w_ref, w_out_ref, sems = refs
    me, group = lax.axis_index("wide"), lax.axis_index("grp")
    position, quarter = me // 4, me % 4
    blocks, dim, lanes = x_ref.shape
    pairs = blocks // 2
    depth = w0.shape[0]
    out_width = w0.shape[1]
    width = w_out_ref.shape[1]
    first_copy = pltpu.make_async_copy(w_out_hbm, w_out_ref, sems.at[8])
    first_copy.start()
    copies = []
    common, share = rest[0].shape[0], rest[1].shape[0]
    places = [(w0, 0, 0), (w1, 1, 0)]
    for k in (2, 3):
        both, mine, theirs = rest[3 * (k - 2) : 3 * (k - 1)]
        places += [(both, k, 0), (mine, k, common + share * group), (theirs, k, common + share * (1 - group))]
    for n, (source, k, first) in enumerate(places):
        spot = pl.multiple_of(flipped(quarter, k) * depth + first, 16)
        copies.append(pltpu.make_async_copy(source, w_ref.at[pl.ds(spot, source.shape[0]), :], sems.at[n]))
        copies[-1].start()
    left = lax.broadcasted_iota(jnp.int32, (dim, lanes), 1) < lanes // 2
    for pair in range(pairs):
        first, second = x_ref[pair].astype(F32), x_ref[pairs + pair].astype(F32)
        upper = jnp.where(left, first, pltpu.roll(second, lanes // 2, 1))
        lower = jnp.where(left, pltpu.roll(first, lanes // 2, 1), second)
        att_ref[2 * dim * pair : 2 * dim * (pair + 1), :] = jnp.concatenate([upper, lower], 0).astype(BF)
    first_copy.wait()
    mixed = lax.dot_general(
        att_ref[...], w_out_ref[...], (((0,), (0,)), ((), ())), preferred_element_type=F32
    )
    mixed = mixed.astype(BF).astype(F32)
    centre = jnp.sum(mixed, axis=1, keepdims=True) / width
    centered = mixed - centre
    square = jnp.sum(centered * centered, axis=1, keepdims=True)
    here = pl.ds(pl.multiple_of(position * width, LANES), width)
    gain, bias = gain_ref[:, here], bias_ref[:, here]
    row = lax.broadcasted_iota(jnp.int32, (16, width), 0)
    extra = jnp.zeros((16, width), F32)
    for k, line in enumerate(pieces(gain, 2) + pieces(bias, 2)):
        extra = jnp.where(row == k, line, extra)
    left_side = jnp.concatenate([(centered * gain).astype(BF), extra.astype(BF)], 0)
    lane = lax.broadcasted_iota(jnp.int32, (lanes, LANES), 1)
    stats = jnp.zeros((lanes, LANES), F32)
    for k, column in enumerate(pieces(centre, 3) + pieces(square, 3)):
        stats = jnp.where(lane == k, column, stats)
    stats = stats.astype(BF)
    for copy in copies:
        copy.wait()
    planes, tokens, _ = out_ref.shape
    half = tokens // 2
    step = 2 * LANES
    shared = [None] * tokens
    for begin in range(0, out_width, step):
        part = jnp.dot(left_side, w_ref[:, begin : begin + step], preferred_element_type=F32)
        for plane in range(planes):
            out_ref[flipped(position, plane), :, begin : begin + step] = part[plane * tokens : (plane + 1) * tokens].astype(BF)
        scale = part[lanes : lanes + 1] + part[lanes + 1 : lanes + 2]
        shift = part[lanes + 2 : lanes + 3] + part[lanes + 3 : lanes + 4]
        for k in range(step // LANES):
            shared[begin // LANES + k] = scale[:, k * LANES : (k + 1) * LANES]
            shared[half + begin // LANES + k] = shift[:, k * LANES : (k + 1) * LANES]
    shared = jnp.concatenate(shared, 0).astype(BF)
    for plane in range(planes):
        out_ref[flipped(position, plane), :, out_width : out_width + LANES] = shared
        out_ref[flipped(position, plane), :, out_width + LANES :] = stats[plane * tokens : (plane + 1) * tokens]


def route_kernel(x0, x1, x2, x3, router_ref, ids_ref, out_ref, *, merge_width, experts):
    blocks = (x0, x1, x2, x3)
    planes, tokens = len(blocks), x0.shape[0]
    out_width = out_ref.shape[1] - LANES
    half = tokens // 2
    stats = [blocks[p][:, out_width + LANES :].astype(F32) for p in range(planes)]
    shared = [blocks[p][:, out_width : out_width + LANES].astype(F32) for p in range(planes)]
    centres = [s[:, 0:1] + s[:, 1:2] + s[:, 2:3] for s in stats]
    squares = [s[:, 3:4] + s[:, 4:5] + s[:, 5:6] for s in stats]
    mean = sum(centres) / planes
    offsets = [c - mean for c in centres]
    spread = sum(q + (merge_width // planes) * (o * o) for q, o in zip(squares, offsets)) / merge_width
    inverse = lax.rsqrt(spread + norm_eps)
    bias = sum(shared)
    for k in range(out_width // LANES):
        cut = slice(k * LANES, (k + 1) * LANES)
        total = sum(blocks[p][:, cut].astype(F32) for p in range(planes))
        total += sum(offsets[p] * shared[p][k : k + 1] for p in range(planes))
        out_ref[:, cut] = (total * inverse + bias[half + k : half + k + 1]).astype(BF)
    logits = jnp.dot(out_ref[:, :out_width], router_ref[...], preferred_element_type=F32)
    lane = lax.broadcasted_iota(jnp.int32, (tokens, LANES), 1)
    expert = lane % experts
    chosen = lane < 0
    for k in range(ids_ref.shape[1]):
        chosen = chosen | (ids_ref[:, k : k + 1] == expert)
    gates = jnp.where(chosen & (lane < 2 * experts), 1.0 / (1.0 + jnp.exp(-logits)), 0.0)
    total = jnp.sum(jnp.where(lane < experts, gates, 0.0), axis=1, keepdims=True)
    weight = route_scale * gates / total
    high, low = pieces(weight, 2)
    out_ref[:, out_width:] = jnp.where(lane < experts, high, low).astype(BF)


def expert_kernel(*refs, experts, cuts):
    *blocks, gate_hbm, up_hbm, down_hbm, own_ref, other_ref, x_ref, gate_ref, up_ref, down_ref, sems = refs
    tokens, width = own_ref.shape[1:]
    half = len(blocks) // 2
    copies = []
    for k, cut in enumerate(cuts):
        for kind, source, target in ((0, gate_hbm, gate_ref), (1, up_hbm, up_ref)):
            copies.append(pltpu.make_async_copy(source.at[0, cut, :], target.at[cut, :], sems.at[2 * k + kind]))
            copies[-1].start()
    last = pltpu.make_async_copy(down_hbm.at[0], down_ref, sems.at[2 * len(cuts)])
    last.start()
    expert = lax.axis_index("wide") // 2
    lane = lax.broadcasted_iota(jnp.int32, (tokens, LANES), 1)
    weights = []
    for k, block in enumerate(blocks):
        x_ref[k * tokens : (k + 1) * tokens, :] = block[:, :width]
        picked = (lane == expert) | (lane == expert + experts)
        picked = jnp.where(picked, block[:, width:].astype(F32), 0.0)
        weights.append(jnp.sum(picked, axis=1, keepdims=True))
    inputs = x_ref[...]
    turned = (((1,), (1,)), ((), ()))

    def gated(gate, up):
        return (gate / (1.0 + jnp.exp(-gate)) * up).astype(BF)

    hidden, earlier = [], None
    for k, cut in enumerate(cuts):
        copies[2 * k].wait()
        gate = lax.dot_general(inputs, gate_ref[cut, :], turned, preferred_element_type=F32)
        copies[2 * k + 1].wait()
        up = lax.dot_general(inputs, up_ref[cut, :], turned, preferred_element_type=F32)
        if earlier is not None:
            hidden.append(gated(*earlier))
        earlier = gate, up
    hidden = jnp.concatenate(hidden + [gated(*earlier)], 1)
    last.wait()
    step = 4 * LANES

    def product_of(begin):
        return jnp.dot(hidden, down_ref[:, begin : begin + step], preferred_element_type=F32)

    following = product_of(0)
    for begin in range(0, width, step):
        product = following
        following = product_of(begin + step) if begin + step < width else None
        for k in range(len(blocks)):
            value = (product[k * tokens : (k + 1) * tokens] * weights[k]).astype(BF)
            out_ref = own_ref if k < half else other_ref
            out_ref[k % half, :, begin : begin + step] = value


def crossed(value, mask):
    pairs = [(source, source ^ mask) for source in range(lax.axis_size("wide"))]
    return lax.ppermute(value, "wide", pairs)


def local(
    qkv, grid, w_out, ln_gain, ln_bias, w_merge, w_router, expert_ids, slot_pos, w_gate, w_up, w_down
):
    devices = lax.axis_size("wide")
    rows = qkv.shape[0]
    vit_width = w_out.shape[0]
    experts = w_router.shape[1]
    out_width = w_merge.shape[1]
    tokens = rows // 4
    peers = devices // CLIPS
    suits = (
        devices == HEADS
        and peers == 8
        and rows == LANES
        and devices == 2 * experts
        and 2 * out_width == tokens * LANES
        and 4 * w_merge.shape[0] == vit_width
        and lax.axis_size("grp") == 2
        and w_merge.shape[0] % 32 == 0
    )
    if not suits:
        return general(
            qkv, grid, w_out, ln_gain, ln_bias, w_merge, w_router, expert_ids, slot_pos, w_gate, w_up, w_down
        )
    part = vit_width // peers
    dim = vit_width // HEADS
    depth = w_merge.shape[0]
    share = depth // 64 * 16
    packed = pl.pallas_call(
        pack_kernel,
        out_shape=jax.ShapeDtypeStruct((peers, 3 * part, rows), BF),
        in_specs=[VMEM],
        out_specs=VMEM,
        compiler_params=params(8),
    )(qkv)
    common, shared = pl.pallas_call(
        share_kernel,
        out_shape=[
            jax.ShapeDtypeStruct((depth - 2 * share, out_width), BF),
            jax.ShapeDtypeStruct((share, out_width), BF),
        ],
        in_specs=[HBM],
        out_specs=[VMEM] * 2,
        scratch_shapes=[pltpu.SemaphoreType.DMA((2,))],
        compiler_params=params(8),
        cost_estimate=cost(2**31, 2**24),
    )(w_merge)
    clips = [[c * peers + i for i in range(peers)] for c in range(CLIPS)]
    gathered = lax.all_to_all(
        packed, "wide", split_axis=0, concat_axis=0, tiled=True, axis_index_groups=clips
    )
    gathered, common, shared, held = lax.optimization_barrier((gathered, common, shared, w_merge))
    mine_y = crossed(shared, 2)
    common_y = crossed(common, 2)
    attended = pl.pallas_call(
        attend_kernel,
        out_shape=jax.ShapeDtypeStruct((devices, dim, rows), BF),
        in_specs=[VMEM, SMEM],
        out_specs=VMEM,
        compiler_params=params(20),
        cost_estimate=cost(2**32, 2**22, 2**21),
    )(gathered, grid)
    held_c = crossed(held, 1)
    attended, mine_y = lax.optimization_barrier((attended, mine_y))
    theirs_y = lax.ppermute(mine_y, "grp", [(0, 1), (1, 0)])
    mine_yc = crossed(mine_y, 1)
    returned = lax.all_to_all(attended, "wide", split_axis=0, concat_axis=0, tiled=True)
    returned, common_y, theirs_y = lax.optimization_barrier((returned, common_y, theirs_y))
    common_yc, theirs_yc = crossed(common_y, 1), crossed(theirs_y, 1)
    planes = devices // 4
    message = out_width + 2 * LANES
    partial = pl.pallas_call(
        merge_kernel,
        out_shape=jax.ShapeDtypeStruct((planes, tokens, message), BF),
        in_specs=[VMEM, HBM, VMEM, VMEM] + [pl.BlockSpec(memory_space=pl.ANY)] * 8,
        out_specs=VMEM,
        scratch_shapes=[
            pltpu.VMEM((vit_width, rows), BF),
            pltpu.VMEM((vit_width, out_width), BF),
            pltpu.VMEM((vit_width, vit_width), BF),
            pltpu.SemaphoreType.DMA((9,)),
        ],
        compiler_params=params(50),
    )(
        returned,
        w_out,
        ln_gain.reshape(1, 4 * vit_width),
        ln_bias.reshape(1, 4 * vit_width),
        w_merge,
        held_c,
        common_y,
        mine_y,
        theirs_y,
        common_yc,
        mine_yc,
        theirs_yc,
    )
    along = (8, 12, 4)
    arrived = [partial[0]] + [crossed(partial[mask // 4], mask) for mask in along]
    router = jnp.concatenate(
        [w_router, w_router, jnp.zeros((out_width, LANES - 2 * experts), BF)], 1
    )
    routed = pl.pallas_call(
        lambda *refs: route_kernel(*refs, merge_width=4 * vit_width, experts=experts),
        out_shape=jax.ShapeDtypeStruct((tokens, out_width + LANES), BF),
        in_specs=[VMEM] * 6,
        out_specs=VMEM,
        compiler_params=params(6),
    )(*arrived, router, expert_ids)
    near = [routed] + [crossed(routed, mask) for mask in along]
    far = [crossed(block, 2) for block in near]
    *near, far[0] = lax.optimization_barrier((*near, far[0]))
    gate_turned, up_turned = jnp.swapaxes(w_gate, 1, 2), jnp.swapaxes(w_up, 1, 2)

    inner = w_down.shape[1]
    cuts = [slice(k, min(k + 2 * LANES, inner)) for k in range(0, inner, 2 * LANES)]

    def experts_of(blocks):
        return pl.pallas_call(
            lambda *refs: expert_kernel(*refs, experts=experts, cuts=cuts),
            out_shape=[jax.ShapeDtypeStruct((planes, tokens, out_width), BF)] * 2,
            in_specs=[VMEM] * (2 * planes) + [HBM] * 3,
            out_specs=[VMEM, VMEM],
            scratch_shapes=[
                pltpu.VMEM((2 * planes * tokens, out_width), BF),
                pltpu.VMEM((inner, out_width), BF),
                pltpu.VMEM((inner, out_width), BF),
                pltpu.VMEM((inner, out_width), BF),
                pltpu.SemaphoreType.DMA((2 * len(cuts) + 1,)),
            ],
            compiler_params=params(50),
            cost_estimate=cost(2**32, 2**24),
        )(*blocks, *[crossed(block, 1) for block in blocks], gate_turned, up_turned, w_down)

    def scattered(blocks):
        others = [crossed(blocks[1 + along.index(mask)], mask) for mask in along]
        return blocks[0].astype(F32) + sum(block.astype(F32) for block in others)

    def paired(own, other):
        return (own.astype(F32) + crossed(other, 1).astype(F32)).astype(BF)

    near_own, near_other = experts_of(near)
    *far, near_own, near_other = lax.optimization_barrier((*far, near_own, near_other))
    far_own, far_other = experts_of(far)
    near_sum = scattered(paired(near_own, near_other))
    far_out, near_sum = lax.optimization_barrier((paired(far_own, far_other), near_sum))
    across = [crossed(far_out[k], 2 + mask) for k, mask in enumerate(along, 1)]
    across.append(crossed(far_out[0], 2))
    return (near_sum + sum(block.astype(F32) for block in across)).astype(BF)


def solution(mesh):
    placed = (
        P(("grp", "wide"), None),
        P("grp", None),
        P(),
        P(),
        P(),
        P("wide", None),
        P(),
        P(("grp", "wide"), None),
        P(("grp", "wide"), None),
        P("wide", None, None),
        P("wide", None, None),
        P("wide", None, None),
    )
    return jax.shard_map(
        local, mesh=mesh, in_specs=placed, out_specs=P(("grp", "wide"), None), check_vma=False
    )
```

```python
import jax
import jax.numpy as jnp
from jax import lax
from jax.experimental import pallas as pl
from jax.experimental.pallas import tpu as pltpu
from jax.sharding import PartitionSpec as P

HEADS = 16
CLIPS = 2


route_scale = 2.446
norm_eps = 1e-05


def swapped(value, axis, stride):
    mask = 2**stride
    pairs = [(source, source ^ mask) for source in range(lax.axis_size(axis))]
    return lax.ppermute(value, axis, pairs)


def ordered_pair(own_part, partner, upper_bit):
    return jnp.where(
        upper_bit == 1,
        jnp.concatenate([partner, own_part], 0),
        jnp.concatenate([own_part, partner], 0),
    )


def general(
    qkv,
    grid,
    w_out,
    ln_gain,
    ln_bias,
    w_merge,
    w_router,
    expert_ids,
    slot_pos,
    w_gate,
    w_up,
    w_down,
):
    devices = lax.axis_size("wide")
    position_self = lax.axis_index("wide")
    vit_width = w_out.shape[0]
    head_dim = vit_width // HEADS
    groups = devices // HEADS
    local_rows = qkv.shape[0]
    sub_rows = local_rows // groups
    per_clip = devices // CLIPS
    query_send = (
        qkv[:, :vit_width]
        .reshape(groups, sub_rows, HEADS, head_dim)
        .transpose(2, 0, 1, 3)
        .reshape(devices, sub_rows, head_dim)
    )
    key_value = jnp.concatenate(
        [
            qkv[:, vit_width : 2 * vit_width].reshape(local_rows, HEADS, head_dim),
            qkv[:, 2 * vit_width :].reshape(local_rows, HEADS, head_dim),
        ],
        axis=2,
    )
    spread_send = jnp.broadcast_to(
        key_value.transpose(1, 0, 2)[:, None], (HEADS, groups, local_rows, 2 * head_dim)
    ).reshape(devices, local_rows, 2 * head_dim)
    queries, key_rows = (
        lax.all_to_all(query_send, "wide", split_axis=0, concat_axis=0, tiled=True),
        lax.all_to_all(spread_send, "wide", split_axis=0, concat_axis=0, tiled=True),
    )
    key_rows = key_rows[None]
    key_groups = key_rows.shape[0]
    key_count = key_rows.shape[2]
    key_place = (
        jnp.arange(per_clip, dtype=jnp.int32)[None, :, None] * local_rows
        + jnp.arange(key_groups, dtype=jnp.int32)[:, None, None] * local_rows
        + jnp.arange(key_count, dtype=jnp.int32)[None, None, :]
    ).reshape(-1)
    patch_counts = grid[:, 0] * grid[:, 1]
    clip_queries = queries.reshape(CLIPS, per_clip * sub_rows, head_dim)
    query_block_rows = min(512, per_clip * sub_rows)
    score_scale = head_dim ** (-0.5)

    def attend(clip_index):
        key_block = lax.dynamic_slice_in_dim(key_rows, clip_index * per_clip, per_clip, 1).reshape(
            -1, 2 * head_dim
        )
        visible = key_place < lax.dynamic_index_in_dim(patch_counts, clip_index, 0, keepdims=False)
        query_all = lax.dynamic_index_in_dim(clip_queries, clip_index, 0, keepdims=False)

        def one_block(query_block):
            scores = (
                lax.dot_general(
                    query_block,
                    key_block[:, :head_dim],
                    (((1,), (1,)), ((), ())),
                    preferred_element_type=jnp.float32,
                )
                * score_scale
            )
            scores = jnp.where(visible[None, :], scores, -jnp.inf)
            highest = jnp.max(scores, axis=1, keepdims=True)
            weights = jnp.exp(scores - highest)
            running = jnp.sum(weights, axis=1, keepdims=True)
            mixture = jnp.dot(
                weights.astype(jnp.bfloat16),
                key_block[:, head_dim:],
                preferred_element_type=jnp.float32,
            )
            return (mixture / running).astype(jnp.bfloat16)

        return lax.map(one_block, query_all.reshape(-1, query_block_rows, head_dim)).reshape(
            -1, head_dim
        )

    attended = lax.map(attend, jnp.arange(CLIPS, dtype=jnp.int32))
    returned = lax.all_to_all(
        attended.reshape(devices, sub_rows, head_dim),
        "wide",
        split_axis=0,
        concat_axis=0,
        tiled=True,
    )
    attention = (
        returned.reshape(HEADS, groups, sub_rows, head_dim)
        .transpose(1, 2, 0, 3)
        .reshape(local_rows, vit_width)
    )
    projected = jnp.dot(attention, w_out, preferred_element_type=jnp.float32).astype(jnp.bfloat16)
    merged = projected.reshape(local_rows // 4, 4 * vit_width).astype(jnp.float32)
    centre = jnp.mean(merged, axis=1, keepdims=True)
    centered = merged - centre
    spread = jnp.mean(centered * centered, axis=1, keepdims=True)
    normed = (centered * lax.rsqrt(spread + norm_eps) * ln_gain + ln_bias).astype(jnp.bfloat16)
    tok_groups = min(8, devices)
    feat_groups = devices // tok_groups
    merge_rows = w_merge
    for bit_index in range(tok_groups.bit_length() - 1):
        partner = swapped(merge_rows, "wide", bit_index)
        upper_bit = position_self // (1 << bit_index) % 2
        merge_rows = ordered_pair(merge_rows, partner, upper_bit)
    token_count = normed.shape[0]
    part_rows = token_count // tok_groups
    feat_width = normed.shape[1] // feat_groups
    out_width = w_merge.shape[1]
    merge_send = (
        normed.reshape(tok_groups, part_rows, feat_groups, feat_width)
        .transpose(2, 0, 1, 3)
        .reshape(devices, part_rows, feat_width)
    )
    flat_rows = lax.all_to_all(merge_send, "wide", split_axis=0, concat_axis=0, tiled=True).reshape(
        -1, feat_width
    )
    partial_value = jnp.dot(flat_rows, merge_rows, preferred_element_type=jnp.float32).reshape(
        devices, -1, out_width
    )
    summed = lax.all_to_all(partial_value, "wide", split_axis=0, concat_axis=0, tiled=True)
    tokens = (
        jnp.sum(summed.reshape(feat_groups, tok_groups, part_rows, out_width), axis=0)
        .reshape(token_count, out_width)
        .astype(jnp.bfloat16)
    )
    logits = jnp.dot(tokens, w_router, preferred_element_type=jnp.float32)
    experts = w_router.shape[1]
    top_count = expert_ids.shape[1]
    matches = expert_ids[:, :, None] == jnp.arange(experts, dtype=jnp.int32)[None, None, :]
    chosen = jnp.sum(jnp.where(matches, logits[:, None, :], 0.0), axis=2)
    gate_values = jax.nn.sigmoid(chosen)
    route_weight = route_scale * gate_values / jnp.sum(gate_values, axis=1, keepdims=True)
    capacity = min(token_count, 2 * token_count * top_count // experts)
    slot_count = experts * capacity
    target = expert_ids * capacity + slot_pos
    one_hot = jnp.any(
        target[None, :, :] == jnp.arange(slot_count, dtype=jnp.int32)[:, None, None], axis=2
    ).astype(jnp.bfloat16)
    buffer = jnp.dot(one_hot, tokens, preferred_element_type=jnp.float32).astype(jnp.bfloat16)
    gate_half = w_gate[0]
    up_half = w_up[0]
    down_half = w_down[0]
    half_cap = capacity // 2
    dispatch = buffer.reshape(devices, half_cap, out_width)
    portion = lax.all_to_all(dispatch, "wide", split_axis=0, concat_axis=0, tiled=True)
    item_count = portion.shape[1]
    partner_rows = swapped(portion, "wide", 0)
    both_rows = jnp.concatenate([portion, partner_rows], axis=1)
    flat_rows = both_rows.reshape(-1, out_width)
    gate_part = jnp.dot(flat_rows, gate_half, preferred_element_type=jnp.float32)
    up_part = jnp.dot(flat_rows, up_half, preferred_element_type=jnp.float32)
    hidden = (jax.nn.silu(gate_part) * up_part).astype(jnp.bfloat16)
    product = (
        jnp.dot(hidden, down_half, preferred_element_type=jnp.float32)
        .astype(jnp.bfloat16)
        .reshape(devices, 2 * item_count, out_width)
    )
    from_partner = swapped(product[:, item_count:], "wide", 0)
    joined = (
        product[:, :item_count].astype(jnp.float32) + from_partner.astype(jnp.float32)
    ).astype(jnp.bfloat16)
    answers = lax.all_to_all(joined, "wide", split_axis=0, concat_axis=0, tiled=True)
    slot_result = answers.reshape(slot_count, out_width)
    slot_result = lax.optimization_barrier(slot_result)
    picked = jnp.take(slot_result, target.reshape(-1), axis=0).reshape(
        token_count, top_count, out_width
    )
    return jnp.sum(picked.astype(jnp.float32) * route_weight[:, :, None], axis=1).astype(
        jnp.bfloat16
    )


BF = jnp.bfloat16
F32 = jnp.float32
VMEM = pl.BlockSpec(memory_space=pltpu.VMEM)
SMEM = pl.BlockSpec(memory_space=pltpu.SMEM)
HBM = pl.BlockSpec(memory_space=pltpu.HBM)
LANES = 128
MASKED = -1e30
LOG2E = 1.4426950408889634


def params(mib):
    return pltpu.CompilerParams(vmem_limit_bytes=mib * 2**20)


def cost(flops, size, exps=0):
    return pl.CostEstimate(flops=flops, bytes_accessed=size, transcendentals=exps)


def flipped(number, bits):
    low = (number % 2 + bits % 2) % 2
    return 2 * ((number // 2 + bits // 2) % 2) + low


def pieces(value, count):
    out = []
    for _ in range(count):
        piece = value.astype(BF).astype(F32)
        out.append(piece)
        value = value - piece
    return out


def pack_kernel(qkv_ref, out_ref):
    rows, width = qkv_ref.shape
    tokens = rows // 4
    peers, parts, _ = out_ref.shape
    source = lax.broadcasted_iota(jnp.int32, (rows, rows), 0)
    place = lax.broadcasted_iota(jnp.int32, (rows, rows), 1)
    order = jnp.where(source == 4 * (place % tokens) + place // tokens, 1.0, 0.0).astype(BF)
    part = parts // 3
    third = width // 3
    for kind in range(3):
        turned = lax.dot_general(
            qkv_ref[:, kind * third : (kind + 1) * third],
            order,
            (((0,), (0,)), ((), ())),
            preferred_element_type=F32,
        ).astype(BF)
        for peer in range(peers):
            out_ref[peer, kind * part : (kind + 1) * part, :] = turned[peer * part : (peer + 1) * part]


def share_kernel(merge_ref, common_ref, share_ref, sems):
    common, share = common_ref.shape[0], share_ref.shape[0]
    spot = pl.multiple_of(common + share * lax.axis_index("grp"), 16)
    copies = [
        pltpu.make_async_copy(merge_ref.at[pl.ds(spot, share), :], share_ref, sems.at[0]),
        pltpu.make_async_copy(merge_ref.at[pl.ds(0, common), :], common_ref, sems.at[1]),
    ]
    for copy in copies:
        copy.start()
    for copy in copies:
        copy.wait()


def attend_kernel(x_ref, grid_ref, out_ref):
    peers, parts, lanes = x_ref.shape
    part = parts // 3
    dim = part // 2
    quarters = 4
    sides = peers // quarters
    tokens = lanes // 4
    clip = lax.axis_index("wide") // peers
    count = grid_ref[clip, 0] * grid_ref[clip, 1]
    factor = dim ** (-0.5) * LOG2E
    keys = jnp.concatenate([x_ref[s, part : 2 * part, :] for s in range(peers)], 1)
    lane = lax.broadcasted_iota(jnp.int32, (16, peers * lanes), 1)
    row = lax.broadcasted_iota(jnp.int32, (16, peers * lanes), 0)
    inner = lane % lanes
    place = lane // lanes * lanes + 4 * (inner % tokens) + inner // tokens
    hidden = jnp.where((row == 0) & (place >= count), MASKED, 0.0).astype(BF)
    keys = jnp.concatenate([keys, hidden], 0).T
    values = jnp.concatenate([x_ref[s, 2 * part :, :] for s in range(peers)], 1).astype(F32)
    values = [values[:dim].astype(BF), values[dim:].astype(BF)]
    ones = jnp.where(lax.broadcasted_iota(jnp.int32, (16, sides * lanes), 0) == 0, 1.0, 0.0).astype(BF)
    head_row = lax.broadcasted_iota(jnp.int32, (part, sides * lanes), 0) // dim
    group = lax.broadcasted_iota(jnp.int32, (dim, lanes), 1) // tokens
    def scores_of(item):
        quarter, head = item // 2, item % 2
        query = jnp.concatenate(
            [x_ref[quarter + quarters * s, :part, :] for s in range(sides)], 1
        ).astype(F32)
        own = jnp.concatenate([jnp.where(head_row == head, query, 0.0).astype(BF), ones], 0)
        return jnp.dot(keys, own, preferred_element_type=F32)

    scores = scores_of(0)
    for item in range(2 * quarters):
        quarter, head = item // 2, item % 2
        following = scores_of(item + 1) if item + 1 < 2 * quarters else None
        highest = jnp.max(scores, axis=0, keepdims=True)
        weights = jnp.exp2((scores - highest) * factor)
        total = jnp.sum(weights, axis=0, keepdims=True)
        value = jnp.dot(values[head], weights.astype(BF), preferred_element_type=F32) / total
        mixed = [] if head == 0 else mixed
        mixed += [value[:, s * lanes : (s + 1) * lanes] for s in range(sides)]
        scores = following
        if head == 0:
            continue
        for position in range(4):
            block = mixed[position]
            for g in range(4):
                if g != position:
                    shift = (g - position) * tokens % lanes
                    block = jnp.where(group == g, pltpu.roll(mixed[g], shift, 1), block)
            out_ref[quarters * position + quarter] = block.astype(BF)


def merge_kernel(
    x_ref, w_out_hbm, gain_ref, bias_ref, *refs
):
    w0, w1, *rest, out_ref, att_ref, w_ref, w_out_ref, sems = refs
    me, group = lax.axis_index("wide"), lax.axis_index("grp")
    position, quarter = me // 4, me % 4
    blocks, dim, lanes = x_ref.shape
    pairs = blocks // 2
    depth = w0.shape[0]
    out_width = w0.shape[1]
    width = w_out_ref.shape[1]
    first_copy = pltpu.make_async_copy(w_out_hbm, w_out_ref, sems.at[8])
    first_copy.start()
    copies = []
    common, share = rest[0].shape[0], rest[1].shape[0]
    places = [(w0, 0, 0), (w1, 1, 0)]
    for k in (2, 3):
        both, mine, theirs = rest[3 * (k - 2) : 3 * (k - 1)]
        places += [(both, k, 0), (mine, k, common + share * group), (theirs, k, common + share * (1 - group))]
    for n, (source, k, first) in enumerate(places):
        spot = pl.multiple_of(flipped(quarter, k) * depth + first, 16)
        copies.append(pltpu.make_async_copy(source, w_ref.at[pl.ds(spot, source.shape[0]), :], sems.at[n]))
        copies[-1].start()
    left = lax.broadcasted_iota(jnp.int32, (dim, lanes), 1) < lanes // 2
    for pair in range(pairs):
        first, second = x_ref[pair].astype(F32), x_ref[pairs + pair].astype(F32)
        upper = jnp.where(left, first, pltpu.roll(second, lanes // 2, 1))
        lower = jnp.where(left, pltpu.roll(first, lanes // 2, 1), second)
        att_ref[2 * dim * pair : 2 * dim * (pair + 1), :] = jnp.concatenate([upper, lower], 0).astype(BF)
    first_copy.wait()
    mixed = lax.dot_general(
        att_ref[...], w_out_ref[...], (((0,), (0,)), ((), ())), preferred_element_type=F32
    )
    mixed = mixed.astype(BF).astype(F32)
    centre = jnp.sum(mixed, axis=1, keepdims=True) / width
    centered = mixed - centre
    square = jnp.sum(centered * centered, axis=1, keepdims=True)
    here = pl.ds(pl.multiple_of(position * width, LANES), width)
    gain, bias = gain_ref[:, here], bias_ref[:, here]
    row = lax.broadcasted_iota(jnp.int32, (16, width), 0)
    extra = jnp.zeros((16, width), F32)
    for k, line in enumerate(pieces(gain, 2) + pieces(bias, 2)):
        extra = jnp.where(row == k, line, extra)
    left_side = jnp.concatenate([(centered * gain).astype(BF), extra.astype(BF)], 0)
    lane = lax.broadcasted_iota(jnp.int32, (lanes, LANES), 1)
    stats = jnp.zeros((lanes, LANES), F32)
    for k, column in enumerate(pieces(centre, 3) + pieces(square, 3)):
        stats = jnp.where(lane == k, column, stats)
    stats = stats.astype(BF)
    for copy in copies:
        copy.wait()
    planes, tokens, _ = out_ref.shape
    half = tokens // 2
    step = 2 * LANES
    shared = [None] * tokens
    for begin in range(0, out_width, step):
        part = jnp.dot(left_side, w_ref[:, begin : begin + step], preferred_element_type=F32)
        for plane in range(planes):
            out_ref[flipped(position, plane), :, begin : begin + step] = part[plane * tokens : (plane + 1) * tokens].astype(BF)
        scale = part[lanes : lanes + 1] + part[lanes + 1 : lanes + 2]
        shift = part[lanes + 2 : lanes + 3] + part[lanes + 3 : lanes + 4]
        for k in range(step // LANES):
            shared[begin // LANES + k] = scale[:, k * LANES : (k + 1) * LANES]
            shared[half + begin // LANES + k] = shift[:, k * LANES : (k + 1) * LANES]
    shared = jnp.concatenate(shared, 0).astype(BF)
    for plane in range(planes):
        out_ref[flipped(position, plane), :, out_width : out_width + LANES] = shared
        out_ref[flipped(position, plane), :, out_width + LANES :] = stats[plane * tokens : (plane + 1) * tokens]


def route_kernel(x0, x1, x2, x3, router_ref, ids_ref, out_ref, *, merge_width, experts):
    blocks = (x0, x1, x2, x3)
    planes, tokens = len(blocks), x0.shape[0]
    out_width = out_ref.shape[1] - LANES
    half = tokens // 2
    stats = [blocks[p][:, out_width + LANES :].astype(F32) for p in range(planes)]
    shared = [blocks[p][:, out_width : out_width + LANES].astype(F32) for p in range(planes)]
    centres = [s[:, 0:1] + s[:, 1:2] + s[:, 2:3] for s in stats]
    squares = [s[:, 3:4] + s[:, 4:5] + s[:, 5:6] for s in stats]
    mean = sum(centres) / planes
    offsets = [c - mean for c in centres]
    spread = sum(q + (merge_width // planes) * (o * o) for q, o in zip(squares, offsets)) / merge_width
    inverse = lax.rsqrt(spread + norm_eps)
    bias = sum(shared)
    for k in range(out_width // LANES):
        cut = slice(k * LANES, (k + 1) * LANES)
        total = sum(blocks[p][:, cut].astype(F32) for p in range(planes))
        total += sum(offsets[p] * shared[p][k : k + 1] for p in range(planes))
        out_ref[:, cut] = (total * inverse + bias[half + k : half + k + 1]).astype(BF)
    logits = jnp.dot(out_ref[:, :out_width], router_ref[...], preferred_element_type=F32)
    lane = lax.broadcasted_iota(jnp.int32, (tokens, LANES), 1)
    expert = lane % experts
    chosen = lane < 0
    for k in range(ids_ref.shape[1]):
        chosen = chosen | (ids_ref[:, k : k + 1] == expert)
    gates = jnp.where(chosen & (lane < 2 * experts), 1.0 / (1.0 + jnp.exp(-logits)), 0.0)
    total = jnp.sum(jnp.where(lane < experts, gates, 0.0), axis=1, keepdims=True)
    weight = route_scale * gates / total
    high, low = pieces(weight, 2)
    out_ref[:, out_width:] = jnp.where(lane < experts, high, low).astype(BF)


def expert_kernel(*refs, experts, cuts):
    *blocks, gate_hbm, up_hbm, down_hbm, own_ref, other_ref, x_ref, gate_ref, up_ref, down_ref, sems = refs
    tokens, width = own_ref.shape[1:]
    half = len(blocks) // 2
    copies = []
    for k, cut in enumerate(cuts):
        for kind, source, target in ((0, gate_hbm, gate_ref), (1, up_hbm, up_ref)):
            copies.append(pltpu.make_async_copy(source.at[0, cut, :], target.at[cut, :], sems.at[2 * k + kind]))
            copies[-1].start()
    last = pltpu.make_async_copy(down_hbm.at[0], down_ref, sems.at[2 * len(cuts)])
    last.start()
    expert = lax.axis_index("wide") // 2
    lane = lax.broadcasted_iota(jnp.int32, (tokens, LANES), 1)
    weights = []
    for k, block in enumerate(blocks):
        x_ref[k * tokens : (k + 1) * tokens, :] = block[:, :width]
        picked = (lane == expert) | (lane == expert + experts)
        picked = jnp.where(picked, block[:, width:].astype(F32), 0.0)
        weights.append(jnp.sum(picked, axis=1, keepdims=True))
    inputs = x_ref[...]
    turned = (((1,), (1,)), ((), ()))

    def gated(gate, up):
        return (gate / (1.0 + jnp.exp(-gate)) * up).astype(BF)

    hidden, earlier = [], None
    for k, cut in enumerate(cuts):
        copies[2 * k].wait()
        gate = lax.dot_general(inputs, gate_ref[cut, :], turned, preferred_element_type=F32)
        copies[2 * k + 1].wait()
        up = lax.dot_general(inputs, up_ref[cut, :], turned, preferred_element_type=F32)
        if earlier is not None:
            hidden.append(gated(*earlier))
        earlier = gate, up
    hidden = jnp.concatenate(hidden + [gated(*earlier)], 1)
    last.wait()
    step = 4 * LANES

    def product_of(begin):
        return jnp.dot(hidden, down_ref[:, begin : begin + step], preferred_element_type=F32)

    following = product_of(0)
    for begin in range(0, width, step):
        product = following
        following = product_of(begin + step) if begin + step < width else None
        for k in range(len(blocks)):
            value = (product[k * tokens : (k + 1) * tokens] * weights[k]).astype(BF)
            out_ref = own_ref if k < half else other_ref
            out_ref[k % half, :, begin : begin + step] = value


def crossed(value, mask):
    pairs = [(source, source ^ mask) for source in range(lax.axis_size("wide"))]
    return lax.ppermute(value, "wide", pairs)


def local(
    qkv, grid, w_out, ln_gain, ln_bias, w_merge, w_router, expert_ids, slot_pos, w_gate, w_up, w_down
):
    devices = lax.axis_size("wide")
    rows = qkv.shape[0]
    vit_width = w_out.shape[0]
    experts = w_router.shape[1]
    out_width = w_merge.shape[1]
    tokens = rows // 4
    peers = devices // CLIPS
    suits = (
        devices == HEADS
        and peers == 8
        and rows == LANES
        and devices == 2 * experts
        and 2 * out_width == tokens * LANES
        and 4 * w_merge.shape[0] == vit_width
        and lax.axis_size("grp") == 2
        and w_merge.shape[0] % 32 == 0
    )
    if not suits:
        return general(
            qkv, grid, w_out, ln_gain, ln_bias, w_merge, w_router, expert_ids, slot_pos, w_gate, w_up, w_down
        )
    part = vit_width // peers
    dim = vit_width // HEADS
    depth = w_merge.shape[0]
    share = depth // 64 * 16
    packed = pl.pallas_call(
        pack_kernel,
        out_shape=jax.ShapeDtypeStruct((peers, 3 * part, rows), BF),
        in_specs=[VMEM],
        out_specs=VMEM,
        compiler_params=params(8),
    )(qkv)
    common, shared = pl.pallas_call(
        share_kernel,
        out_shape=[
            jax.ShapeDtypeStruct((depth - 2 * share, out_width), BF),
            jax.ShapeDtypeStruct((share, out_width), BF),
        ],
        in_specs=[HBM],
        out_specs=[VMEM] * 2,
        scratch_shapes=[pltpu.SemaphoreType.DMA((2,))],
        compiler_params=params(8),
        cost_estimate=cost(2**31, 2**24),
    )(w_merge)
    clips = [[c * peers + i for i in range(peers)] for c in range(CLIPS)]
    gathered = lax.all_to_all(
        packed, "wide", split_axis=0, concat_axis=0, tiled=True, axis_index_groups=clips
    )
    gathered, common, shared, held = lax.optimization_barrier((gathered, common, shared, w_merge))
    mine_y = crossed(shared, 2)
    attended = pl.pallas_call(
        attend_kernel,
        out_shape=jax.ShapeDtypeStruct((devices, dim, rows), BF),
        in_specs=[VMEM, SMEM],
        out_specs=VMEM,
        compiler_params=params(20),
        cost_estimate=cost(2**32, 2**22, 2**21),
    )(gathered, grid)
    held_c = crossed(held, 1)
    attended, mine_y, common = lax.optimization_barrier((attended, mine_y, common))
    common_y = crossed(common, 2)
    theirs_y = lax.ppermute(mine_y, "grp", [(0, 1), (1, 0)])
    mine_yc = crossed(mine_y, 1)
    returned = lax.all_to_all(attended, "wide", split_axis=0, concat_axis=0, tiled=True)
    returned, common_y, theirs_y = lax.optimization_barrier((returned, common_y, theirs_y))
    common_yc, theirs_yc = crossed(common_y, 1), crossed(theirs_y, 1)
    planes = devices // 4
    message = out_width + 2 * LANES
    partial = pl.pallas_call(
        merge_kernel,
        out_shape=jax.ShapeDtypeStruct((planes, tokens, message), BF),
        in_specs=[VMEM, HBM, VMEM, VMEM] + [pl.BlockSpec(memory_space=pl.ANY)] * 8,
        out_specs=VMEM,
        scratch_shapes=[
            pltpu.VMEM((vit_width, rows), BF),
            pltpu.VMEM((vit_width, out_width), BF),
            pltpu.VMEM((vit_width, vit_width), BF),
            pltpu.SemaphoreType.DMA((9,)),
        ],
        compiler_params=params(50),
    )(
        returned,
        w_out,
        ln_gain.reshape(1, 4 * vit_width),
        ln_bias.reshape(1, 4 * vit_width),
        w_merge,
        held_c,
        common_y,
        mine_y,
        theirs_y,
        common_yc,
        mine_yc,
        theirs_yc,
    )
    along = (8, 12, 4)
    arrived = [partial[0]] + [crossed(partial[mask // 4], mask) for mask in along]
    router = jnp.concatenate(
        [w_router, w_router, jnp.zeros((out_width, LANES - 2 * experts), BF)], 1
    )
    routed = pl.pallas_call(
        lambda *refs: route_kernel(*refs, merge_width=4 * vit_width, experts=experts),
        out_shape=jax.ShapeDtypeStruct((tokens, out_width + LANES), BF),
        in_specs=[VMEM] * 6,
        out_specs=VMEM,
        compiler_params=params(6),
    )(*arrived, router, expert_ids)
    near = [routed] + [crossed(routed, mask) for mask in along]
    far = [crossed(block, 2) for block in near]
    *near, far[0] = lax.optimization_barrier((*near, far[0]))
    gate_turned, up_turned = jnp.swapaxes(w_gate, 1, 2), jnp.swapaxes(w_up, 1, 2)

    inner = w_down.shape[1]
    cuts = [slice(k, min(k + 2 * LANES, inner)) for k in range(0, inner, 2 * LANES)]

    def experts_of(blocks):
        return pl.pallas_call(
            lambda *refs: expert_kernel(*refs, experts=experts, cuts=cuts),
            out_shape=[jax.ShapeDtypeStruct((planes, tokens, out_width), BF)] * 2,
            in_specs=[VMEM] * (2 * planes) + [HBM] * 3,
            out_specs=[VMEM, VMEM],
            scratch_shapes=[
                pltpu.VMEM((2 * planes * tokens, out_width), BF),
                pltpu.VMEM((inner, out_width), BF),
                pltpu.VMEM((inner, out_width), BF),
                pltpu.VMEM((inner, out_width), BF),
                pltpu.SemaphoreType.DMA((2 * len(cuts) + 1,)),
            ],
            compiler_params=params(50),
            cost_estimate=cost(2**32, 2**24),
        )(*blocks, *[crossed(block, 1) for block in blocks], gate_turned, up_turned, w_down)

    def scattered(blocks):
        others = [crossed(blocks[1 + along.index(mask)], mask) for mask in along]
        return blocks[0].astype(F32) + sum(block.astype(F32) for block in others)

    def paired(own, other):
        return (own.astype(F32) + crossed(other, 1).astype(F32)).astype(BF)

    near_own, near_other = experts_of(near)
    *far, near_own, near_other = lax.optimization_barrier((*far, near_own, near_other))
    far_own, far_other = experts_of(far)
    near_sum = scattered(paired(near_own, near_other))
    far_out, near_sum = lax.optimization_barrier((paired(far_own, far_other), near_sum))
    across = [crossed(far_out[k], 2 + mask) for k, mask in enumerate(along, 1)]
    across.append(crossed(far_out[0], 2))
    return (near_sum + sum(block.astype(F32) for block in across)).astype(BF)


def solution(mesh):
    placed = (
        P(("grp", "wide"), None),
        P("grp", None),
        P(),
        P(),
        P(),
        P("wide", None),
        P(),
        P(("grp", "wide"), None),
        P(("grp", "wide"), None),
        P("wide", None, None),
        P("wide", None, None),
        P("wide", None, None),
    )
    return jax.shard_map(
        local, mesh=mesh, in_specs=placed, out_specs=P(("grp", "wide"), None), check_vma=False
    )
```

```python
import jax
import jax.numpy as jnp
from jax import lax
from jax.experimental import pallas as pl
from jax.experimental.pallas import tpu as pltpu
from jax.sharding import PartitionSpec as P

HEADS = 16
CLIPS = 2


route_scale = 2.446
norm_eps = 1e-05


def swapped(value, axis, stride):
    mask = 2**stride
    pairs = [(source, source ^ mask) for source in range(lax.axis_size(axis))]
    return lax.ppermute(value, axis, pairs)


def ordered_pair(own_part, partner, upper_bit):
    return jnp.where(
        upper_bit == 1,
        jnp.concatenate([partner, own_part], 0),
        jnp.concatenate([own_part, partner], 0),
    )


def general(
    qkv,
    grid,
    w_out,
    ln_gain,
    ln_bias,
    w_merge,
    w_router,
    expert_ids,
    slot_pos,
    w_gate,
    w_up,
    w_down,
):
    devices = lax.axis_size("wide")
    position_self = lax.axis_index("wide")
    vit_width = w_out.shape[0]
    head_dim = vit_width // HEADS
    groups = devices // HEADS
    local_rows = qkv.shape[0]
    sub_rows = local_rows // groups
    per_clip = devices // CLIPS
    query_send = (
        qkv[:, :vit_width]
        .reshape(groups, sub_rows, HEADS, head_dim)
        .transpose(2, 0, 1, 3)
        .reshape(devices, sub_rows, head_dim)
    )
    key_value = jnp.concatenate(
        [
            qkv[:, vit_width : 2 * vit_width].reshape(local_rows, HEADS, head_dim),
            qkv[:, 2 * vit_width :].reshape(local_rows, HEADS, head_dim),
        ],
        axis=2,
    )
    spread_send = jnp.broadcast_to(
        key_value.transpose(1, 0, 2)[:, None], (HEADS, groups, local_rows, 2 * head_dim)
    ).reshape(devices, local_rows, 2 * head_dim)
    queries, key_rows = (
        lax.all_to_all(query_send, "wide", split_axis=0, concat_axis=0, tiled=True),
        lax.all_to_all(spread_send, "wide", split_axis=0, concat_axis=0, tiled=True),
    )
    key_rows = key_rows[None]
    key_groups = key_rows.shape[0]
    key_count = key_rows.shape[2]
    key_place = (
        jnp.arange(per_clip, dtype=jnp.int32)[None, :, None] * local_rows
        + jnp.arange(key_groups, dtype=jnp.int32)[:, None, None] * local_rows
        + jnp.arange(key_count, dtype=jnp.int32)[None, None, :]
    ).reshape(-1)
    patch_counts = grid[:, 0] * grid[:, 1]
    clip_queries = queries.reshape(CLIPS, per_clip * sub_rows, head_dim)
    query_block_rows = min(512, per_clip * sub_rows)
    score_scale = head_dim ** (-0.5)

    def attend(clip_index):
        key_block = lax.dynamic_slice_in_dim(key_rows, clip_index * per_clip, per_clip, 1).reshape(
            -1, 2 * head_dim
        )
        visible = key_place < lax.dynamic_index_in_dim(patch_counts, clip_index, 0, keepdims=False)
        query_all = lax.dynamic_index_in_dim(clip_queries, clip_index, 0, keepdims=False)

        def one_block(query_block):
            scores = (
                lax.dot_general(
                    query_block,
                    key_block[:, :head_dim],
                    (((1,), (1,)), ((), ())),
                    preferred_element_type=jnp.float32,
                )
                * score_scale
            )
            scores = jnp.where(visible[None, :], scores, -jnp.inf)
            highest = jnp.max(scores, axis=1, keepdims=True)
            weights = jnp.exp(scores - highest)
            running = jnp.sum(weights, axis=1, keepdims=True)
            mixture = jnp.dot(
                weights.astype(jnp.bfloat16),
                key_block[:, head_dim:],
                preferred_element_type=jnp.float32,
            )
            return (mixture / running).astype(jnp.bfloat16)

        return lax.map(one_block, query_all.reshape(-1, query_block_rows, head_dim)).reshape(
            -1, head_dim
        )

    attended = lax.map(attend, jnp.arange(CLIPS, dtype=jnp.int32))
    returned = lax.all_to_all(
        attended.reshape(devices, sub_rows, head_dim),
        "wide",
        split_axis=0,
        concat_axis=0,
        tiled=True,
    )
    attention = (
        returned.reshape(HEADS, groups, sub_rows, head_dim)
        .transpose(1, 2, 0, 3)
        .reshape(local_rows, vit_width)
    )
    projected = jnp.dot(attention, w_out, preferred_element_type=jnp.float32).astype(jnp.bfloat16)
    merged = projected.reshape(local_rows // 4, 4 * vit_width).astype(jnp.float32)
    centre = jnp.mean(merged, axis=1, keepdims=True)
    centered = merged - centre
    spread = jnp.mean(centered * centered, axis=1, keepdims=True)
    normed = (centered * lax.rsqrt(spread + norm_eps) * ln_gain + ln_bias).astype(jnp.bfloat16)
    tok_groups = min(8, devices)
    feat_groups = devices // tok_groups
    merge_rows = w_merge
    for bit_index in range(tok_groups.bit_length() - 1):
        partner = swapped(merge_rows, "wide", bit_index)
        upper_bit = position_self // (1 << bit_index) % 2
        merge_rows = ordered_pair(merge_rows, partner, upper_bit)
    token_count = normed.shape[0]
    part_rows = token_count // tok_groups
    feat_width = normed.shape[1] // feat_groups
    out_width = w_merge.shape[1]
    merge_send = (
        normed.reshape(tok_groups, part_rows, feat_groups, feat_width)
        .transpose(2, 0, 1, 3)
        .reshape(devices, part_rows, feat_width)
    )
    flat_rows = lax.all_to_all(merge_send, "wide", split_axis=0, concat_axis=0, tiled=True).reshape(
        -1, feat_width
    )
    partial_value = jnp.dot(flat_rows, merge_rows, preferred_element_type=jnp.float32).reshape(
        devices, -1, out_width
    )
    summed = lax.all_to_all(partial_value, "wide", split_axis=0, concat_axis=0, tiled=True)
    tokens = (
        jnp.sum(summed.reshape(feat_groups, tok_groups, part_rows, out_width), axis=0)
        .reshape(token_count, out_width)
        .astype(jnp.bfloat16)
    )
    logits = jnp.dot(tokens, w_router, preferred_element_type=jnp.float32)
    experts = w_router.shape[1]
    top_count = expert_ids.shape[1]
    matches = expert_ids[:, :, None] == jnp.arange(experts, dtype=jnp.int32)[None, None, :]
    chosen = jnp.sum(jnp.where(matches, logits[:, None, :], 0.0), axis=2)
    gate_values = jax.nn.sigmoid(chosen)
    route_weight = route_scale * gate_values / jnp.sum(gate_values, axis=1, keepdims=True)
    capacity = min(token_count, 2 * token_count * top_count // experts)
    slot_count = experts * capacity
    target = expert_ids * capacity + slot_pos
    one_hot = jnp.any(
        target[None, :, :] == jnp.arange(slot_count, dtype=jnp.int32)[:, None, None], axis=2
    ).astype(jnp.bfloat16)
    buffer = jnp.dot(one_hot, tokens, preferred_element_type=jnp.float32).astype(jnp.bfloat16)
    gate_half = w_gate[0]
    up_half = w_up[0]
    down_half = w_down[0]
    half_cap = capacity // 2
    dispatch = buffer.reshape(devices, half_cap, out_width)
    portion = lax.all_to_all(dispatch, "wide", split_axis=0, concat_axis=0, tiled=True)
    item_count = portion.shape[1]
    partner_rows = swapped(portion, "wide", 0)
    both_rows = jnp.concatenate([portion, partner_rows], axis=1)
    flat_rows = both_rows.reshape(-1, out_width)
    gate_part = jnp.dot(flat_rows, gate_half, preferred_element_type=jnp.float32)
    up_part = jnp.dot(flat_rows, up_half, preferred_element_type=jnp.float32)
    hidden = (jax.nn.silu(gate_part) * up_part).astype(jnp.bfloat16)
    product = (
        jnp.dot(hidden, down_half, preferred_element_type=jnp.float32)
        .astype(jnp.bfloat16)
        .reshape(devices, 2 * item_count, out_width)
    )
    from_partner = swapped(product[:, item_count:], "wide", 0)
    joined = (
        product[:, :item_count].astype(jnp.float32) + from_partner.astype(jnp.float32)
    ).astype(jnp.bfloat16)
    answers = lax.all_to_all(joined, "wide", split_axis=0, concat_axis=0, tiled=True)
    slot_result = answers.reshape(slot_count, out_width)
    slot_result = lax.optimization_barrier(slot_result)
    picked = jnp.take(slot_result, target.reshape(-1), axis=0).reshape(
        token_count, top_count, out_width
    )
    return jnp.sum(picked.astype(jnp.float32) * route_weight[:, :, None], axis=1).astype(
        jnp.bfloat16
    )


BF = jnp.bfloat16
F32 = jnp.float32
VMEM = pl.BlockSpec(memory_space=pltpu.VMEM)
SMEM = pl.BlockSpec(memory_space=pltpu.SMEM)
HBM = pl.BlockSpec(memory_space=pltpu.HBM)
LANES = 128
MASKED = -1e30
LOG2E = 1.4426950408889634


def params(mib):
    return pltpu.CompilerParams(vmem_limit_bytes=mib * 2**20)


def cost(flops, size, exps=0):
    return pl.CostEstimate(flops=flops, bytes_accessed=size, transcendentals=exps)


def flipped(number, bits):
    low = (number % 2 + bits % 2) % 2
    return 2 * ((number // 2 + bits // 2) % 2) + low


def pieces(value, count):
    out = []
    for _ in range(count):
        piece = value.astype(BF).astype(F32)
        out.append(piece)
        value = value - piece
    return out


def pack_kernel(qkv_ref, out_ref):
    rows, width = qkv_ref.shape
    tokens = rows // 4
    peers, parts, _ = out_ref.shape
    source = lax.broadcasted_iota(jnp.int32, (rows, rows), 0)
    place = lax.broadcasted_iota(jnp.int32, (rows, rows), 1)
    order = jnp.where(source == 4 * (place % tokens) + place // tokens, 1.0, 0.0).astype(BF)
    part = parts // 3
    third = width // 3
    for kind in range(3):
        turned = lax.dot_general(
            qkv_ref[:, kind * third : (kind + 1) * third],
            order,
            (((0,), (0,)), ((), ())),
            preferred_element_type=F32,
        ).astype(BF)
        for peer in range(peers):
            out_ref[peer, kind * part : (kind + 1) * part, :] = turned[peer * part : (peer + 1) * part]


def share_kernel(merge_ref, common_ref, share_ref, sems):
    common, share = common_ref.shape[0], share_ref.shape[0]
    spot = pl.multiple_of(common + share * lax.axis_index("grp"), 16)
    copies = [
        pltpu.make_async_copy(merge_ref.at[pl.ds(spot, share), :], share_ref, sems.at[0]),
        pltpu.make_async_copy(merge_ref.at[pl.ds(0, common), :], common_ref, sems.at[1]),
    ]
    for copy in copies:
        copy.start()
    for copy in copies:
        copy.wait()


def attend_kernel(x_ref, grid_ref, out_ref):
    peers, parts, lanes = x_ref.shape
    part = parts // 3
    dim = part // 2
    quarters = 4
    sides = peers // quarters
    tokens = lanes // 4
    clip = lax.axis_index("wide") // peers
    count = grid_ref[clip, 0] * grid_ref[clip, 1]
    factor = dim ** (-0.5) * LOG2E
    keys = jnp.concatenate([x_ref[s, part : 2 * part, :] for s in range(peers)], 1)
    lane = lax.broadcasted_iota(jnp.int32, (16, peers * lanes), 1)
    row = lax.broadcasted_iota(jnp.int32, (16, peers * lanes), 0)
    inner = lane % lanes
    place = lane // lanes * lanes + 4 * (inner % tokens) + inner // tokens
    hidden = jnp.where((row == 0) & (place >= count), MASKED, 0.0).astype(BF)
    keys = jnp.concatenate([keys, hidden], 0).T
    values = jnp.concatenate([x_ref[s, 2 * part :, :] for s in range(peers)], 1).astype(F32)
    values = [values[:dim].astype(BF), values[dim:].astype(BF)]
    ones = jnp.where(lax.broadcasted_iota(jnp.int32, (16, sides * lanes), 0) == 0, 1.0, 0.0).astype(BF)
    head_row = lax.broadcasted_iota(jnp.int32, (part, sides * lanes), 0) // dim
    group = lax.broadcasted_iota(jnp.int32, (dim, lanes), 1) // tokens
    def scores_of(item):
        quarter, head = item // 2, item % 2
        query = jnp.concatenate(
            [x_ref[quarter + quarters * s, :part, :] for s in range(sides)], 1
        ).astype(F32)
        own = jnp.concatenate([jnp.where(head_row == head, query, 0.0).astype(BF), ones], 0)
        return jnp.dot(keys, own, preferred_element_type=F32)

    scores = scores_of(0)
    for item in range(2 * quarters):
        quarter, head = item // 2, item % 2
        following = scores_of(item + 1) if item + 1 < 2 * quarters else None
        highest = jnp.max(scores, axis=0, keepdims=True)
        weights = jnp.exp2((scores - highest) * factor)
        total = jnp.sum(weights, axis=0, keepdims=True)
        value = jnp.dot(values[head], weights.astype(BF), preferred_element_type=F32) / total
        mixed = [] if head == 0 else mixed
        mixed += [value[:, s * lanes : (s + 1) * lanes] for s in range(sides)]
        scores = following
        if head == 0:
            continue
        for position in range(4):
            block = mixed[position]
            for g in range(4):
                if g != position:
                    shift = (g - position) * tokens % lanes
                    block = jnp.where(group == g, pltpu.roll(mixed[g], shift, 1), block)
            out_ref[quarters * position + quarter] = block.astype(BF)


def merge_kernel(
    x_ref, w_out_hbm, gain_ref, bias_ref, *refs
):
    w0, w1, *rest, out_ref, att_ref, w_ref, w_out_ref, sems = refs
    me, group = lax.axis_index("wide"), lax.axis_index("grp")
    position, quarter = me // 4, me % 4
    blocks, dim, lanes = x_ref.shape
    pairs = blocks // 2
    depth = w0.shape[0]
    out_width = w0.shape[1]
    width = w_out_ref.shape[1]
    first_copy = pltpu.make_async_copy(w_out_hbm, w_out_ref, sems.at[8])
    first_copy.start()
    copies = []
    common, share = rest[0].shape[0], rest[1].shape[0]
    places = [(w0, 0, 0), (w1, 1, 0)]
    for k in (2, 3):
        both, mine, theirs = rest[3 * (k - 2) : 3 * (k - 1)]
        places += [(both, k, 0), (mine, k, common + share * group), (theirs, k, common + share * (1 - group))]
    for n, (source, k, first) in enumerate(places):
        spot = pl.multiple_of(flipped(quarter, k) * depth + first, 16)
        copies.append(pltpu.make_async_copy(source, w_ref.at[pl.ds(spot, source.shape[0]), :], sems.at[n]))
        copies[-1].start()
    left = lax.broadcasted_iota(jnp.int32, (dim, lanes), 1) < lanes // 2
    for pair in range(pairs):
        first, second = x_ref[pair].astype(F32), x_ref[pairs + pair].astype(F32)
        upper = jnp.where(left, first, pltpu.roll(second, lanes // 2, 1))
        lower = jnp.where(left, pltpu.roll(first, lanes // 2, 1), second)
        att_ref[2 * dim * pair : 2 * dim * (pair + 1), :] = jnp.concatenate([upper, lower], 0).astype(BF)
    first_copy.wait()
    mixed = lax.dot_general(
        att_ref[...], w_out_ref[...], (((0,), (0,)), ((), ())), preferred_element_type=F32
    )
    mixed = mixed.astype(BF).astype(F32)
    centre = jnp.sum(mixed, axis=1, keepdims=True) / width
    centered = mixed - centre
    square = jnp.sum(centered * centered, axis=1, keepdims=True)
    here = pl.ds(pl.multiple_of(position * width, LANES), width)
    gain, bias = gain_ref[:, here], bias_ref[:, here]
    row = lax.broadcasted_iota(jnp.int32, (16, width), 0)
    extra = jnp.zeros((16, width), F32)
    for k, line in enumerate(pieces(gain, 2) + pieces(bias, 2)):
        extra = jnp.where(row == k, line, extra)
    left_side = jnp.concatenate([(centered * gain).astype(BF), extra.astype(BF)], 0)
    lane = lax.broadcasted_iota(jnp.int32, (lanes, LANES), 1)
    stats = jnp.zeros((lanes, LANES), F32)
    for k, column in enumerate(pieces(centre, 3) + pieces(square, 3)):
        stats = jnp.where(lane == k, column, stats)
    stats = stats.astype(BF)
    for copy in copies:
        copy.wait()
    planes, tokens, _ = out_ref.shape
    half = tokens // 2
    step = 2 * LANES
    shared = [None] * tokens
    for begin in range(0, out_width, step):
        part = jnp.dot(left_side, w_ref[:, begin : begin + step], preferred_element_type=F32)
        for plane in range(planes):
            out_ref[flipped(position, plane), :, begin : begin + step] = part[plane * tokens : (plane + 1) * tokens].astype(BF)
        scale = part[lanes : lanes + 1] + part[lanes + 1 : lanes + 2]
        shift = part[lanes + 2 : lanes + 3] + part[lanes + 3 : lanes + 4]
        for k in range(step // LANES):
            shared[begin // LANES + k] = scale[:, k * LANES : (k + 1) * LANES]
            shared[half + begin // LANES + k] = shift[:, k * LANES : (k + 1) * LANES]
    shared = jnp.concatenate(shared, 0).astype(BF)
    for plane in range(planes):
        out_ref[flipped(position, plane), :, out_width : out_width + LANES] = shared
        out_ref[flipped(position, plane), :, out_width + LANES :] = stats[plane * tokens : (plane + 1) * tokens]


def route_kernel(x0, x1, x2, x3, router_ref, ids_ref, out_ref, *, merge_width, experts):
    blocks = (x0, x1, x2, x3)
    planes, tokens = len(blocks), x0.shape[0]
    out_width = out_ref.shape[1] - LANES
    half = tokens // 2
    stats = [blocks[p][:, out_width + LANES :].astype(F32) for p in range(planes)]
    shared = [blocks[p][:, out_width : out_width + LANES].astype(F32) for p in range(planes)]
    centres = [s[:, 0:1] + s[:, 1:2] + s[:, 2:3] for s in stats]
    squares = [s[:, 3:4] + s[:, 4:5] + s[:, 5:6] for s in stats]
    mean = sum(centres) / planes
    offsets = [c - mean for c in centres]
    spread = sum(q + (merge_width // planes) * (o * o) for q, o in zip(squares, offsets)) / merge_width
    inverse = lax.rsqrt(spread + norm_eps)
    bias = sum(shared)
    for k in range(out_width // LANES):
        cut = slice(k * LANES, (k + 1) * LANES)
        total = sum(blocks[p][:, cut].astype(F32) for p in range(planes))
        total += sum(offsets[p] * shared[p][k : k + 1] for p in range(planes))
        out_ref[:, cut] = (total * inverse + bias[half + k : half + k + 1]).astype(BF)
    logits = jnp.dot(out_ref[:, :out_width], router_ref[...], preferred_element_type=F32)
    lane = lax.broadcasted_iota(jnp.int32, (tokens, LANES), 1)
    expert = lane % experts
    chosen = lane < 0
    for k in range(ids_ref.shape[1]):
        chosen = chosen | (ids_ref[:, k : k + 1] == expert)
    gates = jnp.where(chosen & (lane < 2 * experts), 1.0 / (1.0 + jnp.exp(-logits)), 0.0)
    total = jnp.sum(jnp.where(lane < experts, gates, 0.0), axis=1, keepdims=True)
    weight = route_scale * gates / total
    high, low = pieces(weight, 2)
    out_ref[:, out_width:] = jnp.where(lane < experts, high, low).astype(BF)


def expert_kernel(*refs, experts, cuts):
    *blocks, gate_hbm, up_hbm, down_hbm, own_ref, other_ref, x_ref, gate_ref, up_ref, down_ref, sems = refs
    tokens, width = own_ref.shape[1:]
    half = own_ref.shape[0]
    places = [(b, slice(r, r + tokens)) for b in blocks for r in range(0, b.shape[0], tokens)]
    copies = []
    for k, cut in enumerate(cuts):
        for kind, source, target in ((0, gate_hbm, gate_ref), (1, up_hbm, up_ref)):
            copies.append(pltpu.make_async_copy(source.at[0, cut, :], target.at[cut, :], sems.at[2 * k + kind]))
            copies[-1].start()
    last = pltpu.make_async_copy(down_hbm.at[0], down_ref, sems.at[2 * len(cuts)])
    last.start()
    expert = lax.axis_index("wide") // 2
    lane = lax.broadcasted_iota(jnp.int32, (tokens, LANES), 1)
    weights = []
    for k, (block, rows) in enumerate(places):
        x_ref[k * tokens : (k + 1) * tokens, :] = block[rows, :width]
        picked = (lane == expert) | (lane == expert + experts)
        picked = jnp.where(picked, block[rows, width:].astype(F32), 0.0)
        weights.append(jnp.sum(picked, axis=1, keepdims=True))
    inputs = x_ref[...]
    turned = (((1,), (1,)), ((), ()))

    def gated(gate, up):
        return (gate / (1.0 + jnp.exp(-gate)) * up).astype(BF)

    hidden, earlier = [], None
    for k, cut in enumerate(cuts):
        copies[2 * k].wait()
        gate = lax.dot_general(inputs, gate_ref[cut, :], turned, preferred_element_type=F32)
        copies[2 * k + 1].wait()
        up = lax.dot_general(inputs, up_ref[cut, :], turned, preferred_element_type=F32)
        if earlier is not None:
            hidden.append(gated(*earlier))
        earlier = gate, up
    hidden = jnp.concatenate(hidden + [gated(*earlier)], 1)
    last.wait()
    step = 4 * LANES

    def product_of(begin):
        return jnp.dot(hidden, down_ref[:, begin : begin + step], preferred_element_type=F32)

    following = product_of(0)
    for begin in range(0, width, step):
        product = following
        following = product_of(begin + step) if begin + step < width else None
        for k in range(len(places)):
            value = (product[k * tokens : (k + 1) * tokens] * weights[k]).astype(BF)
            out_ref = own_ref if k < half else other_ref
            out_ref[k % half, :, begin : begin + step] = value


def join_kernel(*refs):
    *blocks, out_ref = refs
    rows = blocks[0].shape[0]
    for k, block in enumerate(blocks):
        out_ref[k * rows : (k + 1) * rows, :] = block[...]


def crossed(value, mask):
    pairs = [(source, source ^ mask) for source in range(lax.axis_size("wide"))]
    return lax.ppermute(value, "wide", pairs)


def local(
    qkv, grid, w_out, ln_gain, ln_bias, w_merge, w_router, expert_ids, slot_pos, w_gate, w_up, w_down
):
    devices = lax.axis_size("wide")
    rows = qkv.shape[0]
    vit_width = w_out.shape[0]
    experts = w_router.shape[1]
    out_width = w_merge.shape[1]
    tokens = rows // 4
    peers = devices // CLIPS
    suits = (
        devices == HEADS
        and peers == 8
        and rows == LANES
        and devices == 2 * experts
        and 2 * out_width == tokens * LANES
        and 4 * w_merge.shape[0] == vit_width
        and lax.axis_size("grp") == 2
        and w_merge.shape[0] % 32 == 0
    )
    if not suits:
        return general(
            qkv, grid, w_out, ln_gain, ln_bias, w_merge, w_router, expert_ids, slot_pos, w_gate, w_up, w_down
        )
    part = vit_width // peers
    dim = vit_width // HEADS
    depth = w_merge.shape[0]
    share = depth // 64 * 16
    packed = pl.pallas_call(
        pack_kernel,
        out_shape=jax.ShapeDtypeStruct((peers, 3 * part, rows), BF),
        in_specs=[VMEM],
        out_specs=VMEM,
        compiler_params=params(8),
    )(qkv)
    common, shared = pl.pallas_call(
        share_kernel,
        out_shape=[
            jax.ShapeDtypeStruct((depth - 2 * share, out_width), BF),
            jax.ShapeDtypeStruct((share, out_width), BF),
        ],
        in_specs=[HBM],
        out_specs=[VMEM] * 2,
        scratch_shapes=[pltpu.SemaphoreType.DMA((2,))],
        compiler_params=params(8),
        cost_estimate=cost(2**31, 2**24),
    )(w_merge)
    clips = [[c * peers + i for i in range(peers)] for c in range(CLIPS)]
    gathered = lax.all_to_all(
        packed, "wide", split_axis=0, concat_axis=0, tiled=True, axis_index_groups=clips
    )
    gathered, common, shared, held = lax.optimization_barrier((gathered, common, shared, w_merge))
    mine_y = crossed(shared, 2)
    common_y = crossed(common, 2)
    attended = pl.pallas_call(
        attend_kernel,
        out_shape=jax.ShapeDtypeStruct((devices, dim, rows), BF),
        in_specs=[VMEM, SMEM],
        out_specs=VMEM,
        compiler_params=params(20),
        cost_estimate=cost(2**32, 2**22, 2**21),
    )(gathered, grid)
    held_c = crossed(held, 1)
    attended, mine_y = lax.optimization_barrier((attended, mine_y))
    theirs_y = lax.ppermute(mine_y, "grp", [(0, 1), (1, 0)])
    mine_yc = crossed(mine_y, 1)
    returned = lax.all_to_all(attended, "wide", split_axis=0, concat_axis=0, tiled=True)
    returned, common_y, theirs_y = lax.optimization_barrier((returned, common_y, theirs_y))
    common_yc, theirs_yc = crossed(common_y, 1), crossed(theirs_y, 1)
    planes = devices // 4
    message = out_width + 2 * LANES
    partial = pl.pallas_call(
        merge_kernel,
        out_shape=jax.ShapeDtypeStruct((planes, tokens, message), BF),
        in_specs=[VMEM, HBM, VMEM, VMEM] + [pl.BlockSpec(memory_space=pl.ANY)] * 8,
        out_specs=VMEM,
        scratch_shapes=[
            pltpu.VMEM((vit_width, rows), BF),
            pltpu.VMEM((vit_width, out_width), BF),
            pltpu.VMEM((vit_width, vit_width), BF),
            pltpu.SemaphoreType.DMA((9,)),
        ],
        compiler_params=params(50),
    )(
        returned,
        w_out,
        ln_gain.reshape(1, 4 * vit_width),
        ln_bias.reshape(1, 4 * vit_width),
        w_merge,
        held_c,
        common_y,
        mine_y,
        theirs_y,
        common_yc,
        mine_yc,
        theirs_yc,
    )
    along = (8, 12, 4)
    arrived = [partial[0]] + [crossed(partial[mask // 4], mask) for mask in along]
    router = jnp.concatenate(
        [w_router, w_router, jnp.zeros((out_width, LANES - 2 * experts), BF)], 1
    )
    routed = pl.pallas_call(
        lambda *refs: route_kernel(*refs, merge_width=4 * vit_width, experts=experts),
        out_shape=jax.ShapeDtypeStruct((tokens, out_width + LANES), BF),
        in_specs=[VMEM] * 6,
        out_specs=VMEM,
        compiler_params=params(6),
    )(*arrived, router, expert_ids)
    joined = pl.pallas_call(
        join_kernel,
        out_shape=jax.ShapeDtypeStruct((len(along) * tokens, out_width + LANES), BF),
        in_specs=[VMEM] * len(along),
        out_specs=VMEM,
        compiler_params=params(6),
    )(*[crossed(routed, mask) for mask in along])
    near = [routed, joined]
    far = [crossed(block, 2) for block in near]
    *near, far[0] = lax.optimization_barrier((*near, far[0]))
    gate_turned, up_turned = jnp.swapaxes(w_gate, 1, 2), jnp.swapaxes(w_up, 1, 2)

    inner = w_down.shape[1]
    cuts = [slice(k, min(k + 2 * LANES, inner)) for k in range(0, inner, 2 * LANES)]

    def experts_of(blocks):
        return pl.pallas_call(
            lambda *refs: expert_kernel(*refs, experts=experts, cuts=cuts),
            out_shape=[jax.ShapeDtypeStruct((planes, tokens, out_width), BF)] * 2,
            in_specs=[VMEM] * (2 * len(blocks)) + [HBM] * 3,
            out_specs=[VMEM, VMEM],
            scratch_shapes=[
                pltpu.VMEM((2 * planes * tokens, out_width), BF),
                pltpu.VMEM((inner, out_width), BF),
                pltpu.VMEM((inner, out_width), BF),
                pltpu.VMEM((inner, out_width), BF),
                pltpu.SemaphoreType.DMA((2 * len(cuts) + 1,)),
            ],
            compiler_params=params(50),
            cost_estimate=cost(2**32, 2**24),
        )(*blocks, *[crossed(block, 1) for block in blocks], gate_turned, up_turned, w_down)

    def scattered(blocks):
        others = [crossed(blocks[1 + along.index(mask)], mask) for mask in along]
        return blocks[0].astype(F32) + sum(block.astype(F32) for block in others)

    def paired(own, other):
        return (own.astype(F32) + crossed(other, 1).astype(F32)).astype(BF)

    near_own, near_other = experts_of(near)
    *far, near_own, near_other = lax.optimization_barrier((*far, near_own, near_other))
    far_own, far_other = experts_of(far)
    near_sum = scattered(paired(near_own, near_other))
    far_out, near_sum = lax.optimization_barrier((paired(far_own, far_other), near_sum))
    across = [crossed(far_out[k], 2 + mask) for k, mask in enumerate(along, 1)]
    across.append(crossed(far_out[0], 2))
    return (near_sum + sum(block.astype(F32) for block in across)).astype(BF)


def solution(mesh):
    placed = (
        P(("grp", "wide"), None),
        P("grp", None),
        P(),
        P(),
        P(),
        P("wide", None),
        P(),
        P(("grp", "wide"), None),
        P(("grp", "wide"), None),
        P("wide", None, None),
        P("wide", None, None),
        P("wide", None, None),
    )
    return jax.shard_map(
        local, mesh=mesh, in_specs=placed, out_specs=P(("grp", "wide"), None), check_vma=False
    )
```

```python
import jax
import jax.numpy as jnp
from jax import lax
from jax.experimental import pallas as pl
from jax.experimental.pallas import tpu as pltpu
from jax.sharding import PartitionSpec as P

HEADS = 16
CLIPS = 2


route_scale = 2.446
norm_eps = 1e-05


def swapped(value, axis, stride):
    mask = 2**stride
    pairs = [(source, source ^ mask) for source in range(lax.axis_size(axis))]
    return lax.ppermute(value, axis, pairs)


def ordered_pair(own_part, partner, upper_bit):
    return jnp.where(
        upper_bit == 1,
        jnp.concatenate([partner, own_part], 0),
        jnp.concatenate([own_part, partner], 0),
    )


def general(
    qkv,
    grid,
    w_out,
    ln_gain,
    ln_bias,
    w_merge,
    w_router,
    expert_ids,
    slot_pos,
    w_gate,
    w_up,
    w_down,
):
    devices = lax.axis_size("wide")
    position_self = lax.axis_index("wide")
    vit_width = w_out.shape[0]
    head_dim = vit_width // HEADS
    groups = devices // HEADS
    local_rows = qkv.shape[0]
    sub_rows = local_rows // groups
    per_clip = devices // CLIPS
    query_send = (
        qkv[:, :vit_width]
        .reshape(groups, sub_rows, HEADS, head_dim)
        .transpose(2, 0, 1, 3)
        .reshape(devices, sub_rows, head_dim)
    )
    key_value = jnp.concatenate(
        [
            qkv[:, vit_width : 2 * vit_width].reshape(local_rows, HEADS, head_dim),
            qkv[:, 2 * vit_width :].reshape(local_rows, HEADS, head_dim),
        ],
        axis=2,
    )
    spread_send = jnp.broadcast_to(
        key_value.transpose(1, 0, 2)[:, None], (HEADS, groups, local_rows, 2 * head_dim)
    ).reshape(devices, local_rows, 2 * head_dim)
    queries, key_rows = (
        lax.all_to_all(query_send, "wide", split_axis=0, concat_axis=0, tiled=True),
        lax.all_to_all(spread_send, "wide", split_axis=0, concat_axis=0, tiled=True),
    )
    key_rows = key_rows[None]
    key_groups = key_rows.shape[0]
    key_count = key_rows.shape[2]
    key_place = (
        jnp.arange(per_clip, dtype=jnp.int32)[None, :, None] * local_rows
        + jnp.arange(key_groups, dtype=jnp.int32)[:, None, None] * local_rows
        + jnp.arange(key_count, dtype=jnp.int32)[None, None, :]
    ).reshape(-1)
    patch_counts = grid[:, 0] * grid[:, 1]
    clip_queries = queries.reshape(CLIPS, per_clip * sub_rows, head_dim)
    query_block_rows = min(512, per_clip * sub_rows)
    score_scale = head_dim ** (-0.5)

    def attend(clip_index):
        key_block = lax.dynamic_slice_in_dim(key_rows, clip_index * per_clip, per_clip, 1).reshape(
            -1, 2 * head_dim
        )
        visible = key_place < lax.dynamic_index_in_dim(patch_counts, clip_index, 0, keepdims=False)
        query_all = lax.dynamic_index_in_dim(clip_queries, clip_index, 0, keepdims=False)

        def one_block(query_block):
            scores = (
                lax.dot_general(
                    query_block,
                    key_block[:, :head_dim],
                    (((1,), (1,)), ((), ())),
                    preferred_element_type=jnp.float32,
                )
                * score_scale
            )
            scores = jnp.where(visible[None, :], scores, -jnp.inf)
            highest = jnp.max(scores, axis=1, keepdims=True)
            weights = jnp.exp(scores - highest)
            running = jnp.sum(weights, axis=1, keepdims=True)
            mixture = jnp.dot(
                weights.astype(jnp.bfloat16),
                key_block[:, head_dim:],
                preferred_element_type=jnp.float32,
            )
            return (mixture / running).astype(jnp.bfloat16)

        return lax.map(one_block, query_all.reshape(-1, query_block_rows, head_dim)).reshape(
            -1, head_dim
        )

    attended = lax.map(attend, jnp.arange(CLIPS, dtype=jnp.int32))
    returned = lax.all_to_all(
        attended.reshape(devices, sub_rows, head_dim),
        "wide",
        split_axis=0,
        concat_axis=0,
        tiled=True,
    )
    attention = (
        returned.reshape(HEADS, groups, sub_rows, head_dim)
        .transpose(1, 2, 0, 3)
        .reshape(local_rows, vit_width)
    )
    projected = jnp.dot(attention, w_out, preferred_element_type=jnp.float32).astype(jnp.bfloat16)
    merged = projected.reshape(local_rows // 4, 4 * vit_width).astype(jnp.float32)
    centre = jnp.mean(merged, axis=1, keepdims=True)
    centered = merged - centre
    spread = jnp.mean(centered * centered, axis=1, keepdims=True)
    normed = (centered * lax.rsqrt(spread + norm_eps) * ln_gain + ln_bias).astype(jnp.bfloat16)
    tok_groups = min(8, devices)
    feat_groups = devices // tok_groups
    merge_rows = w_merge
    for bit_index in range(tok_groups.bit_length() - 1):
        partner = swapped(merge_rows, "wide", bit_index)
        upper_bit = position_self // (1 << bit_index) % 2
        merge_rows = ordered_pair(merge_rows, partner, upper_bit)
    token_count = normed.shape[0]
    part_rows = token_count // tok_groups
    feat_width = normed.shape[1] // feat_groups
    out_width = w_merge.shape[1]
    merge_send = (
        normed.reshape(tok_groups, part_rows, feat_groups, feat_width)
        .transpose(2, 0, 1, 3)
        .reshape(devices, part_rows, feat_width)
    )
    flat_rows = lax.all_to_all(merge_send, "wide", split_axis=0, concat_axis=0, tiled=True).reshape(
        -1, feat_width
    )
    partial_value = jnp.dot(flat_rows, merge_rows, preferred_element_type=jnp.float32).reshape(
        devices, -1, out_width
    )
    summed = lax.all_to_all(partial_value, "wide", split_axis=0, concat_axis=0, tiled=True)
    tokens = (
        jnp.sum(summed.reshape(feat_groups, tok_groups, part_rows, out_width), axis=0)
        .reshape(token_count, out_width)
        .astype(jnp.bfloat16)
    )
    logits = jnp.dot(tokens, w_router, preferred_element_type=jnp.float32)
    experts = w_router.shape[1]
    top_count = expert_ids.shape[1]
    matches = expert_ids[:, :, None] == jnp.arange(experts, dtype=jnp.int32)[None, None, :]
    chosen = jnp.sum(jnp.where(matches, logits[:, None, :], 0.0), axis=2)
    gate_values = jax.nn.sigmoid(chosen)
    route_weight = route_scale * gate_values / jnp.sum(gate_values, axis=1, keepdims=True)
    capacity = min(token_count, 2 * token_count * top_count // experts)
    slot_count = experts * capacity
    target = expert_ids * capacity + slot_pos
    one_hot = jnp.any(
        target[None, :, :] == jnp.arange(slot_count, dtype=jnp.int32)[:, None, None], axis=2
    ).astype(jnp.bfloat16)
    buffer = jnp.dot(one_hot, tokens, preferred_element_type=jnp.float32).astype(jnp.bfloat16)
    gate_half = w_gate[0]
    up_half = w_up[0]
    down_half = w_down[0]
    half_cap = capacity // 2
    dispatch = buffer.reshape(devices, half_cap, out_width)
    portion = lax.all_to_all(dispatch, "wide", split_axis=0, concat_axis=0, tiled=True)
    item_count = portion.shape[1]
    partner_rows = swapped(portion, "wide", 0)
    both_rows = jnp.concatenate([portion, partner_rows], axis=1)
    flat_rows = both_rows.reshape(-1, out_width)
    gate_part = jnp.dot(flat_rows, gate_half, preferred_element_type=jnp.float32)
    up_part = jnp.dot(flat_rows, up_half, preferred_element_type=jnp.float32)
    hidden = (jax.nn.silu(gate_part) * up_part).astype(jnp.bfloat16)
    product = (
        jnp.dot(hidden, down_half, preferred_element_type=jnp.float32)
        .astype(jnp.bfloat16)
        .reshape(devices, 2 * item_count, out_width)
    )
    from_partner = swapped(product[:, item_count:], "wide", 0)
    joined = (
        product[:, :item_count].astype(jnp.float32) + from_partner.astype(jnp.float32)
    ).astype(jnp.bfloat16)
    answers = lax.all_to_all(joined, "wide", split_axis=0, concat_axis=0, tiled=True)
    slot_result = answers.reshape(slot_count, out_width)
    slot_result = lax.optimization_barrier(slot_result)
    picked = jnp.take(slot_result, target.reshape(-1), axis=0).reshape(
        token_count, top_count, out_width
    )
    return jnp.sum(picked.astype(jnp.float32) * route_weight[:, :, None], axis=1).astype(
        jnp.bfloat16
    )


BF = jnp.bfloat16
F32 = jnp.float32
VMEM = pl.BlockSpec(memory_space=pltpu.VMEM)
SMEM = pl.BlockSpec(memory_space=pltpu.SMEM)
HBM = pl.BlockSpec(memory_space=pltpu.HBM)
LANES = 128
MASKED = -1e30
LOG2E = 1.4426950408889634


def params(mib):
    return pltpu.CompilerParams(vmem_limit_bytes=mib * 2**20)


def cost(flops, size, exps=0):
    return pl.CostEstimate(flops=flops, bytes_accessed=size, transcendentals=exps)


def flipped(number, bits):
    low = (number % 2 + bits % 2) % 2
    return 2 * ((number // 2 + bits // 2) % 2) + low


def pieces(value, count):
    out = []
    for _ in range(count):
        piece = value.astype(BF).astype(F32)
        out.append(piece)
        value = value - piece
    return out


def pack_kernel(qkv_ref, out_ref):
    rows, width = qkv_ref.shape
    tokens = rows // 4
    peers, parts, _ = out_ref.shape
    source = lax.broadcasted_iota(jnp.int32, (rows, rows), 0)
    place = lax.broadcasted_iota(jnp.int32, (rows, rows), 1)
    order = jnp.where(source == 4 * (place % tokens) + place // tokens, 1.0, 0.0).astype(BF)
    part = parts // 3
    third = width // 3
    for kind in range(3):
        turned = lax.dot_general(
            qkv_ref[:, kind * third : (kind + 1) * third],
            order,
            (((0,), (0,)), ((), ())),
            preferred_element_type=F32,
        ).astype(BF)
        for peer in range(peers):
            out_ref[peer, kind * part : (kind + 1) * part, :] = turned[peer * part : (peer + 1) * part]


def share_kernel(merge_ref, common_ref, share_ref, sems):
    common, share = common_ref.shape[0], share_ref.shape[0]
    spot = pl.multiple_of(common + share * lax.axis_index("grp"), 16)
    copies = [
        pltpu.make_async_copy(merge_ref.at[pl.ds(spot, share), :], share_ref, sems.at[0]),
        pltpu.make_async_copy(merge_ref.at[pl.ds(0, common), :], common_ref, sems.at[1]),
    ]
    for copy in copies:
        copy.start()
    for copy in copies:
        copy.wait()


def attend_kernel(x_ref, grid_ref, out_ref):
    peers, parts, lanes = x_ref.shape
    part = parts // 3
    dim = part // 2
    quarters = 4
    sides = peers // quarters
    tokens = lanes // 4
    clip = lax.axis_index("wide") // peers
    count = grid_ref[clip, 0] * grid_ref[clip, 1]
    factor = dim ** (-0.5) * LOG2E
    keys = jnp.concatenate([x_ref[s, part : 2 * part, :] for s in range(peers)], 1)
    lane = lax.broadcasted_iota(jnp.int32, (16, peers * lanes), 1)
    row = lax.broadcasted_iota(jnp.int32, (16, peers * lanes), 0)
    inner = lane % lanes
    place = lane // lanes * lanes + 4 * (inner % tokens) + inner // tokens
    hidden = jnp.where((row == 0) & (place >= count), MASKED, 0.0).astype(BF)
    keys = jnp.concatenate([keys, hidden], 0).T
    values = jnp.concatenate([x_ref[s, 2 * part :, :] for s in range(peers)], 1).astype(F32)
    values = [values[:dim].astype(BF), values[dim:].astype(BF)]
    ones = jnp.where(lax.broadcasted_iota(jnp.int32, (16, sides * lanes), 0) == 0, 1.0, 0.0).astype(BF)
    head_row = lax.broadcasted_iota(jnp.int32, (part, sides * lanes), 0) // dim
    group = lax.broadcasted_iota(jnp.int32, (dim, lanes), 1) // tokens
    def scores_of(item):
        quarter, head = item // 2, item % 2
        query = jnp.concatenate(
            [x_ref[quarter + quarters * s, :part, :] for s in range(sides)], 1
        ).astype(F32)
        own = jnp.concatenate([jnp.where(head_row == head, query, 0.0).astype(BF), ones], 0)
        return jnp.dot(keys, own, preferred_element_type=F32)

    scores = scores_of(0)
    for item in range(2 * quarters):
        quarter, head = item // 2, item % 2
        following = scores_of(item + 1) if item + 1 < 2 * quarters else None
        highest = jnp.max(scores, axis=0, keepdims=True)
        weights = jnp.exp2((scores - highest) * factor)
        total = jnp.sum(weights, axis=0, keepdims=True)
        value = jnp.dot(values[head], weights.astype(BF), preferred_element_type=F32) / total
        mixed = [] if head == 0 else mixed
        mixed += [value[:, s * lanes : (s + 1) * lanes] for s in range(sides)]
        scores = following
        if head == 0:
            continue
        for position in range(4):
            block = mixed[position]
            for g in range(4):
                if g != position:
                    shift = (g - position) * tokens % lanes
                    block = jnp.where(group == g, pltpu.roll(mixed[g], shift, 1), block)
            out_ref[quarters * position + quarter] = block.astype(BF)


def merge_kernel(
    x_ref, w_out_hbm, gain_ref, bias_ref, *refs
):
    w0, w1, *rest, out_ref, att_ref, w_ref, w_out_ref, sems = refs
    me, group = lax.axis_index("wide"), lax.axis_index("grp")
    position, quarter = me // 4, me % 4
    blocks, dim, lanes = x_ref.shape
    pairs = blocks // 2
    depth = w0.shape[0]
    out_width = w0.shape[1]
    width = w_out_ref.shape[1]
    first_copy = pltpu.make_async_copy(w_out_hbm, w_out_ref, sems.at[8])
    first_copy.start()
    copies = []
    common, share = rest[0].shape[0], rest[1].shape[0]
    places = [(w0, 0, 0), (w1, 1, 0)]
    for k in (2, 3):
        both, mine, theirs = rest[3 * (k - 2) : 3 * (k - 1)]
        places += [(both, k, 0), (mine, k, common + share * group), (theirs, k, common + share * (1 - group))]
    for n, (source, k, first) in enumerate(places):
        spot = pl.multiple_of(flipped(quarter, k) * depth + first, 16)
        copies.append(pltpu.make_async_copy(source, w_ref.at[pl.ds(spot, source.shape[0]), :], sems.at[n]))
        copies[-1].start()
    left = lax.broadcasted_iota(jnp.int32, (dim, lanes), 1) < lanes // 2
    for pair in range(pairs):
        first, second = x_ref[pair].astype(F32), x_ref[pairs + pair].astype(F32)
        upper = jnp.where(left, first, pltpu.roll(second, lanes // 2, 1))
        lower = jnp.where(left, pltpu.roll(first, lanes // 2, 1), second)
        att_ref[2 * dim * pair : 2 * dim * (pair + 1), :] = jnp.concatenate([upper, lower], 0).astype(BF)
    first_copy.wait()
    mixed = lax.dot_general(
        att_ref[...], w_out_ref[...], (((0,), (0,)), ((), ())), preferred_element_type=F32
    )
    mixed = mixed.astype(BF).astype(F32)
    centre = jnp.sum(mixed, axis=1, keepdims=True) / width
    centered = mixed - centre
    square = jnp.sum(centered * centered, axis=1, keepdims=True)
    here = pl.ds(pl.multiple_of(position * width, LANES), width)
    gain, bias = gain_ref[:, here], bias_ref[:, here]
    row = lax.broadcasted_iota(jnp.int32, (16, width), 0)
    extra = jnp.zeros((16, width), F32)
    for k, line in enumerate(pieces(gain, 2) + pieces(bias, 2)):
        extra = jnp.where(row == k, line, extra)
    left_side = jnp.concatenate([(centered * gain).astype(BF), extra.astype(BF)], 0)
    lane = lax.broadcasted_iota(jnp.int32, (lanes, LANES), 1)
    stats = jnp.zeros((lanes, LANES), F32)
    for k, column in enumerate(pieces(centre, 3) + pieces(square, 3)):
        stats = jnp.where(lane == k, column, stats)
    stats = stats.astype(BF)
    for copy in copies:
        copy.wait()
    planes, tokens, _ = out_ref.shape
    half = tokens // 2
    step = 2 * LANES
    shared = [None] * tokens
    for begin in range(0, out_width, step):
        part = jnp.dot(left_side, w_ref[:, begin : begin + step], preferred_element_type=F32)
        for plane in range(planes):
            out_ref[flipped(position, plane), :, begin : begin + step] = part[plane * tokens : (plane + 1) * tokens].astype(BF)
        scale = part[lanes : lanes + 1] + part[lanes + 1 : lanes + 2]
        shift = part[lanes + 2 : lanes + 3] + part[lanes + 3 : lanes + 4]
        for k in range(step // LANES):
            shared[begin // LANES + k] = scale[:, k * LANES : (k + 1) * LANES]
            shared[half + begin // LANES + k] = shift[:, k * LANES : (k + 1) * LANES]
    shared = jnp.concatenate(shared, 0).astype(BF)
    for plane in range(planes):
        out_ref[flipped(position, plane), :, out_width : out_width + LANES] = shared
        out_ref[flipped(position, plane), :, out_width + LANES :] = stats[plane * tokens : (plane + 1) * tokens]


def route_kernel(x0, x1, x2, x3, router_ref, ids_ref, out_ref, *, merge_width, experts):
    blocks = (x0, x1, x2, x3)
    planes, tokens = len(blocks), x0.shape[0]
    out_width = out_ref.shape[1] - LANES
    half = tokens // 2
    stats = [blocks[p][:, out_width + LANES :].astype(F32) for p in range(planes)]
    shared = [blocks[p][:, out_width : out_width + LANES].astype(F32) for p in range(planes)]
    centres = [s[:, 0:1] + s[:, 1:2] + s[:, 2:3] for s in stats]
    squares = [s[:, 3:4] + s[:, 4:5] + s[:, 5:6] for s in stats]
    mean = sum(centres) / planes
    offsets = [c - mean for c in centres]
    spread = sum(q + (merge_width // planes) * (o * o) for q, o in zip(squares, offsets)) / merge_width
    inverse = lax.rsqrt(spread + norm_eps)
    bias = sum(shared)
    for k in range(out_width // LANES):
        cut = slice(k * LANES, (k + 1) * LANES)
        total = sum(blocks[p][:, cut].astype(F32) for p in range(planes))
        total += sum(offsets[p] * shared[p][k : k + 1] for p in range(planes))
        out_ref[:, cut] = (total * inverse + bias[half + k : half + k + 1]).astype(BF)
    logits = jnp.dot(out_ref[:, :out_width], router_ref[...], preferred_element_type=F32)
    lane = lax.broadcasted_iota(jnp.int32, (tokens, LANES), 1)
    expert = lane % experts
    chosen = lane < 0
    for k in range(ids_ref.shape[1]):
        chosen = chosen | (ids_ref[:, k : k + 1] == expert)
    gates = jnp.where(chosen & (lane < 2 * experts), 1.0 / (1.0 + jnp.exp(-logits)), 0.0)
    total = jnp.sum(jnp.where(lane < experts, gates, 0.0), axis=1, keepdims=True)
    weight = route_scale * gates / total
    high, low = pieces(weight, 2)
    out_ref[:, out_width:] = jnp.where(lane < experts, high, low).astype(BF)


def expert_kernel(*refs, experts, cuts):
    *blocks, gate_hbm, up_hbm, down_hbm, own_ref, other_ref, x_ref, gate_ref, up_ref, down_ref, sems = refs
    tokens, width = own_ref.shape[1:]
    half = own_ref.shape[0]
    places = [(b, slice(r, r + tokens)) for b in blocks for r in range(0, b.shape[0], tokens)]
    copies = []
    for k, cut in enumerate(cuts):
        for kind, source, target in ((0, gate_hbm, gate_ref), (1, up_hbm, up_ref)):
            copies.append(pltpu.make_async_copy(source.at[0, cut, :], target.at[cut, :], sems.at[2 * k + kind]))
            copies[-1].start()
    last = pltpu.make_async_copy(down_hbm.at[0], down_ref, sems.at[2 * len(cuts)])
    last.start()
    expert = lax.axis_index("wide") // 2
    lane = lax.broadcasted_iota(jnp.int32, (tokens, LANES), 1)
    weights = []
    for k, (block, rows) in enumerate(places):
        x_ref[k * tokens : (k + 1) * tokens, :] = block[rows, :width]
        picked = (lane == expert) | (lane == expert + experts)
        picked = jnp.where(picked, block[rows, width:].astype(F32), 0.0)
        weights.append(jnp.sum(picked, axis=1, keepdims=True))
    inputs = x_ref[...]
    turned = (((1,), (1,)), ((), ()))

    def gated(gate, up):
        return (gate / (1.0 + jnp.exp(-gate)) * up).astype(BF)

    hidden, earlier = [], None
    for k, cut in enumerate(cuts):
        copies[2 * k].wait()
        gate = lax.dot_general(inputs, gate_ref[cut, :], turned, preferred_element_type=F32)
        copies[2 * k + 1].wait()
        up = lax.dot_general(inputs, up_ref[cut, :], turned, preferred_element_type=F32)
        if earlier is not None:
            hidden.append(gated(*earlier))
        earlier = gate, up
    hidden = jnp.concatenate(hidden + [gated(*earlier)], 1)
    last.wait()
    step = 4 * LANES

    def product_of(begin):
        return jnp.dot(hidden, down_ref[:, begin : begin + step], preferred_element_type=F32)

    following = product_of(0)
    for begin in range(0, width, step):
        product = following
        following = product_of(begin + step) if begin + step < width else None
        for k in range(len(places)):
            value = (product[k * tokens : (k + 1) * tokens] * weights[k]).astype(BF)
            out_ref = own_ref if k < half else other_ref
            out_ref[k % half, :, begin : begin + step] = value


def join_kernel(*refs):
    *blocks, out_ref = refs
    rows = blocks[0].shape[0]
    for k, block in enumerate(blocks):
        out_ref[k * rows : (k + 1) * rows, :] = block[...]


def crossed(value, mask):
    pairs = [(source, source ^ mask) for source in range(lax.axis_size("wide"))]
    return lax.ppermute(value, "wide", pairs)


def local(
    qkv, grid, w_out, ln_gain, ln_bias, w_merge, w_router, expert_ids, slot_pos, w_gate, w_up, w_down
):
    devices = lax.axis_size("wide")
    rows = qkv.shape[0]
    vit_width = w_out.shape[0]
    experts = w_router.shape[1]
    out_width = w_merge.shape[1]
    tokens = rows // 4
    peers = devices // CLIPS
    suits = (
        devices == HEADS
        and peers == 8
        and rows == LANES
        and devices == 2 * experts
        and 2 * out_width == tokens * LANES
        and 4 * w_merge.shape[0] == vit_width
        and lax.axis_size("grp") == 2
        and w_merge.shape[0] % 32 == 0
    )
    if not suits:
        return general(
            qkv, grid, w_out, ln_gain, ln_bias, w_merge, w_router, expert_ids, slot_pos, w_gate, w_up, w_down
        )
    part = vit_width // peers
    dim = vit_width // HEADS
    depth = w_merge.shape[0]
    share = depth // 96 * 16
    packed = pl.pallas_call(
        pack_kernel,
        out_shape=jax.ShapeDtypeStruct((peers, 3 * part, rows), BF),
        in_specs=[VMEM],
        out_specs=VMEM,
        compiler_params=params(8),
    )(qkv)
    common, shared = pl.pallas_call(
        share_kernel,
        out_shape=[
            jax.ShapeDtypeStruct((depth - 2 * share, out_width), BF),
            jax.ShapeDtypeStruct((share, out_width), BF),
        ],
        in_specs=[HBM],
        out_specs=[VMEM] * 2,
        scratch_shapes=[pltpu.SemaphoreType.DMA((2,))],
        compiler_params=params(8),
        cost_estimate=cost(2**31, 2**24),
    )(w_merge)
    clips = [[c * peers + i for i in range(peers)] for c in range(CLIPS)]
    gathered = lax.all_to_all(
        packed, "wide", split_axis=0, concat_axis=0, tiled=True, axis_index_groups=clips
    )
    gathered, common, shared, held = lax.optimization_barrier((gathered, common, shared, w_merge))
    mine_y = crossed(shared, 2)
    common_y = crossed(common, 2)
    attended = pl.pallas_call(
        attend_kernel,
        out_shape=jax.ShapeDtypeStruct((devices, dim, rows), BF),
        in_specs=[VMEM, SMEM],
        out_specs=VMEM,
        compiler_params=params(20),
        cost_estimate=cost(2**32, 2**22, 2**21),
    )(gathered, grid)
    held_c = crossed(held, 1)
    attended, mine_y = lax.optimization_barrier((attended, mine_y))
    theirs_y = lax.ppermute(mine_y, "grp", [(0, 1), (1, 0)])
    mine_yc = crossed(mine_y, 1)
    returned = lax.all_to_all(attended, "wide", split_axis=0, concat_axis=0, tiled=True)
    returned, common_y, theirs_y = lax.optimization_barrier((returned, common_y, theirs_y))
    common_yc, theirs_yc = crossed(common_y, 1), crossed(theirs_y, 1)
    planes = devices // 4
    message = out_width + 2 * LANES
    partial = pl.pallas_call(
        merge_kernel,
        out_shape=jax.ShapeDtypeStruct((planes, tokens, message), BF),
        in_specs=[VMEM, HBM, VMEM, VMEM] + [pl.BlockSpec(memory_space=pl.ANY)] * 8,
        out_specs=VMEM,
        scratch_shapes=[
            pltpu.VMEM((vit_width, rows), BF),
            pltpu.VMEM((vit_width, out_width), BF),
            pltpu.VMEM((vit_width, vit_width), BF),
            pltpu.SemaphoreType.DMA((9,)),
        ],
        compiler_params=params(50),
    )(
        returned,
        w_out,
        ln_gain.reshape(1, 4 * vit_width),
        ln_bias.reshape(1, 4 * vit_width),
        w_merge,
        held_c,
        common_y,
        mine_y,
        theirs_y,
        common_yc,
        mine_yc,
        theirs_yc,
    )
    along = (8, 12, 4)
    arrived = [partial[0]] + [crossed(partial[mask // 4], mask) for mask in along]
    router = jnp.concatenate(
        [w_router, w_router, jnp.zeros((out_width, LANES - 2 * experts), BF)], 1
    )
    routed = pl.pallas_call(
        lambda *refs: route_kernel(*refs, merge_width=4 * vit_width, experts=experts),
        out_shape=jax.ShapeDtypeStruct((tokens, out_width + LANES), BF),
        in_specs=[VMEM] * 6,
        out_specs=VMEM,
        compiler_params=params(6),
    )(*arrived, router, expert_ids)
    joined = pl.pallas_call(
        join_kernel,
        out_shape=jax.ShapeDtypeStruct((len(along) * tokens, out_width + LANES), BF),
        in_specs=[VMEM] * len(along),
        out_specs=VMEM,
        compiler_params=params(6),
    )(*[crossed(routed, mask) for mask in along])
    near = [routed, joined]
    far = [crossed(block, 2) for block in near]
    *near, far[0] = lax.optimization_barrier((*near, far[0]))
    gate_turned, up_turned = jnp.swapaxes(w_gate, 1, 2), jnp.swapaxes(w_up, 1, 2)

    inner = w_down.shape[1]
    cuts = [slice(k, min(k + 2 * LANES, inner)) for k in range(0, inner, 2 * LANES)]

    def experts_of(blocks):
        return pl.pallas_call(
            lambda *refs: expert_kernel(*refs, experts=experts, cuts=cuts),
            out_shape=[jax.ShapeDtypeStruct((planes, tokens, out_width), BF)] * 2,
            in_specs=[VMEM] * (2 * len(blocks)) + [HBM] * 3,
            out_specs=[VMEM, VMEM],
            scratch_shapes=[
                pltpu.VMEM((2 * planes * tokens, out_width), BF),
                pltpu.VMEM((inner, out_width), BF),
                pltpu.VMEM((inner, out_width), BF),
                pltpu.VMEM((inner, out_width), BF),
                pltpu.SemaphoreType.DMA((2 * len(cuts) + 1,)),
            ],
            compiler_params=params(50),
            cost_estimate=cost(2**32, 2**24),
        )(*blocks, *[crossed(block, 1) for block in blocks], gate_turned, up_turned, w_down)

    def scattered(blocks):
        others = [crossed(blocks[1 + along.index(mask)], mask) for mask in along]
        return blocks[0].astype(F32) + sum(block.astype(F32) for block in others)

    def paired(own, other):
        return (own.astype(F32) + crossed(other, 1).astype(F32)).astype(BF)

    near_own, near_other = experts_of(near)
    *far, near_own, near_other = lax.optimization_barrier((*far, near_own, near_other))
    far_own, far_other = experts_of(far)
    near_sum = scattered(paired(near_own, near_other))
    far_out, near_sum = lax.optimization_barrier((paired(far_own, far_other), near_sum))
    across = [crossed(far_out[k], 2 + mask) for k, mask in enumerate(along, 1)]
    across.append(crossed(far_out[0], 2))
    return (near_sum + sum(block.astype(F32) for block in across)).astype(BF)


def solution(mesh):
    placed = (
        P(("grp", "wide"), None),
        P("grp", None),
        P(),
        P(),
        P(),
        P("wide", None),
        P(),
        P(("grp", "wide"), None),
        P(("grp", "wide"), None),
        P("wide", None, None),
        P("wide", None, None),
        P("wide", None, None),
    )
    return jax.shard_map(
        local, mesh=mesh, in_specs=placed, out_specs=P(("grp", "wide"), None), check_vma=False
    )
```
